32 devices in a mesh: chan: 8 (over y, x, core), tm: 4 (over z).
Axes of the slice: x: 2, y: 2, z: 4, core: 2. Of those that a mesh axis runs over, the one named last changes fastest.
Arguments:
- spectra: bfloat16 [64, 8, 2, 768], P(None, 'tm', None, 'chan'), may hold values from -120 to 120
- bad_channels: int32 [768], P('chan'), may hold values 0 or 1
- tile_list: int32 [64, 2], P('chan'), may hold values from 0 to 5, as said below
Outputs:
- correlations: float32 [64, 32, 128, 128], P(('chan', 'tm'))
The draws below stay inside these ranges and needn't reach their ends.
Inputs may be any that keep to these rules, and one draw needn't show every extreme that they name: `tile_list`: each row (a, b) has a <= b; a pair may appear more than once.
All inputs are finite; a program needn't handle non-finite values. No bound on the sum of `bad_channels` on one device may be relied on, other than what follows from the above.
Results may differ from the reference program's by a relative error of at most 0.004.
Values may be sent and summed in bfloat16 or wider, within the bound.
No kernel may reach another device: no remote copies, remote signals or barrier semaphores. Data moves between devices by JAX's collectives and lax.ppermute only.
A program may use at most 128 MiB of HBM per device.

```python
import math
import jax
import jax.numpy as jnp
from jax import lax

F = 64
LAGS = 32
TILE = 128
CHANNELS = 768
HOURS = 8
TILES = 64


def draw_spectra(key, part):
    key_base, key_bins, key_chan = jax.random.split(key, 3)
    full_shape = (F, HOURS, 2, CHANNELS)
    noise_base = jnp.clip(jax.random.normal(key_base, full_shape, jnp.float32), -4.0, 4.0)
    bin_scale = jnp.exp(jax.random.uniform(key_bins, (F, 1, 1, CHANNELS), jnp.float32, 0.0, math.log(10.0)))
    chan_scale = jnp.exp(jax.random.uniform(key_chan, (1, HOURS, 1, CHANNELS), jnp.float32, math.log(0.3), math.log(3.0)))
    return (noise_base * bin_scale * chan_scale).astype(jnp.bfloat16)


def draw_tile_list(key, part):
    block_total = CHANNELS // TILE
    key_one, key_two = jax.random.split(key, 2)
    pick_one = jax.random.randint(key_one, (TILES,), 0, block_total)
    pick_two = jax.random.randint(key_two, (TILES,), 0, block_total)
    lower_idx = jnp.minimum(pick_one, pick_two)
    upper_idx = jnp.maximum(pick_one, pick_two)
    upper_idx = upper_idx.at[0].set(block_total - 1)
    lower_idx = lower_idx.at[1].set(0)
    return jnp.stack([lower_idx, upper_idx], axis=1).astype(jnp.int32)


def with_ends(drawn, rng, least, largest):
    longest = drawn.shape.index(max(drawn.shape))
    spots = []
    for shift in (0, 1):
        where = [jax.random.randint(jax.random.fold_in(rng, axis), (), 0, length) for axis, length in enumerate(drawn.shape)]
        where[longest] = (where[longest] + shift) % drawn.shape[longest]
        spots.append(tuple(where))
    return drawn.at[spots[0]].set(least).at[spots[1]].set(largest)


def setup_inputs(seed: int = 0) -> dict:
    splits = jax.random.split(jax.random.key(seed), 4)
    return {
        "spectra": draw_spectra(jax.random.fold_in(splits[3], 71), 0),
        "bad_channels": with_ends((jax.random.randint(splits[1], (CHANNELS,), 0, 8) < 1).astype(jnp.int32), jax.random.fold_in(splits[1], 1), 0, 1),
        "tile_list": draw_tile_list(jax.random.fold_in(splits[3], 71), 0),
    }


EPSILON = 1e-06

def whiten(spectra, bad_channels):
    values = spectra.astype(jnp.float32)
    power = lax.optimization_barrier(jnp.mean(values * values, axis=(0, 2)))
    keep_mask = (1 - bad_channels).astype(jnp.float32)
    white = values * lax.rsqrt(power + EPSILON)[None, :, None, :] * keep_mask[None, None, None, :]
    return white.astype(jnp.bfloat16)

def lag_table(hour_count):
    bin_number = jnp.arange(F, dtype=jnp.float32) + 1.0
    lag_steps = jnp.arange(LAGS, dtype=jnp.float32) - float(LAGS // 2)
    phases = math.pi / F * bin_number[:, None] * lag_steps[None, :]
    norm_scale = 1.0 / math.sqrt(F * hour_count)
    return jnp.stack([jnp.cos(phases) * norm_scale, -jnp.sin(phases) * norm_scale], axis=1)

def take_block(spectra_all, block_index):
    return lax.dynamic_slice_in_dim(spectra_all, (block_index * TILE).astype(jnp.int32), TILE, axis=3)

def cross_spec(spectra_all, tile_pair):
    left_block = take_block(spectra_all, tile_pair[0]).astype(jnp.float32)
    right_block = take_block(spectra_all, tile_pair[1]).astype(jnp.float32)
    bin_total = left_block.shape[0]
    hour_count = left_block.shape[1]
    row_block = left_block.reshape(bin_total, 2 * hour_count, TILE)
    turned = jnp.stack([-right_block[:, :, 1], right_block[:, :, 0]], axis=2)
    col_block = jnp.concatenate([right_block, turned], axis=3).reshape(bin_total, 2 * hour_count, 2 * TILE)
    return jnp.einsum('fki,fkj->fij', row_block, col_block, precision=lax.Precision.HIGHEST)

def transform(cross, table):
    parted = cross.reshape(cross.shape[0], TILE, 2, TILE)
    return jnp.einsum('fixj,fxt->tij', parted, table, precision=lax.Precision.HIGHEST)

def reference(spectra, bad_channels, tile_list):
    white = whiten(spectra, bad_channels)
    table = lag_table(HOURS)

    def tile_lags(tile_pair):
        return transform(cross_spec(white, tile_pair), table)
    return lax.map(tile_lags, tile_list)
```

```python
import functools
import math

import jax
import jax.numpy as jnp
import numpy as np
from jax import lax
from jax.experimental import pallas as pl
from jax.experimental.pallas import tpu as pltpu
from jax.sharding import PartitionSpec as P

F = 64
LAGS = 32
TILE = 128
EPSILON = 1e-06
COARSE = 8
LEFT_TURNS = LAGS // COARSE
PAIR = 2


def turn_tables(hours, hours_dev):
    bins = np.repeat(np.arange(1, F + 1, dtype=np.float64), hours_dev)
    left = math.pi / F * bins[None] * (COARSE * np.arange(LEFT_TURNS) - LAGS // 2)[:, None]
    right = -math.pi / F * bins[None] * np.arange(COARSE)[:, None]
    norm = 1.0 / math.sqrt(F * hours)
    left_table = np.stack([np.cos(left) * norm, np.sin(left) * norm], axis=1)
    right_table = np.stack([np.cos(right), np.sin(right)], axis=1)
    return left_table.astype(np.float32), right_table.astype(np.float32)


def whiten_kernel(spectra_ref, bad_ref, out_ref):
    bins, hours, _, chans = spectra_ref.shape
    rows = bins * hours * 2
    values = spectra_ref[...].reshape(rows, chans).astype(jnp.float32)
    row = lax.broadcasted_iota(jnp.int32, (rows, chans), 0)
    hour = (row // 2) % hours
    squares = values * values
    keep = (1 - bad_ref[...]).astype(jnp.float32)
    scale = jnp.zeros((rows, chans), jnp.float32)
    for h in range(hours):
        power = jnp.sum(jnp.where(hour == h, squares, 0.0), axis=0, keepdims=True) * (1.0 / (2 * bins))
        scale = jnp.where(hour == h, lax.rsqrt(power + EPSILON) * keep, scale)
    white = (values * scale).astype(jnp.bfloat16)
    src = lax.broadcasted_iota(jnp.int32, (rows, rows), 0)
    dst = lax.broadcasted_iota(jnp.int32, (rows, rows), 1)
    move = jnp.where((src % 2) * (rows // 2) + src // 2 == dst, 1.0, 0.0).astype(jnp.bfloat16)
    out_ref[...] = lax.dot_general(
        white, move, (((0,), (0,)), ((), ())), preferred_element_type=jnp.float32
    ).astype(jnp.bfloat16)


def whiten(spectra, bad_channels):
    bins, hours, _, chans = spectra.shape
    return pl.pallas_call(
        whiten_kernel,
        out_shape=jax.ShapeDtypeStruct((chans, bins * hours * 2), jnp.bfloat16),
        name="whiten",
    )(spectra, bad_channels.reshape(1, chans))


def turned(block, cos, sin):
    half = block.shape[1] // 2
    re = block[:, :half].astype(jnp.float32)
    im = block[:, half:].astype(jnp.float32)
    return jnp.concatenate([re * cos - im * sin, re * sin + im * cos], axis=1).astype(jnp.bfloat16)


def correlate_kernel(pairs_ref, left_ref, right_ref, left_table_ref, right_table_ref, out_ref, left_turned, right_turned):
    groups = left_ref.shape[0]
    lanes = left_ref.shape[2]

    @pl.when(pl.program_id(1) == 0)
    def _():
        for g in range(groups):
            block = left_ref[g]
            for u in range(LEFT_TURNS):
                left_turned[u * TILE:(u + 1) * TILE, g * lanes:(g + 1) * lanes] = turned(
                    block, left_table_ref[u, 0:1, :], left_table_ref[u, 1:2, :]
                )

    for g in range(groups):
        block = right_ref[g]
        for s in range(PAIR):
            right_turned[s * TILE:(s + 1) * TILE, g * lanes:(g + 1) * lanes] = turned(
                block, right_table_ref[s, 0:1, :], right_table_ref[s, 1:2, :]
            )
    total = lax.dot_general(
        left_turned[...], right_turned[...], (((1,), (1,)), ((), ())), preferred_element_type=jnp.float32
    )
    for u in range(LEFT_TURNS):
        for s in range(PAIR):
            out_ref[0, u, s] = total[u * TILE:(u + 1) * TILE, s * TILE:(s + 1) * TILE]


def correlate(spectra_all, pairs, hours):
    groups, _, lanes = spectra_all.shape
    tiles = pairs.shape[0]
    half = lanes // 2
    left_table, right_table = turn_tables(hours, half // F)
    out = pl.pallas_call(
        correlate_kernel,
        out_shape=jax.ShapeDtypeStruct((tiles, LEFT_TURNS, COARSE, TILE, TILE), jnp.float32),
        grid_spec=pltpu.PrefetchScalarGridSpec(
            num_scalar_prefetch=1,
            grid=(tiles, COARSE // PAIR),
            in_specs=[
                pl.BlockSpec((groups, TILE, lanes), lambda t, j, pairs: (0, pairs[t, 0], 0)),
                pl.BlockSpec((groups, TILE, lanes), lambda t, j, pairs: (0, pairs[t, 1], 0)),
                pl.BlockSpec((LEFT_TURNS, 2, half), lambda t, j, pairs: (0, 0, 0)),
                pl.BlockSpec((PAIR, 2, half), lambda t, j, pairs: (j, 0, 0)),
            ],
            out_specs=pl.BlockSpec((1, LEFT_TURNS, PAIR, TILE, TILE), lambda t, j, pairs: (t, 0, j, 0, 0)),
            scratch_shapes=[
                pltpu.VMEM((LEFT_TURNS * TILE, groups * lanes), jnp.bfloat16),
                pltpu.VMEM((PAIR * TILE, groups * lanes), jnp.bfloat16),
            ],
        ),
        compiler_params=pltpu.CompilerParams(vmem_limit_bytes=32 * 1024 * 1024),
        name="correlate",
    )(pairs, spectra_all, spectra_all, jnp.asarray(left_table), jnp.asarray(right_table))
    return out.reshape(tiles, LAGS, TILE, TILE)


def per_device(spectra, bad_channels, tile_list):
    groups = lax.axis_size("tm")
    hours = spectra.shape[1] * groups
    tile_dev = tile_list.shape[0] // groups
    white = whiten(spectra, bad_channels)
    gathered = lax.all_gather(white, ("tm", "chan"), axis=0, tiled=True)
    spectra_all = gathered.reshape(groups, gathered.shape[0] // groups, gathered.shape[1])
    pairs = lax.dynamic_slice_in_dim(tile_list, lax.axis_index("tm") * tile_dev, tile_dev, axis=0)
    return correlate(spectra_all, pairs, hours)


def solution(mesh):
    placed = (P(None, "tm", None, "chan"), P("chan"), P("chan", None))
    return jax.shard_map(
        per_device,
        mesh=mesh,
        in_specs=placed,
        out_specs=P(("chan", "tm"), None, None, None),
        check_vma=False,
    )
```

```python
import functools
import math

import jax
import jax.numpy as jnp
import numpy as np
from jax import lax
from jax.experimental import pallas as pl
from jax.experimental.pallas import tpu as pltpu
from jax.sharding import PartitionSpec as P

F = 64
LAGS = 32
TILE = 128
EPSILON = 1e-06
COARSE = 8
LEFT_TURNS = LAGS // COARSE
PAIR = 2


def turn_tables(hours, hours_dev):
    bins = np.repeat(np.arange(1, F + 1, dtype=np.float64), hours_dev)
    left = math.pi / F * bins[None] * (COARSE * np.arange(LEFT_TURNS) - LAGS // 2)[:, None]
    right = -math.pi / F * bins[None] * np.arange(COARSE)[:, None]
    norm = 1.0 / math.sqrt(F * hours)
    left_table = np.stack([np.cos(left) * norm, np.sin(left) * norm], axis=1)
    right_table = np.stack([np.cos(right), np.sin(right)], axis=1)
    return left_table.astype(np.float32), right_table.astype(np.float32)


def whiten_kernel(spectra_ref, bad_ref, out_ref):
    bins, hours, _, chans = spectra_ref.shape
    rows = bins * hours * 2
    values = spectra_ref[...].reshape(rows, chans).astype(jnp.float32)
    row = lax.broadcasted_iota(jnp.int32, (rows, chans), 0)
    hour = (row // 2) % hours
    squares = values * values
    keep = (1 - bad_ref[...]).astype(jnp.float32)
    scale = jnp.zeros((rows, chans), jnp.float32)
    for h in range(hours):
        power = jnp.sum(jnp.where(hour == h, squares, 0.0), axis=0, keepdims=True) * (1.0 / (2 * bins))
        scale = jnp.where(hour == h, lax.rsqrt(power + EPSILON) * keep, scale)
    white = (values * scale).astype(jnp.bfloat16)
    src = lax.broadcasted_iota(jnp.int32, (rows, rows), 0)
    dst = lax.broadcasted_iota(jnp.int32, (rows, rows), 1)
    move = jnp.where((src % 2) * (rows // 2) + src // 2 == dst, 1.0, 0.0).astype(jnp.bfloat16)
    out_ref[...] = lax.dot_general(
        white, move, (((0,), (0,)), ((), ())), preferred_element_type=jnp.float32
    ).astype(jnp.bfloat16)


def whiten(spectra, bad_channels):
    bins, hours, _, chans = spectra.shape
    return pl.pallas_call(
        whiten_kernel,
        out_shape=jax.ShapeDtypeStruct((chans, bins * hours * 2), jnp.bfloat16),
        name="whiten",
    )(spectra, bad_channels.reshape(1, chans))


def turned(block, cos, sin):
    half = block.shape[1] // 2
    re = block[:, :half].astype(jnp.float32)
    im = block[:, half:].astype(jnp.float32)
    return jnp.concatenate([re * cos - im * sin, re * sin + im * cos], axis=1).astype(jnp.bfloat16)


def correlate_kernel(where_ref, *refs):
    pieces = refs[:-9]
    left_table_hbm, right_table_hbm, out_ref, spectra, left_table, right_table, left_turned, right_turned, sem = refs[-9:]
    tile, step = pl.program_id(0), pl.program_id(1)
    groups, _, lanes = spectra.shape
    rows = pieces[0].shape[1]

    @pl.when((tile == 0) & (step == 0))
    def _():
        own = where_ref[0]
        copies = [
            pltpu.make_async_copy(left_table_hbm, left_table, sem),
            pltpu.make_async_copy(right_table_hbm, right_table, sem),
        ]
        for k, piece in enumerate(pieces):
            place = pl.multiple_of((own ^ k) * rows, 32)
            copies.append(pltpu.make_async_copy(piece, spectra.at[:, pl.ds(place, rows), :], sem))
        for copy in copies:
            copy.start()
        for copy in copies:
            copy.wait()

    @pl.when(step == 0)
    def _():
        place = pl.multiple_of(where_ref[1 + 2 * tile] * TILE, TILE)
        for g in range(groups):
            block = spectra[g, pl.ds(place, TILE), :]
            for u in range(LEFT_TURNS):
                left_turned[u * TILE:(u + 1) * TILE, g * lanes:(g + 1) * lanes] = turned(
                    block, left_table[u, 0:1, :], left_table[u, 1:2, :]
                )

    place = pl.multiple_of(where_ref[2 + 2 * tile] * TILE, TILE)
    for g in range(groups):
        block = spectra[g, pl.ds(place, TILE), :]
        for s in range(PAIR):
            turn = step * PAIR + s
            right_turned[s * TILE:(s + 1) * TILE, g * lanes:(g + 1) * lanes] = turned(
                block, right_table[turn, 0:1, :], right_table[turn, 1:2, :]
            )
    total = lax.dot_general(
        left_turned[...], right_turned[...], (((1,), (1,)), ((), ())), preferred_element_type=jnp.float32
    )
    for u in range(LEFT_TURNS):
        for s in range(PAIR):
            out_ref[0, u, s] = total[u * TILE:(u + 1) * TILE, s * TILE:(s + 1) * TILE]


def correlate(pieces, pairs, own, hours):
    groups, rows, lanes = pieces[0].shape
    tiles = pairs.shape[0]
    half = lanes // 2
    left_table, right_table = turn_tables(hours, half // F)
    where = jnp.concatenate([own.reshape(1), pairs.reshape(-1)]).astype(jnp.int32)
    out = pl.pallas_call(
        correlate_kernel,
        out_shape=jax.ShapeDtypeStruct((tiles, LEFT_TURNS, COARSE, TILE, TILE), jnp.float32),
        grid_spec=pltpu.PrefetchScalarGridSpec(
            num_scalar_prefetch=1,
            grid=(tiles, COARSE // PAIR),
            in_specs=[pl.BlockSpec(memory_space=pl.ANY)] * (len(pieces) + 2),
            out_specs=pl.BlockSpec((1, LEFT_TURNS, PAIR, TILE, TILE), lambda t, j, where: (t, 0, j, 0, 0)),
            scratch_shapes=[
                pltpu.VMEM((groups, len(pieces) * rows, lanes), jnp.bfloat16),
                pltpu.VMEM(left_table.shape, jnp.float32),
                pltpu.VMEM(right_table.shape, jnp.float32),
                pltpu.VMEM((LEFT_TURNS * TILE, groups * lanes), jnp.bfloat16),
                pltpu.VMEM((PAIR * TILE, groups * lanes), jnp.bfloat16),
                pltpu.SemaphoreType.DMA,
            ],
        ),
        compiler_params=pltpu.CompilerParams(vmem_limit_bytes=40 * 1024 * 1024),
        name="correlate",
    )(where, *pieces, jnp.asarray(left_table), jnp.asarray(right_table))
    return out.reshape(tiles, LAGS, TILE, TILE)


def swap(array, axis, k):
    if k == 0:
        return array
    return lax.ppermute(array, axis, [(i, i ^ k) for i in range(lax.axis_size(axis))])


def gather_pieces(white):
    stack = jnp.stack([swap(white, "tm", k) for k in range(lax.axis_size("tm"))])
    pieces = {k: swap(stack, "chan", k) for k in range(0, lax.axis_size("chan"), 2)}
    for k in list(pieces):
        pieces[k + 1] = swap(pieces[k], "chan", 1)
    return [pieces[k] for k in sorted(pieces)]


def per_device(spectra, bad_channels, tile_list):
    groups = lax.axis_size("tm")
    hours = spectra.shape[1] * groups
    tile_dev = tile_list.shape[0] // groups
    white = whiten(spectra, bad_channels)
    pieces = gather_pieces(white)
    pairs = lax.dynamic_slice_in_dim(tile_list, lax.axis_index("tm") * tile_dev, tile_dev, axis=0)
    return correlate(pieces, pairs, lax.axis_index("chan"), hours)


def solution(mesh):
    placed = (P(None, "tm", None, "chan"), P("chan"), P("chan", None))
    return jax.shard_map(
        per_device,
        mesh=mesh,
        in_specs=placed,
        out_specs=P(("chan", "tm"), None, None, None),
        check_vma=False,
    )
```

```python
import math

import jax
import jax.numpy as jnp
from jax import lax
from jax.experimental import pallas as pl
from jax.experimental.pallas import tpu as pltpu
from jax.sharding import PartitionSpec as P

F = 64
LAGS = 32
TILE = 128
EPSILON = 1e-06
CORES = 2
COARSE = (-12, -4, 4, 12)
FINE = (-4, -3, -2, -1, 0, 1, 2, 3)
SEGMENT = 32


def whiten_kernel(spectra_ref, bad_ref, out_ref):
    bins, hours, _, chans = spectra_ref.shape
    rows = bins * hours * 2
    values = spectra_ref[...].reshape(rows, chans).astype(jnp.float32)
    row = lax.broadcasted_iota(jnp.int32, (rows, chans), 0)
    hour = (row // 2) % hours
    squares = values * values
    keep = (1 - bad_ref[...]).astype(jnp.float32)
    scale = jnp.zeros((rows, chans), jnp.float32)
    for h in range(hours):
        power = jnp.sum(jnp.where(hour == h, squares, 0.0), axis=0, keepdims=True) * (1.0 / (2 * bins))
        scale = jnp.where(hour == h, lax.rsqrt(power + EPSILON) * keep, scale)
    white = (values * scale).astype(jnp.bfloat16)
    src = lax.broadcasted_iota(jnp.int32, (rows, rows), 0)
    dst = lax.broadcasted_iota(jnp.int32, (rows, rows), 1)
    move = jnp.where((src % 2) * (rows // 2) + src // 2 == dst, 1.0, 0.0).astype(jnp.bfloat16)
    turned = lax.dot_general(
        white, move, (((0,), (0,)), ((), ())), preferred_element_type=jnp.float32
    ).astype(jnp.bfloat16)
    for copy in range(out_ref.shape[0]):
        out_ref[copy] = turned


def whiten(spectra, bad_channels, copies):
    bins, hours, _, chans = spectra.shape
    return pl.pallas_call(
        whiten_kernel,
        out_shape=jax.ShapeDtypeStruct((copies, chans, bins * hours * 2), jnp.bfloat16),
        name="whiten",
    )(spectra, bad_channels.reshape(1, chans))


def turn_by(re, im, cos, sin, both):
    rc, rs, ic, is_ = re * cos, re * sin, im * cos, im * sin
    forward = (rc - is_, rs + ic)
    return (forward, (rc + is_, ic - rs)) if both else (forward,)


def correlate_kernel(norm, where_ref, own_ref, sib_ref, out_ref, left_turned, right_turned, staging, sem):
    tiles = staging.shape[0]
    _, groups, rows, lanes = own_ref.shape
    half = lanes // 2
    hours_dev = half // F
    core = where_ref[0]
    bin_number = lax.broadcasted_iota(jnp.int32, (8, half), 1) // hours_dev + 1
    step = lax.broadcasted_iota(jnp.int32, (8, half), 0)
    step = jnp.where(step == 6, 12, step)
    turn = (step * bin_number) % (2 * F)
    angle = jnp.where(turn >= F, turn - 2 * F, turn).astype(jnp.float32) * (math.pi / F)
    cos, sin = jnp.cos(angle), jnp.sin(angle)
    table = {k: (cos[i:i + 1], sin[i:i + 1]) for k, i in ((1, 1), (2, 2), (3, 3), (4, 4), (12, 6))}

    def load(block, g):
        parts = []
        for i in range(TILE // SEGMENT):
            first = block * TILE + i * SEGMENT
            chan = first // rows
            place = pl.multiple_of(first % rows, SEGMENT)
            own = own_ref[chan // CORES, g, pl.ds(place, SEGMENT), :]
            sib = sib_ref[chan // CORES, g, pl.ds(place, SEGMENT), :]
            parts.append(jnp.where(chan % CORES == core, own, sib))
        whole = jnp.concatenate(parts, axis=0).astype(jnp.float32)
        return whole[:, :half], whole[:, half:]

    def store(ref, slot, index, g, value):
        rows_at = pl.ds(index * TILE, TILE)
        ref[slot, rows_at, g * lanes:g * lanes + half] = value[0].astype(jnp.bfloat16)
        ref[slot, rows_at, g * lanes + half:(g + 1) * lanes] = value[1].astype(jnp.bfloat16)

    copies = []
    pair = 2
    for t in range(tiles):
        slot = t % left_turned.shape[0]
        for g in range(groups):
            re, im = load(where_ref[1 + 2 * t], g)
            re, im = re * norm, im * norm
            for k in (4, 12):
                forward, backward = turn_by(re, im, *table[k], True)
                store(left_turned, slot, COARSE.index(k), g, forward)
                store(left_turned, slot, COARSE.index(-k), g, backward)
            re, im = load(where_ref[2 + 2 * t], g)
            store(right_turned, slot, FINE.index(0), g, (re, im))
            for k in (1, 2, 3):
                forward, backward = turn_by(re, im, *table[k], True)
                store(right_turned, slot, FINE.index(-k), g, forward)
                store(right_turned, slot, FINE.index(k), g, backward)
            store(right_turned, slot, FINE.index(-4), g, turn_by(re, im, *table[4], False)[0])
        for j in range(len(FINE) // pair):
            total = lax.dot_general(
                left_turned[slot],
                right_turned[slot, j * pair * TILE:(j + 1) * pair * TILE, :],
                (((1,), (1,)), ((), ())),
                preferred_element_type=jnp.float32,
            )
            for u in range(len(COARSE)):
                for s in range(pair):
                    staging[t, u, j * pair + s] = total[u * TILE:(u + 1) * TILE, s * TILE:(s + 1) * TILE]
            fine = pl.ds(j * pair, pair)
            copy = pltpu.make_async_copy(staging.at[t, :, fine], out_ref.at[t, :, fine], sem)
            copy.start()
            copies.append(copy)
    for copy in copies:
        copy.wait()


def correlate(own, sib, where, tiles, hours):
    _, groups, _, lanes = own.shape
    shape = (tiles, len(COARSE), len(FINE), TILE, TILE)
    norm = 1.0 / math.sqrt(F * hours)
    slots = min(tiles, 2)
    vmem = pl.BlockSpec(memory_space=pltpu.VMEM)
    out = pl.pallas_call(
        lambda *refs: correlate_kernel(norm, *refs),
        out_shape=jax.ShapeDtypeStruct(shape, jnp.float32),
        in_specs=[pl.BlockSpec(memory_space=pltpu.SMEM), vmem, vmem],
        out_specs=pl.BlockSpec(memory_space=pl.ANY),
        scratch_shapes=[
            pltpu.VMEM((slots, len(COARSE) * TILE, groups * lanes), jnp.bfloat16),
            pltpu.VMEM((slots, len(FINE) * TILE, groups * lanes), jnp.bfloat16),
            pltpu.VMEM(shape, jnp.float32),
            pltpu.SemaphoreType.DMA,
        ],
        compiler_params=pltpu.CompilerParams(vmem_limit_bytes=44 * 1024 * 1024),
        name="correlate",
    )(where, own, sib)
    return out.reshape(tiles, LAGS, TILE, TILE)


def gather(white):
    stack = lax.all_to_all(white, "tm", split_axis=0, concat_axis=0)
    chips = lax.axis_size("chan") // CORES
    same_core = [[chip * CORES + core for chip in range(chips)] for core in range(CORES)]
    own = lax.all_to_all(
        jnp.broadcast_to(stack[None], (chips, *stack.shape)),
        "chan", split_axis=0, concat_axis=0, axis_index_groups=same_core,
    )
    sib = lax.ppermute(own, "chan", [(i, i ^ 1) for i in range(chips * CORES)])
    return own, sib


def per_device(spectra, bad_channels, tile_list):
    groups = lax.axis_size("tm")
    hours = spectra.shape[1] * groups
    tiles = tile_list.shape[0] // groups
    white = whiten(spectra, bad_channels, groups)
    own, sib = gather(white)
    pairs = lax.dynamic_slice_in_dim(tile_list, lax.axis_index("tm") * tiles, tiles, axis=0)
    core = lax.axis_index("chan") % CORES
    where = jnp.concatenate([core.reshape(1), pairs.reshape(-1)]).astype(jnp.int32)
    return correlate(own, sib, where, tiles, hours)


def solution(mesh):
    placed = (P(None, "tm", None, "chan"), P("chan"), P("chan", None))
    return jax.shard_map(
        per_device,
        mesh=mesh,
        in_specs=placed,
        out_specs=P(("chan", "tm"), None, None, None),
        check_vma=False,
    )
```

```python
import math

import jax
import jax.numpy as jnp
from jax import lax
from jax.experimental import pallas as pl
from jax.experimental.pallas import tpu as pltpu
from jax.sharding import PartitionSpec as P

F = 64
LAGS = 32
TILE = 128
EPSILON = 1e-06
COARSE = (-12, -4, 4, 12)
FINE_PAIRS = ((-4, 0), (-1, 1), (-2, 2), (-3, 3))


def whiten_kernel(spectra_ref, bad_ref, out_ref):
    bins, hours, _, chans = spectra_ref.shape
    rows = bins * hours * 2
    values = spectra_ref[...].reshape(rows, chans).astype(jnp.float32)
    row = lax.broadcasted_iota(jnp.int32, (rows, chans), 0)
    hour = (row // 2) % hours
    squares = values * values
    keep = (1 - bad_ref[...]).astype(jnp.float32)
    scale = jnp.zeros((rows, chans), jnp.float32)
    for h in range(hours):
        power = jnp.sum(jnp.where(hour == h, squares, 0.0), axis=0, keepdims=True) * (1.0 / (2 * bins))
        scale = jnp.where(hour == h, lax.rsqrt(power + EPSILON) * keep, scale)
    white = (values * scale).astype(jnp.bfloat16)
    src = lax.broadcasted_iota(jnp.int32, (rows, rows), 0)
    dst = lax.broadcasted_iota(jnp.int32, (rows, rows), 1)
    move = jnp.where((src % 2) * (rows // 2) + src // 2 == dst, 1.0, 0.0).astype(jnp.bfloat16)
    out_ref[...] = lax.dot_general(
        white, move, (((0,), (0,)), ((), ())), preferred_element_type=jnp.float32
    ).astype(jnp.bfloat16)


def whiten(spectra, bad_channels):
    bins, hours, _, chans = spectra.shape
    return pl.pallas_call(
        whiten_kernel,
        out_shape=jax.ShapeDtypeStruct((chans, bins * hours * 2), jnp.bfloat16),
        name="whiten",
    )(spectra, bad_channels.reshape(1, chans))


def turn_by(re, im, cos, sin, both):
    rc, rs, ic, is_ = re * cos, re * sin, im * cos, im * sin
    forward = (rc - is_, rs + ic)
    return (forward, (rc + is_, ic - rs)) if both else (forward,)


def correlate_kernel(norm, where_ref, *refs):
    pieces = refs[:-6]
    out_ref, spectra, left_turned, right_turned, staging, sem = refs[-6:]
    tiles = staging.shape[0]
    groups, _, lanes = spectra.shape
    half = lanes // 2
    hours_dev = half // F
    bin_number = lax.broadcasted_iota(jnp.int32, (8, half), 1) // hours_dev + 1
    step = lax.broadcasted_iota(jnp.int32, (8, half), 0)
    step = jnp.where(step == 6, 12, step)
    turn = (step * bin_number) % (2 * F)
    angle = jnp.where(turn >= F, turn - 2 * F, turn).astype(jnp.float32) * (math.pi / F)
    cos, sin = jnp.cos(angle), jnp.sin(angle)
    table = {k: (cos[i:i + 1], sin[i:i + 1]) for k, i in ((1, 1), (2, 2), (3, 3), (4, 4), (12, 6))}

    chans = spectra.shape[1] // pieces[0].shape[1]
    first = 0
    for start in range(0, len(pieces), chans):
        depth, rows, _ = pieces[start].shape
        for k in range(chans):
            place = pl.multiple_of((where_ref[0] ^ k) * rows, 32)
            spectra[first:first + depth, pl.ds(place, rows), :] = pieces[start + k][...]
        first += depth

    def load(block, g):
        whole = spectra[g, pl.ds(pl.multiple_of(block * TILE, TILE), TILE), :].astype(jnp.float32)
        return whole[:, :half], whole[:, half:]

    def store(ref, slot, index, g, value):
        rows_at = pl.ds(index * TILE, TILE)
        ref[slot, rows_at, g * lanes:g * lanes + half] = value[0].astype(jnp.bfloat16)
        ref[slot, rows_at, g * lanes + half:(g + 1) * lanes] = value[1].astype(jnp.bfloat16)

    copies = []
    for t in range(tiles):
        slot = t % left_turned.shape[0]
        for g in range(groups):
            re, im = load(where_ref[1 + 2 * t], g)
            re, im = re * norm, im * norm
            for k in (4, 12):
                forward, backward = turn_by(re, im, *table[k], True)
                store(left_turned, slot, COARSE.index(k), g, forward)
                store(left_turned, slot, COARSE.index(-k), g, backward)
        for j in range(len(FINE_PAIRS)):
            for g in range(groups):
                re, im = load(where_ref[2 + 2 * t], g)
                if j == 0:
                    store(right_turned, slot, 0, g, turn_by(re, im, *table[4], False)[0])
                    store(right_turned, slot, 1, g, (re, im))
                else:
                    forward, backward = turn_by(re, im, *table[j], True)
                    store(right_turned, slot, 2 * j, g, forward)
                    store(right_turned, slot, 2 * j + 1, g, backward)
            total = lax.dot_general(
                left_turned[slot],
                right_turned[slot, 2 * j * TILE:2 * (j + 1) * TILE, :],
                (((1,), (1,)), ((), ())),
                preferred_element_type=jnp.float32,
            )
            for u in range(len(COARSE)):
                for s in range(2):
                    staging[t, u, 2 * j + s] = total[u * TILE:(u + 1) * TILE, s * TILE:(s + 1) * TILE]
            for s in range(2):
                fine = FINE_PAIRS[j][s] + 4
                copy = pltpu.make_async_copy(staging.at[t, :, 2 * j + s], out_ref.at[t, :, fine], sem)
                copy.start()
                copies.append(copy)
    for copy in copies:
        copy.wait()


def correlate(pieces, where, tiles, hours):
    groups = lax.axis_size("tm")
    _, rows, lanes = pieces[0].shape
    fine = 2 * len(FINE_PAIRS)
    shape = (tiles, len(COARSE), fine, TILE, TILE)
    norm = 1.0 / math.sqrt(F * hours)
    slots = min(tiles, 2)
    vmem = pl.BlockSpec(memory_space=pltpu.VMEM)
    out = pl.pallas_call(
        lambda *refs: correlate_kernel(norm, *refs),
        out_shape=jax.ShapeDtypeStruct(shape, jnp.float32),
        in_specs=[pl.BlockSpec(memory_space=pltpu.SMEM)] + [vmem] * len(pieces),
        out_specs=pl.BlockSpec(memory_space=pl.ANY),
        scratch_shapes=[
            pltpu.VMEM((groups, lax.axis_size("chan") * rows, lanes), jnp.bfloat16),
            pltpu.VMEM((slots, len(COARSE) * TILE, groups * lanes), jnp.bfloat16),
            pltpu.VMEM((slots, fine * TILE, groups * lanes), jnp.bfloat16),
            pltpu.VMEM(shape, jnp.float32),
            pltpu.SemaphoreType.DMA,
        ],
        compiler_params=pltpu.CompilerParams(vmem_limit_bytes=40 * 1024 * 1024),
        name="correlate",
    )(where, *pieces)
    return out.reshape(tiles, LAGS, TILE, TILE)


def swap(array, axis, k):
    return lax.ppermute(array, axis, [(i, i ^ k) for i in range(lax.axis_size(axis))])


def between_chips(half):
    pieces = {0: half}
    for k in range(2, lax.axis_size("chan"), 2):
        pieces[k] = swap(half, "chan", k)
    for k in list(pieces):
        pieces[k + 1] = swap(pieces[k], "chan", 1)
    return [pieces[k] for k in sorted(pieces)]


def gather(white):
    near = [white] + [swap(white, "tm", k) for k in (1,)]
    far = [swap(white, "tm", k) for k in range(2, lax.axis_size("tm"))]
    return between_chips(jnp.stack(near)) + between_chips(jnp.stack(far))


def per_device(spectra, bad_channels, tile_list):
    groups = lax.axis_size("tm")
    hours = spectra.shape[1] * groups
    tiles = tile_list.shape[0] // groups
    white = whiten(spectra, bad_channels)
    pieces = gather(white)
    pairs = lax.dynamic_slice_in_dim(tile_list, lax.axis_index("tm") * tiles, tiles, axis=0)
    where = jnp.concatenate([lax.axis_index("chan").reshape(1), pairs.reshape(-1)]).astype(jnp.int32)
    return correlate(pieces, where, tiles, hours)


def solution(mesh):
    placed = (P(None, "tm", None, "chan"), P("chan"), P("chan", None))
    return jax.shard_map(
        per_device,
        mesh=mesh,
        in_specs=placed,
        out_specs=P(("chan", "tm"), None, None, None),
        check_vma=False,
    )
```

```python
import math

import jax
import jax.numpy as jnp
from jax import lax
from jax.experimental import pallas as pl
from jax.experimental.pallas import tpu as pltpu
from jax.sharding import PartitionSpec as P

F = 64
LAGS = 32
TILE = 128
EPSILON = 1e-06
CORES = 2
COARSE = (-12, -4, 4, 12)
FINE_PAIRS = ((-4, 0), (-1, 1), (-2, 2), (-3, 3))


def whiten_kernel(spectra_ref, bad_ref, out_ref):
    bins, hours, _, chans = spectra_ref.shape
    rows = bins * hours * 2
    values = spectra_ref[...].reshape(rows, chans).astype(jnp.float32)
    row = lax.broadcasted_iota(jnp.int32, (rows, chans), 0)
    hour = (row // 2) % hours
    squares = values * values
    keep = (1 - bad_ref[...]).astype(jnp.float32)
    scale = jnp.zeros((rows, chans), jnp.float32)
    for h in range(hours):
        power = jnp.sum(jnp.where(hour == h, squares, 0.0), axis=0, keepdims=True) * (1.0 / (2 * bins))
        scale = jnp.where(hour == h, lax.rsqrt(power + EPSILON) * keep, scale)
    white = (values * scale).astype(jnp.bfloat16)
    src = lax.broadcasted_iota(jnp.int32, (rows, rows), 0)
    dst = lax.broadcasted_iota(jnp.int32, (rows, rows), 1)
    move = jnp.where((src % 2) * (rows // 2) + src // 2 == dst, 1.0, 0.0).astype(jnp.bfloat16)
    out_ref[...] = lax.dot_general(
        white, move, (((0,), (0,)), ((), ())), preferred_element_type=jnp.float32
    ).astype(jnp.bfloat16)


def whiten(spectra, bad_channels):
    bins, hours, _, chans = spectra.shape
    return pl.pallas_call(
        whiten_kernel,
        out_shape=jax.ShapeDtypeStruct((chans, bins * hours * 2), jnp.bfloat16),
        name="whiten",
    )(spectra, bad_channels.reshape(1, chans))


def turn_by(re, im, cos, sin, both):
    rc, rs, ic, is_ = re * cos, re * sin, im * cos, im * sin
    forward = (rc - is_, rs + ic)
    return (forward, (rc + is_, ic - rs)) if both else (forward,)


def correlate_kernel(norm, add, tiles, where_ref, spectra, *refs):
    out_ref, left_turned, right_turned, sem = refs[-4:]
    groups, _, lanes = spectra.shape
    half = lanes // 2
    hours_dev = half // F
    bin_number = lax.broadcasted_iota(jnp.int32, (8, half), 1) // hours_dev + 1
    step = lax.broadcasted_iota(jnp.int32, (8, half), 0)
    step = jnp.where(step == 6, 12, step)
    turn = (step * bin_number) % (2 * F)
    angle = jnp.where(turn >= F, turn - 2 * F, turn).astype(jnp.float32) * (math.pi / F)
    cos, sin = jnp.cos(angle), jnp.sin(angle)
    table = {k: (cos[i:i + 1], sin[i:i + 1]) for k, i in ((1, 1), (2, 2), (3, 3), (4, 4), (12, 6))}

    def load(block, g):
        whole = spectra[g, pl.ds(pl.multiple_of(block * TILE, TILE), TILE), :].astype(jnp.float32)
        return whole[:, :half], whole[:, half:]

    def store(ref, slot, index, g, value):
        rows_at = pl.ds(index * TILE, TILE)
        ref[slot, rows_at, g * lanes:g * lanes + half] = value[0].astype(jnp.bfloat16)
        ref[slot, rows_at, g * lanes + half:(g + 1) * lanes] = value[1].astype(jnp.bfloat16)

    copies = []
    for t in range(tiles):
        slot = t % left_turned.shape[0]
        for g in range(groups):
            re, im = load(where_ref[2 + 2 * t], g)
            re, im = re * norm, im * norm
            for k in (4, 12):
                forward, backward = turn_by(re, im, *table[k], True)
                store(left_turned, slot, COARSE.index(k), g, forward)
                store(left_turned, slot, COARSE.index(-k), g, backward)
        for j in range(len(FINE_PAIRS)):
            for g in range(groups):
                re, im = load(where_ref[3 + 2 * t], g)
                if j == 0:
                    store(right_turned, slot, 0, g, turn_by(re, im, *table[4], False)[0])
                    store(right_turned, slot, 1, g, (re, im))
                else:
                    forward, backward = turn_by(re, im, *table[j], True)
                    store(right_turned, slot, 2 * j, g, forward)
                    store(right_turned, slot, 2 * j + 1, g, backward)
            total = lax.dot_general(
                left_turned[slot],
                right_turned[slot, 2 * j * TILE:2 * (j + 1) * TILE, :],
                (((1,), (1,)), ((), ())),
                preferred_element_type=jnp.float32,
            )
            partial = refs[0] if add else out_ref
            for u in range(len(COARSE)):
                for s in range(2):
                    fine = FINE_PAIRS[j][s] + 4
                    value = total[u * TILE:(u + 1) * TILE, s * TILE:(s + 1) * TILE]
                    partial[t, u, fine] = partial[t, u, fine] + value if add else value
            if add:
                for s in range(2):
                    fine = FINE_PAIRS[j][s] + 4
                    copy = pltpu.make_async_copy(partial.at[t, :, fine], out_ref.at[t, :, fine], sem)
                    copy.start()
                    copies.append(copy)
    for copy in copies:
        copy.wait()


VMEM = pl.BlockSpec(memory_space=pltpu.VMEM)
SMEM = pl.BlockSpec(memory_space=pltpu.SMEM)


def correlate(spectra, where, tiles, hours, partial=None):
    groups, _, lanes = spectra.shape
    fine = 2 * len(FINE_PAIRS)
    shape = (tiles, len(COARSE), fine, TILE, TILE)
    norm = 1.0 / math.sqrt(F * hours)
    slots = min(tiles, 2)
    add = partial is not None
    more = (partial,) if add else ()
    return pl.pallas_call(
        lambda *refs: correlate_kernel(norm, add, tiles, *refs),
        out_shape=jax.ShapeDtypeStruct(shape, jnp.float32),
        in_specs=[SMEM, VMEM] + [VMEM] * add,
        out_specs=pl.BlockSpec(memory_space=pl.ANY) if add else VMEM,
        scratch_shapes=[
            pltpu.VMEM((slots, len(COARSE) * TILE, groups * lanes), jnp.bfloat16),
            pltpu.VMEM((slots, fine * TILE, groups * lanes), jnp.bfloat16),
            pltpu.SemaphoreType.DMA,
        ],
        compiler_params=pltpu.CompilerParams(vmem_limit_bytes=24 * 1024 * 1024),
        cost_estimate=pl.CostEstimate(
            flops=2 * tiles * TILE * TILE * LAGS * groups * lanes, bytes_accessed=0, transcendentals=0
        ),
        name="correlate_add" if add else "correlate",
    )(where, spectra, *more)


def pack_kernel(windows, sources, where_ref, *refs):
    out_ref = refs[-1]
    first = where_ref[1] == 0
    for w in range(windows):
        for core in range(CORES):
            one, two = sources[0][w, core], sources[1][w, core]
            out_ref[w, core] = jnp.where(first, refs[one][...], refs[two][...])


def pack(where, windows, sources, blocks):
    return pl.pallas_call(
        lambda *refs: pack_kernel(windows, sources, *refs),
        out_shape=jax.ShapeDtypeStruct((windows, CORES, *blocks[0].shape), jnp.bfloat16),
        in_specs=[SMEM] + [VMEM] * len(blocks),
        out_specs=VMEM,
        name="pack",
    )(where, *blocks)


def collect_kernel(where_ref, *refs):
    out_ref = refs[-1]
    _, cores, rows, _ = refs[0].shape
    for k, piece in enumerate(refs[:-1]):
        for core in range(cores):
            place = pl.multiple_of(((where_ref[0] ^ k) * cores + core) * rows, 32)
            out_ref[:, pl.ds(place, rows), :] = piece[:, core]


def collect(where, pieces):
    windows, cores, rows, lanes = pieces[0].shape
    return pl.pallas_call(
        collect_kernel,
        out_shape=jax.ShapeDtypeStruct((windows, len(pieces) * cores * rows, lanes), jnp.bfloat16),
        in_specs=[SMEM] + [VMEM] * len(pieces),
        out_specs=VMEM,
        name="collect",
    )(where, *pieces)


def swap(array, k):
    return lax.ppermute(array, "chan", [(i, i ^ k) for i in range(lax.axis_size("chan"))])


def fetch(block, sources):
    chans, groups = lax.axis_size("chan"), lax.axis_size("tm")
    pairs = []
    for chan in range(chans):
        for tm in range(groups):
            if chan % CORES in sources:
                k, core = sources[chan % CORES]
                source = chan // CORES * CORES + core
                pairs.append((source * groups + (tm ^ k), chan * groups + tm))
    return lax.ppermute(block, ("chan", "tm"), pairs)


def own_windows(white, where):
    groups = lax.axis_size("tm")
    windows = groups // 2
    near, far = list(range(1, windows)), list(range(windows, groups))
    steps = [((k, 0), (far[i], 1)) for i, k in enumerate(near)]
    steps += [((k, 1), (far[i], 0)) for i, k in enumerate(near + [0])]
    steps += [(None, (far[-1], 1))]
    blocks = [white]
    at = ({(0, 0): 0}, {})
    for step in steps:
        sources = {core: source for core, source in enumerate(step) if source}
        for core, source in sources.items():
            at[core][source] = len(blocks)
        blocks.append(fetch(white, sources))
    sources = tuple(
        {(w, core): at[own][(first + w, core)] for w in range(windows) for core in range(CORES)}
        for own, first in enumerate((0, windows))
    )
    return pack(where, windows, sources, blocks)


def per_device(spectra, bad_channels, tile_list):
    groups = lax.axis_size("tm")
    hours = spectra.shape[1] * groups
    tiles = tile_list.shape[0] // groups
    chan = lax.axis_index("chan")
    pairs = lax.dynamic_slice_in_dim(tile_list, lax.axis_index("tm") * tiles, tiles, axis=0)
    place = jnp.stack([chan // CORES, chan % CORES])
    where = jnp.concatenate([place, pairs.reshape(-1)]).astype(jnp.int32)
    packed = own_windows(whiten(spectra, bad_channels), where)
    pieces = [packed] + [swap(packed, k) for k in range(CORES, lax.axis_size("chan"), CORES)]
    one = collect(where, pieces)
    two = swap(one, 1)
    partial = correlate(one, where, tiles, hours)
    out = correlate(two, where, tiles, hours, partial)
    return out.reshape(tiles, LAGS, TILE, TILE)


def solution(mesh):
    placed = (P(None, "tm", None, "chan"), P("chan"), P("chan", None))
    return jax.shard_map(
        per_device,
        mesh=mesh,
        in_specs=placed,
        out_specs=P(("chan", "tm"), None, None, None),
        check_vma=False,
    )
```

```python
import math

import jax
import jax.numpy as jnp
from jax import lax
from jax.experimental import pallas as pl
from jax.experimental.pallas import tpu as pltpu
from jax.sharding import PartitionSpec as P

F = 64
LAGS = 32
TILE = 128
EPSILON = 1e-06
CORES = 2
SMALL = 4 * 1024 * 1024
COARSE = (-12, -4, 4, 12)
FINE_PAIRS = ((-4, 0), (-1, 1), (-2, 2), (-3, 3))


def whiten_kernel(spectra_ref, bad_ref, out_ref):
    bins, hours, _, chans = spectra_ref.shape
    rows = bins * hours * 2
    values = spectra_ref[...].reshape(rows, chans).astype(jnp.float32)
    row = lax.broadcasted_iota(jnp.int32, (rows, chans), 0)
    hour = (row // 2) % hours
    squares = values * values
    keep = (1 - bad_ref[...]).astype(jnp.float32)
    scale = jnp.zeros((rows, chans), jnp.float32)
    for h in range(hours):
        power = jnp.sum(jnp.where(hour == h, squares, 0.0), axis=0, keepdims=True) * (1.0 / (2 * bins))
        scale = jnp.where(hour == h, lax.rsqrt(power + EPSILON) * keep, scale)
    white = (values * scale).astype(jnp.bfloat16)
    src = lax.broadcasted_iota(jnp.int32, (rows, rows), 0)
    dst = lax.broadcasted_iota(jnp.int32, (rows, rows), 1)
    move = jnp.where((src % 2) * (rows // 2) + src // 2 == dst, 1.0, 0.0).astype(jnp.bfloat16)
    out_ref[...] = lax.dot_general(
        white, move, (((0,), (0,)), ((), ())), preferred_element_type=jnp.float32
    ).astype(jnp.bfloat16)


def whiten(spectra, bad_channels):
    bins, hours, _, chans = spectra.shape
    return pl.pallas_call(
        whiten_kernel,
        out_shape=jax.ShapeDtypeStruct((chans, bins * hours * 2), jnp.bfloat16),
        compiler_params=pltpu.CompilerParams(vmem_limit_bytes=SMALL),
        name="whiten",
    )(spectra, bad_channels.reshape(1, chans))


def turn_by(re, im, cos, sin, both):
    rc, rs, ic, is_ = re * cos, re * sin, im * cos, im * sin
    forward = (rc - is_, rs + ic)
    return (forward, (rc + is_, ic - rs)) if both else (forward,)


def correlate_kernel(norm, add, tiles, where_ref, spectra, *refs):
    out_ref, left_turned, right_turned, sem = refs[-4:]
    groups, _, lanes = spectra.shape
    half = lanes // 2
    hours_dev = half // F
    bin_number = lax.broadcasted_iota(jnp.int32, (8, half), 1) // hours_dev + 1
    step = lax.broadcasted_iota(jnp.int32, (8, half), 0)
    step = jnp.where(step == 6, 12, step)
    turn = (step * bin_number) % (2 * F)
    angle = jnp.where(turn >= F, turn - 2 * F, turn).astype(jnp.float32) * (math.pi / F)
    cos, sin = jnp.cos(angle), jnp.sin(angle)
    table = {k: (cos[i:i + 1], sin[i:i + 1]) for k, i in ((1, 1), (2, 2), (3, 3), (4, 4), (12, 6))}

    def load(block, g):
        whole = spectra[g, pl.ds(pl.multiple_of(block * TILE, TILE), TILE), :].astype(jnp.float32)
        return whole[:, :half], whole[:, half:]

    def store(ref, slot, index, g, value):
        rows_at = pl.ds(index * TILE, TILE)
        ref[slot, rows_at, g * lanes:g * lanes + half] = value[0].astype(jnp.bfloat16)
        ref[slot, rows_at, g * lanes + half:(g + 1) * lanes] = value[1].astype(jnp.bfloat16)

    copies = []
    for t in range(tiles):
        slot = t % left_turned.shape[0]
        for g in range(groups):
            re, im = load(where_ref[2 + 2 * t], g)
            re, im = re * norm, im * norm
            for k in (4, 12):
                forward, backward = turn_by(re, im, *table[k], True)
                store(left_turned, slot, COARSE.index(k), g, forward)
                store(left_turned, slot, COARSE.index(-k), g, backward)
        for j in range(len(FINE_PAIRS)):
            for g in range(groups):
                re, im = load(where_ref[3 + 2 * t], g)
                if j == 0:
                    store(right_turned, slot, 0, g, turn_by(re, im, *table[4], False)[0])
                    store(right_turned, slot, 1, g, (re, im))
                else:
                    forward, backward = turn_by(re, im, *table[j], True)
                    store(right_turned, slot, 2 * j, g, forward)
                    store(right_turned, slot, 2 * j + 1, g, backward)
            total = lax.dot_general(
                left_turned[slot],
                right_turned[slot, 2 * j * TILE:2 * (j + 1) * TILE, :],
                (((1,), (1,)), ((), ())),
                preferred_element_type=jnp.float32,
            )
            partial = refs[0] if add else out_ref
            for u in range(len(COARSE)):
                for s in range(2):
                    fine = FINE_PAIRS[j][s] + 4
                    value = total[u * TILE:(u + 1) * TILE, s * TILE:(s + 1) * TILE]
                    partial[t, u, fine] = partial[t, u, fine] + value if add else value
            if add:
                for s in range(2):
                    fine = FINE_PAIRS[j][s] + 4
                    copy = pltpu.make_async_copy(partial.at[t, :, fine], out_ref.at[t, :, fine], sem)
                    copy.start()
                    copies.append(copy)
    for copy in copies:
        copy.wait()


VMEM = pl.BlockSpec(memory_space=pltpu.VMEM)
SMEM = pl.BlockSpec(memory_space=pltpu.SMEM)


def correlate(spectra, where, tiles, hours, partial=None):
    groups, _, lanes = spectra.shape
    fine = 2 * len(FINE_PAIRS)
    shape = (tiles, len(COARSE), fine, TILE, TILE)
    norm = 1.0 / math.sqrt(F * hours)
    slots = min(tiles, 2)
    add = partial is not None
    more = (partial,) if add else ()
    return pl.pallas_call(
        lambda *refs: correlate_kernel(norm, add, tiles, *refs),
        out_shape=jax.ShapeDtypeStruct(shape, jnp.float32),
        in_specs=[SMEM, VMEM] + [VMEM] * add,
        out_specs=pl.BlockSpec(memory_space=pl.ANY) if add else VMEM,
        scratch_shapes=[
            pltpu.VMEM((slots, len(COARSE) * TILE, groups * lanes), jnp.bfloat16),
            pltpu.VMEM((slots, fine * TILE, groups * lanes), jnp.bfloat16),
            pltpu.SemaphoreType.DMA,
        ],
        compiler_params=pltpu.CompilerParams(vmem_limit_bytes=12 * 1024 * 1024),
        cost_estimate=pl.CostEstimate(
            flops=2 * tiles * TILE * TILE * LAGS * groups * lanes, bytes_accessed=0, transcendentals=0
        ),
        name="correlate_add" if add else "correlate",
    )(where, spectra, *more)


def pack_kernel(windows, sources, where_ref, *refs):
    out_ref = refs[-1]
    first = where_ref[1] == 0
    for w in range(windows):
        for core in range(CORES):
            one, two = sources[0][w, core], sources[1][w, core]
            out_ref[w, core] = jnp.where(first, refs[one][...], refs[two][...])


def pack(where, windows, sources, blocks):
    return pl.pallas_call(
        lambda *refs: pack_kernel(windows, sources, *refs),
        out_shape=jax.ShapeDtypeStruct((windows, CORES, *blocks[0].shape), jnp.bfloat16),
        in_specs=[SMEM] + [VMEM] * len(blocks),
        out_specs=VMEM,
        compiler_params=pltpu.CompilerParams(vmem_limit_bytes=SMALL),
        name="pack",
    )(where, *blocks)


def collect_kernel(where_ref, *refs):
    out_ref = refs[-1]
    _, cores, rows, _ = refs[0].shape
    for k, piece in enumerate(refs[:-1]):
        for core in range(cores):
            place = pl.multiple_of(((where_ref[0] ^ k) * cores + core) * rows, 32)
            out_ref[:, pl.ds(place, rows), :] = piece[:, core]


def collect(where, pieces):
    windows, cores, rows, lanes = pieces[0].shape
    return pl.pallas_call(
        collect_kernel,
        out_shape=jax.ShapeDtypeStruct((windows, len(pieces) * cores * rows, lanes), jnp.bfloat16),
        in_specs=[SMEM] + [VMEM] * len(pieces),
        out_specs=VMEM,
        compiler_params=pltpu.CompilerParams(vmem_limit_bytes=SMALL),
        name="collect",
    )(where, *pieces)


def swap(array, k):
    return lax.ppermute(array, "chan", [(i, i ^ k) for i in range(lax.axis_size("chan"))])


def fetch(block, sources):
    chans, groups = lax.axis_size("chan"), lax.axis_size("tm")
    pairs = []
    for chan in range(chans):
        for tm in range(groups):
            if chan % CORES in sources:
                k, core = sources[chan % CORES]
                source = chan // CORES * CORES + core
                pairs.append((source * groups + (tm ^ k), chan * groups + tm))
    return lax.ppermute(block, ("chan", "tm"), pairs)


def own_windows(white, where):
    groups = lax.axis_size("tm")
    windows = groups // 2
    near, far = list(range(1, windows)), list(range(windows, groups))
    steps = [((k, 0), (far[i], 1)) for i, k in enumerate(near)]
    steps += [((k, 1), (far[i], 0)) for i, k in enumerate(near + [0])]
    steps += [(None, (far[-1], 1))]
    blocks = [white]
    at = ({(0, 0): 0}, {})
    for step in steps:
        sources = {core: source for core, source in enumerate(step) if source}
        for core, source in sources.items():
            at[core][source] = len(blocks)
        blocks.append(fetch(white, sources))
    sources = tuple(
        {(w, core): at[own][(first + w, core)] for w in range(windows) for core in range(CORES)}
        for own, first in enumerate((0, windows))
    )
    return pack(where, windows, sources, blocks)


def per_device(spectra, bad_channels, tile_list):
    groups = lax.axis_size("tm")
    hours = spectra.shape[1] * groups
    tiles = tile_list.shape[0] // groups
    chan = lax.axis_index("chan")
    pairs = lax.dynamic_slice_in_dim(tile_list, lax.axis_index("tm") * tiles, tiles, axis=0)
    place = jnp.stack([chan // CORES, chan % CORES])
    where = jnp.concatenate([place, pairs.reshape(-1)]).astype(jnp.int32)
    packed = own_windows(whiten(spectra, bad_channels), where)
    pieces = [packed] + [swap(packed, k) for k in range(CORES, lax.axis_size("chan"), CORES)]
    one = collect(where, pieces)
    two = swap(one, 1)
    partial = correlate(one, where, tiles, hours)
    out = correlate(two, where, tiles, hours, partial)
    return out.reshape(tiles, LAGS, TILE, TILE)


def solution(mesh):
    placed = (P(None, "tm", None, "chan"), P("chan"), P("chan", None))
    return jax.shard_map(
        per_device,
        mesh=mesh,
        in_specs=placed,
        out_specs=P(("chan", "tm"), None, None, None),
        check_vma=False,
    )
```

```python
import math

import jax
import jax.numpy as jnp
from jax import lax
from jax.experimental import pallas as pl
from jax.experimental.pallas import tpu as pltpu
from jax.sharding import PartitionSpec as P

F = 64
LAGS = 32
TILE = 128
EPSILON = 1e-06
CORES = 2
SMALL = 4 * 1024 * 1024
VMEM = pl.BlockSpec(memory_space=pltpu.VMEM)
SMEM = pl.BlockSpec(memory_space=pltpu.SMEM)
COARSE = (-12, -4, 4, 12)
FINE_PAIRS = ((-4, 0), (-1, 1), (-2, 2), (-3, 3))


def whiten_kernel(spectra_ref, keep_ref, out_ref):
    bins, hours, _, chans = spectra_ref.shape
    rows = bins * hours * 2
    values = spectra_ref[...].reshape(rows, chans).astype(jnp.float32)
    row = lax.broadcasted_iota(jnp.int32, (rows, chans), 0)
    hour = (row // 2) % hours
    squares = values * values
    scale = jnp.zeros((rows, chans), jnp.float32)
    for h in range(hours):
        power = jnp.sum(jnp.where(hour == h, squares, 0.0), axis=0, keepdims=True) * (1.0 / (2 * bins))
        scale = jnp.where(hour == h, lax.rsqrt(power + EPSILON) * keep_ref[...], scale)
    white = (values * scale).astype(jnp.bfloat16)
    src = lax.broadcasted_iota(jnp.int32, (rows, rows), 0)
    dst = lax.broadcasted_iota(jnp.int32, (rows, rows), 1)
    move = jnp.where((src % 2) * (rows // 2) + src // 2 == dst, 1.0, 0.0).astype(jnp.bfloat16)
    out_ref[...] = lax.dot_general(
        white, move, (((0,), (0,)), ((), ())), preferred_element_type=jnp.float32
    ).astype(jnp.bfloat16)


def whiten(spectra, bad_channels):
    bins, hours, _, chans = spectra.shape
    keep = (1 - bad_channels).astype(jnp.float32).reshape(1, chans)
    return pl.pallas_call(
        whiten_kernel,
        out_shape=jax.ShapeDtypeStruct((chans, bins * hours * 2), jnp.bfloat16),
        in_specs=[VMEM, VMEM],
        out_specs=VMEM,
        compiler_params=pltpu.CompilerParams(vmem_limit_bytes=SMALL),
        name="whiten",
    )(spectra, keep)


def turn_by(re, im, cos, sin, both):
    rc, rs, ic, is_ = re * cos, re * sin, im * cos, im * sin
    forward = (rc - is_, rs + ic)
    return (forward, (rc + is_, ic - rs)) if both else (forward,)


def correlate_kernel(norm, add, tiles, where_ref, spectra, *refs):
    out_ref, left_turned, right_turned, sem = refs[-4:]
    groups, _, lanes = spectra.shape
    half = lanes // 2
    hours_dev = half // F
    bin_number = lax.broadcasted_iota(jnp.int32, (8, half), 1) // hours_dev + 1
    step = lax.broadcasted_iota(jnp.int32, (8, half), 0)
    step = jnp.where(step == 6, 12, step)
    turn = (step * bin_number) % (2 * F)
    angle = jnp.where(turn >= F, turn - 2 * F, turn).astype(jnp.float32) * (math.pi / F)
    cos, sin = jnp.cos(angle), jnp.sin(angle)
    table = {k: (cos[i:i + 1], sin[i:i + 1]) for k, i in ((1, 1), (2, 2), (3, 3), (4, 4), (12, 6))}

    def load(block, g):
        whole = spectra[g, pl.ds(pl.multiple_of(block * TILE, TILE), TILE), :].astype(jnp.float32)
        return whole[:, :half], whole[:, half:]

    def store(ref, slot, index, g, value):
        rows_at = pl.ds(index * TILE, TILE)
        ref[slot, rows_at, g * lanes:g * lanes + half] = value[0].astype(jnp.bfloat16)
        ref[slot, rows_at, g * lanes + half:(g + 1) * lanes] = value[1].astype(jnp.bfloat16)

    copies = []
    for t in range(tiles):
        slot = t % left_turned.shape[0]
        for g in range(groups):
            re, im = load(where_ref[2 + 2 * t], g)
            re, im = re * norm, im * norm
            for k in (4, 12):
                forward, backward = turn_by(re, im, *table[k], True)
                store(left_turned, slot, COARSE.index(k), g, forward)
                store(left_turned, slot, COARSE.index(-k), g, backward)
        for j in range(len(FINE_PAIRS)):
            for g in range(groups):
                re, im = load(where_ref[3 + 2 * t], g)
                if j == 0:
                    store(right_turned, slot, 0, g, turn_by(re, im, *table[4], False)[0])
                    store(right_turned, slot, 1, g, (re, im))
                else:
                    forward, backward = turn_by(re, im, *table[j], True)
                    store(right_turned, slot, 2 * j, g, forward)
                    store(right_turned, slot, 2 * j + 1, g, backward)
            total = lax.dot_general(
                left_turned[slot],
                right_turned[slot, 2 * j * TILE:2 * (j + 1) * TILE, :],
                (((1,), (1,)), ((), ())),
                preferred_element_type=jnp.float32,
            )
            partial = refs[0] if add else out_ref
            for u in range(len(COARSE)):
                for s in range(2):
                    fine = FINE_PAIRS[j][s] + 4
                    value = total[u * TILE:(u + 1) * TILE, s * TILE:(s + 1) * TILE]
                    partial[t, u, fine] = partial[t, u, fine] + value if add else value
            if add:
                for s in range(2):
                    fine = FINE_PAIRS[j][s] + 4
                    copy = pltpu.make_async_copy(partial.at[t, :, fine], out_ref.at[t, :, fine], sem)
                    copy.start()
                    copies.append(copy)
    for copy in copies:
        copy.wait()


def correlate(spectra, where, tiles, hours, partial=None):
    groups, _, lanes = spectra.shape
    fine = 2 * len(FINE_PAIRS)
    shape = (tiles, len(COARSE), fine, TILE, TILE)
    norm = 1.0 / math.sqrt(F * hours)
    slots = min(tiles, 2)
    add = partial is not None
    more = (partial,) if add else ()
    return pl.pallas_call(
        lambda *refs: correlate_kernel(norm, add, tiles, *refs),
        out_shape=jax.ShapeDtypeStruct(shape, jnp.float32),
        in_specs=[SMEM, VMEM] + [VMEM] * add,
        out_specs=pl.BlockSpec(memory_space=pl.ANY) if add else VMEM,
        scratch_shapes=[
            pltpu.VMEM((slots, len(COARSE) * TILE, groups * lanes), jnp.bfloat16),
            pltpu.VMEM((slots, fine * TILE, groups * lanes), jnp.bfloat16),
            pltpu.SemaphoreType.DMA,
        ],
        compiler_params=pltpu.CompilerParams(vmem_limit_bytes=12 * 1024 * 1024),
        cost_estimate=pl.CostEstimate(
            flops=2 * tiles * TILE * TILE * LAGS * groups * lanes, bytes_accessed=0, transcendentals=0
        ),
        name="correlate_add" if add else "correlate",
    )(where, spectra, *more)


def pack_kernel(choices, where_ref, *refs):
    out_ref = refs[-1]
    first = where_ref[1] == 0
    for slot, (one, two) in enumerate(choices):
        out_ref[slot] = jnp.where(first, refs[one][...], refs[two][...])


def pack(where, choices, blocks):
    return pl.pallas_call(
        lambda *refs: pack_kernel(choices, *refs),
        out_shape=jax.ShapeDtypeStruct((len(choices), *blocks[0].shape), jnp.bfloat16),
        in_specs=[SMEM] + [VMEM] * len(blocks),
        out_specs=VMEM,
        compiler_params=pltpu.CompilerParams(vmem_limit_bytes=SMALL),
        name="pack",
    )(where, *blocks)


def collect_kernel(where_ref, *refs):
    out_ref = refs[-1]
    _, cores, rows, _ = refs[0].shape
    for k, piece in enumerate(refs[:-1]):
        for core in range(cores):
            place = pl.multiple_of(((where_ref[0] ^ k) * cores + core) * rows, 32)
            out_ref[:, pl.ds(place, rows), :] = piece[:, core]


def collect(where, pieces):
    windows, cores, rows, lanes = pieces[0].shape
    return pl.pallas_call(
        collect_kernel,
        out_shape=jax.ShapeDtypeStruct((windows, len(pieces) * cores * rows, lanes), jnp.bfloat16),
        in_specs=[SMEM] + [VMEM] * len(pieces),
        out_specs=VMEM,
        compiler_params=pltpu.CompilerParams(vmem_limit_bytes=SMALL),
        name="collect",
    )(where, *pieces)


def swap(array, k):
    return lax.ppermute(array, "chan", [(i, i ^ k) for i in range(lax.axis_size("chan"))])


def fetch(block, offsets):
    chans, groups = lax.axis_size("chan"), lax.axis_size("tm")
    pairs = [
        (chan * groups + (tm ^ offsets[chan % CORES]), chan * groups + tm)
        for chan in range(chans)
        for tm in range(groups)
        if chan % CORES in offsets
    ]
    return lax.ppermute(block, ("chan", "tm"), pairs)


def own_windows(white, where):
    groups = lax.axis_size("tm")
    windows = groups // 2
    both = pack(where, [(0, 1), (1, 0)], [white, swap(white, 1)])
    blocks = [both]
    for k in range(windows):
        offsets = {1: windows + k} if k + 1 == windows else {0: k + 1, 1: windows + k}
        blocks.append(fetch(both, offsets))
    return pack(where, [(w, w + 1) for w in range(windows)], blocks)


def per_device(spectra, bad_channels, tile_list):
    groups = lax.axis_size("tm")
    hours = spectra.shape[1] * groups
    tiles = tile_list.shape[0] // groups
    chan = lax.axis_index("chan")
    pairs = lax.dynamic_slice_in_dim(tile_list, lax.axis_index("tm") * tiles, tiles, axis=0)
    place = jnp.stack([chan // CORES, chan % CORES])
    where = jnp.concatenate([place, pairs.reshape(-1)]).astype(jnp.int32)
    packed = own_windows(whiten(spectra, bad_channels), where)
    pieces = [packed] + [swap(packed, k) for k in range(CORES, lax.axis_size("chan"), CORES)]
    one = collect(where, pieces)
    two = swap(one, 1)
    partial = correlate(one, where, tiles, hours)
    out = correlate(two, where, tiles, hours, partial)
    return out.reshape(tiles, LAGS, TILE, TILE)


def solution(mesh):
    placed = (P(None, "tm", None, "chan"), P("chan"), P("chan", None))
    return jax.shard_map(
        per_device,
        mesh=mesh,
        in_specs=placed,
        out_specs=P(("chan", "tm"), None, None, None),
        check_vma=False,
    )
```

```python
import math

import jax
import jax.numpy as jnp
from jax import lax
from jax.experimental import pallas as pl
from jax.experimental.pallas import tpu as pltpu
from jax.sharding import PartitionSpec as P

F = 64
LAGS = 32
TILE = 128
EPSILON = 1e-06
SMALL = 4 * 1024 * 1024
VMEM = pl.BlockSpec(memory_space=pltpu.VMEM)
SMEM = pl.BlockSpec(memory_space=pltpu.SMEM)
COARSE = (-12, -4, 4, 12)
FINE_PAIRS = ((-4, 0), (-1, 1), (-2, 2), (-3, 3))


def whiten_kernel(spectra_hbm, bad_hbm, out_ref, spectra_ref, bad_ref, sems):
    copies = [
        pltpu.make_async_copy(spectra_hbm, spectra_ref, sems.at[0]),
        pltpu.make_async_copy(bad_hbm, bad_ref, sems.at[1]),
    ]
    for copy in copies:
        copy.start()
    bins, hours, _, chans = spectra_ref.shape
    rows = bins * hours * 2
    row = lax.broadcasted_iota(jnp.int32, (rows, chans), 0)
    hour = (row // 2) % hours
    src = lax.broadcasted_iota(jnp.int32, (rows, rows), 0)
    dst = lax.broadcasted_iota(jnp.int32, (rows, rows), 1)
    move = jnp.where((src % 2) * (rows // 2) + src // 2 == dst, 1.0, 0.0).astype(jnp.bfloat16)
    for copy in copies:
        copy.wait()
    values = spectra_ref[...].reshape(rows, chans).astype(jnp.float32)
    keep = (1 - bad_ref[...]).astype(jnp.float32)
    squares = values * values
    scale = jnp.zeros((rows, chans), jnp.float32)
    for h in range(hours):
        power = jnp.sum(jnp.where(hour == h, squares, 0.0), axis=0, keepdims=True) * (1.0 / (2 * bins))
        scale = jnp.where(hour == h, lax.rsqrt(power + EPSILON) * keep, scale)
    white = (values * scale).astype(jnp.bfloat16)
    out_ref[...] = lax.dot_general(
        white, move, (((0,), (0,)), ((), ())), preferred_element_type=jnp.float32
    ).astype(jnp.bfloat16)


def whiten(spectra, bad_channels):
    bins, hours, _, chans = spectra.shape
    spectra = pltpu.with_memory_space_constraint(spectra, pltpu.HBM)
    bad_channels = pltpu.with_memory_space_constraint(bad_channels.reshape(1, chans), pltpu.HBM)
    return pl.pallas_call(
        whiten_kernel,
        out_shape=jax.ShapeDtypeStruct((chans, bins * hours * 2), jnp.bfloat16),
        in_specs=[pl.BlockSpec(memory_space=pltpu.HBM)] * 2,
        out_specs=VMEM,
        scratch_shapes=[
            pltpu.VMEM(spectra.shape, spectra.dtype),
            pltpu.VMEM((1, chans), bad_channels.dtype),
            pltpu.SemaphoreType.DMA((2,)),
        ],
        compiler_params=pltpu.CompilerParams(vmem_limit_bytes=SMALL),
        name="whiten",
    )(spectra, bad_channels)


def turn_by(re, im, cos, sin, both):
    rc, rs, ic, is_ = re * cos, re * sin, im * cos, im * sin
    forward = (rc - is_, rs + ic)
    return (forward, (rc + is_, ic - rs)) if both else (forward,)


def correlate_kernel(norm, where_ref, *refs):
    pieces = refs[:-6]
    out_ref, spectra, left_turned, right_turned, staging, sem = refs[-6:]
    tiles = staging.shape[0]
    groups, _, lanes = spectra.shape
    half = lanes // 2
    hours_dev = half // F
    bin_number = lax.broadcasted_iota(jnp.int32, (8, half), 1) // hours_dev + 1
    step = lax.broadcasted_iota(jnp.int32, (8, half), 0)
    step = jnp.where(step == 6, 12, step)
    turn = (step * bin_number) % (2 * F)
    angle = jnp.where(turn >= F, turn - 2 * F, turn).astype(jnp.float32) * (math.pi / F)
    cos, sin = jnp.cos(angle), jnp.sin(angle)
    table = {k: (cos[i:i + 1], sin[i:i + 1]) for k, i in ((1, 1), (2, 2), (3, 3), (4, 4), (12, 6))}

    chans = spectra.shape[1] // pieces[0].shape[1]
    first = 0
    for start in range(0, len(pieces), chans):
        depth, rows, _ = pieces[start].shape
        for k in range(chans):
            place = pl.multiple_of((where_ref[0] ^ k) * rows, 32)
            spectra[first:first + depth, pl.ds(place, rows), :] = pieces[start + k][...]
        first += depth

    def load(block, g):
        whole = spectra[g, pl.ds(pl.multiple_of(block * TILE, TILE), TILE), :].astype(jnp.float32)
        return whole[:, :half], whole[:, half:]

    def store(ref, slot, index, g, value):
        rows_at = pl.ds(index * TILE, TILE)
        ref[slot, rows_at, g * lanes:g * lanes + half] = value[0].astype(jnp.bfloat16)
        ref[slot, rows_at, g * lanes + half:(g + 1) * lanes] = value[1].astype(jnp.bfloat16)

    copies = []
    for t in range(tiles):
        slot = t % left_turned.shape[0]
        for g in range(groups):
            re, im = load(where_ref[1 + 2 * t], g)
            re, im = re * norm, im * norm
            for k in (4, 12):
                forward, backward = turn_by(re, im, *table[k], True)
                store(left_turned, slot, COARSE.index(k), g, forward)
                store(left_turned, slot, COARSE.index(-k), g, backward)
        for j in range(len(FINE_PAIRS)):
            for g in range(groups):
                re, im = load(where_ref[2 + 2 * t], g)
                if j == 0:
                    store(right_turned, slot, 0, g, turn_by(re, im, *table[4], False)[0])
                    store(right_turned, slot, 1, g, (re, im))
                else:
                    forward, backward = turn_by(re, im, *table[j], True)
                    store(right_turned, slot, 2 * j, g, forward)
                    store(right_turned, slot, 2 * j + 1, g, backward)
            total = lax.dot_general(
                left_turned[slot],
                right_turned[slot, 2 * j * TILE:2 * (j + 1) * TILE, :],
                (((1,), (1,)), ((), ())),
                preferred_element_type=jnp.float32,
            )
            for u in range(len(COARSE)):
                for s in range(2):
                    staging[t, u, 2 * j + s] = total[u * TILE:(u + 1) * TILE, s * TILE:(s + 1) * TILE]
            for s in range(2):
                fine = FINE_PAIRS[j][s] + 4
                copy = pltpu.make_async_copy(staging.at[t, :, 2 * j + s], out_ref.at[t, :, fine], sem)
                copy.start()
                copies.append(copy)
    for copy in copies:
        copy.wait()


def correlate(pieces, where, tiles, hours):
    groups = lax.axis_size("tm")
    _, rows, lanes = pieces[0].shape
    fine = 2 * len(FINE_PAIRS)
    shape = (tiles, len(COARSE), fine, TILE, TILE)
    norm = 1.0 / math.sqrt(F * hours)
    slots = min(tiles, 2)
    chans = lax.axis_size("chan") * rows
    turned = slots * (len(COARSE) + fine) * TILE * groups * lanes
    scratch = 2 * (groups * chans * lanes + turned) + 4 * math.prod(shape)
    out = pl.pallas_call(
        lambda *refs: correlate_kernel(norm, *refs),
        out_shape=jax.ShapeDtypeStruct(shape, jnp.float32),
        in_specs=[SMEM] + [VMEM] * len(pieces),
        out_specs=pl.BlockSpec(memory_space=pl.ANY),
        scratch_shapes=[
            pltpu.VMEM((groups, chans, lanes), jnp.bfloat16),
            pltpu.VMEM((slots, len(COARSE) * TILE, groups * lanes), jnp.bfloat16),
            pltpu.VMEM((slots, fine * TILE, groups * lanes), jnp.bfloat16),
            pltpu.VMEM(shape, jnp.float32),
            pltpu.SemaphoreType.DMA,
        ],
        compiler_params=pltpu.CompilerParams(vmem_limit_bytes=scratch + SMALL),
        name="correlate",
    )(where, *pieces)
    return out.reshape(tiles, LAGS, TILE, TILE)


def swap(array, axis, k):
    return lax.ppermute(array, axis, [(i, i ^ k) for i in range(lax.axis_size(axis))])


def between_chips(half):
    pieces = {0: half}
    for k in range(2, lax.axis_size("chan"), 2):
        pieces[k] = swap(half, "chan", k)
    for k in list(pieces):
        pieces[k + 1] = swap(pieces[k], "chan", 1)
    return [pieces[k] for k in sorted(pieces)]


def stack_kernel(one_ref, two_ref, out_ref):
    depth = one_ref.shape[0]
    out_ref[:depth] = one_ref[...]
    out_ref[depth:] = two_ref[...]


def stack(one, two):
    return pl.pallas_call(
        stack_kernel,
        out_shape=jax.ShapeDtypeStruct((2 * one.shape[0], *one.shape[1:]), one.dtype),
        in_specs=[VMEM, VMEM],
        out_specs=VMEM,
        compiler_params=pltpu.CompilerParams(vmem_limit_bytes=SMALL),
        name="stack",
    )(one, two)


def gather(white):
    half = white[None]
    k = lax.axis_size("tm") // 2
    while k > 1:
        half = stack(half, swap(half, "tm", k))
        k //= 2
    return between_chips(half) + between_chips(swap(half, "tm", 1))


def per_device(spectra, bad_channels, tile_list):
    groups = lax.axis_size("tm")
    hours = spectra.shape[1] * groups
    tiles = tile_list.shape[0] // groups
    white = whiten(spectra, bad_channels)
    pieces = gather(white)
    pairs = lax.dynamic_slice_in_dim(tile_list, lax.axis_index("tm") * tiles, tiles, axis=0)
    where = jnp.concatenate([lax.axis_index("chan").reshape(1), pairs.reshape(-1)]).astype(jnp.int32)
    return correlate(pieces, where, tiles, hours)


def solution(mesh):
    placed = (P(None, "tm", None, "chan"), P("chan"), P("chan", None))
    return jax.shard_map(
        per_device,
        mesh=mesh,
        in_specs=placed,
        out_specs=P(("chan", "tm"), None, None, None),
        check_vma=False,
    )
```

```python
import math

import jax
import jax.numpy as jnp
from jax import lax
from jax.experimental import pallas as pl
from jax.experimental.pallas import tpu as pltpu
from jax.sharding import PartitionSpec as P

F = 64
LAGS = 32
TILE = 128
EPSILON = 1e-06
CORES = 2
SMALL = 4 * 1024 * 1024
VMEM = pl.BlockSpec(memory_space=pltpu.VMEM)
SMEM = pl.BlockSpec(memory_space=pltpu.SMEM)
COARSE = (-12, -4, 4, 12)
FINE_PAIRS = ((-4, 0), (-1, 1), (-2, 2), (-3, 3))


def whiten_kernel(spectra_hbm, bad_hbm, out_ref, spectra_ref, bad_ref, sems):
    copies = [
        pltpu.make_async_copy(spectra_hbm, spectra_ref, sems.at[0]),
        pltpu.make_async_copy(bad_hbm, bad_ref, sems.at[1]),
    ]
    for copy in copies:
        copy.start()
    bins, hours, _, chans = spectra_ref.shape
    rows = bins * hours * 2
    row = lax.broadcasted_iota(jnp.int32, (rows, chans), 0)
    hour = (row // 2) % hours
    src = lax.broadcasted_iota(jnp.int32, (rows, rows), 0)
    dst = lax.broadcasted_iota(jnp.int32, (rows, rows), 1)
    move = jnp.where((src % 2) * (rows // 2) + src // 2 == dst, 1.0, 0.0).astype(jnp.bfloat16)
    for copy in copies:
        copy.wait()
    values = spectra_ref[...].reshape(rows, chans).astype(jnp.float32)
    keep = (1 - bad_ref[...]).astype(jnp.float32)
    squares = values * values
    scale = jnp.zeros((rows, chans), jnp.float32)
    for h in range(hours):
        power = jnp.sum(jnp.where(hour == h, squares, 0.0), axis=0, keepdims=True) * (1.0 / (2 * bins))
        scale = jnp.where(hour == h, lax.rsqrt(power + EPSILON) * keep, scale)
    white = (values * scale).astype(jnp.bfloat16)
    out_ref[...] = lax.dot_general(
        white, move, (((0,), (0,)), ((), ())), preferred_element_type=jnp.float32
    ).astype(jnp.bfloat16)


def whiten(spectra, bad_channels):
    bins, hours, _, chans = spectra.shape
    spectra = pltpu.with_memory_space_constraint(spectra, pltpu.HBM)
    bad_channels = pltpu.with_memory_space_constraint(bad_channels.reshape(1, chans), pltpu.HBM)
    return pl.pallas_call(
        whiten_kernel,
        out_shape=jax.ShapeDtypeStruct((chans, bins * hours * 2), jnp.bfloat16),
        in_specs=[pl.BlockSpec(memory_space=pltpu.HBM)] * 2,
        out_specs=VMEM,
        scratch_shapes=[
            pltpu.VMEM(spectra.shape, spectra.dtype),
            pltpu.VMEM((1, chans), bad_channels.dtype),
            pltpu.SemaphoreType.DMA((2,)),
        ],
        compiler_params=pltpu.CompilerParams(vmem_limit_bytes=SMALL),
        name="whiten",
    )(spectra, bad_channels)


def turn_by(re, im, cos, sin, both):
    rc, rs, ic, is_ = re * cos, re * sin, im * cos, im * sin
    forward = (rc - is_, rs + ic)
    return (forward, (rc + is_, ic - rs)) if both else (forward,)


def correlate_kernel(norm, add, tiles, where_ref, *refs):
    pieces = refs[:-5 - add]
    out_ref, spectra, left_turned, right_turned, sem = refs[-5:]
    groups, _, lanes = spectra.shape
    half = lanes // 2
    hours_dev = half // F
    bin_number = lax.broadcasted_iota(jnp.int32, (8, half), 1) // hours_dev + 1
    step = lax.broadcasted_iota(jnp.int32, (8, half), 0)
    step = jnp.where(step == 6, 12, step)
    turn = (step * bin_number) % (2 * F)
    angle = jnp.where(turn >= F, turn - 2 * F, turn).astype(jnp.float32) * (math.pi / F)
    cos, sin = jnp.cos(angle), jnp.sin(angle)
    table = {k: (cos[i:i + 1], sin[i:i + 1]) for k, i in ((1, 1), (2, 2), (3, 3), (4, 4), (12, 6))}

    rows = pieces[0].shape[1]
    for core, piece in enumerate(pieces):
        for k in range(piece.shape[0] // groups):
            place = pl.multiple_of((where_ref[0] ^ (CORES * k + core)) * rows, 32)
            spectra[:, pl.ds(place, rows), :] = piece[k * groups:(k + 1) * groups]

    def load(block, g):
        whole = spectra[g, pl.ds(pl.multiple_of(block * TILE, TILE), TILE), :].astype(jnp.float32)
        return whole[:, :half], whole[:, half:]

    def store(ref, slot, index, g, value):
        rows_at = pl.ds(index * TILE, TILE)
        ref[slot, rows_at, g * lanes:g * lanes + half] = value[0].astype(jnp.bfloat16)
        ref[slot, rows_at, g * lanes + half:(g + 1) * lanes] = value[1].astype(jnp.bfloat16)

    copies = []
    for t in range(tiles):
        slot = t % left_turned.shape[0]
        for g in range(groups):
            re, im = load(where_ref[1 + 2 * t], g)
            re, im = re * norm, im * norm
            for k in (4, 12):
                forward, backward = turn_by(re, im, *table[k], True)
                store(left_turned, slot, COARSE.index(k), g, forward)
                store(left_turned, slot, COARSE.index(-k), g, backward)
        for j in range(len(FINE_PAIRS)):
            for g in range(groups):
                re, im = load(where_ref[2 + 2 * t], g)
                if j == 0:
                    store(right_turned, slot, 0, g, turn_by(re, im, *table[4], False)[0])
                    store(right_turned, slot, 1, g, (re, im))
                else:
                    forward, backward = turn_by(re, im, *table[j], True)
                    store(right_turned, slot, 2 * j, g, forward)
                    store(right_turned, slot, 2 * j + 1, g, backward)
            total = lax.dot_general(
                left_turned[slot],
                right_turned[slot, 2 * j * TILE:2 * (j + 1) * TILE, :],
                (((1,), (1,)), ((), ())),
                preferred_element_type=jnp.float32,
            )
            partial = refs[-6] if add else out_ref
            for u in range(len(COARSE)):
                for s in range(2):
                    fine = FINE_PAIRS[j][s] + 4
                    value = total[u * TILE:(u + 1) * TILE, s * TILE:(s + 1) * TILE]
                    partial[t, u, fine] = partial[t, u, fine] + value if add else value
            if add:
                for s in range(2):
                    fine = FINE_PAIRS[j][s] + 4
                    copy = pltpu.make_async_copy(partial.at[t, :, fine], out_ref.at[t, :, fine], sem)
                    copy.start()
                    copies.append(copy)
    for copy in copies:
        copy.wait()


def correlate(pieces, groups, where, tiles, hours, partial=None):
    depth, rows, lanes = pieces[0].shape
    fine = 2 * len(FINE_PAIRS)
    shape = (tiles, len(COARSE), fine, TILE, TILE)
    norm = 1.0 / math.sqrt(F * hours)
    slots = min(tiles, 2)
    chans = len(pieces) * depth // groups * rows
    scratch = 2 * (groups * chans * lanes + slots * (len(COARSE) + fine) * TILE * groups * lanes)
    add = partial is not None
    more = (partial,) if add else ()
    return pl.pallas_call(
        lambda *refs: correlate_kernel(norm, add, tiles, *refs),
        out_shape=jax.ShapeDtypeStruct(shape, jnp.float32),
        in_specs=[SMEM] + [VMEM] * (len(pieces) + add),
        out_specs=pl.BlockSpec(memory_space=pl.ANY) if add else VMEM,
        scratch_shapes=[
            pltpu.VMEM((groups, chans, lanes), jnp.bfloat16),
            pltpu.VMEM((slots, len(COARSE) * TILE, groups * lanes), jnp.bfloat16),
            pltpu.VMEM((slots, fine * TILE, groups * lanes), jnp.bfloat16),
            pltpu.SemaphoreType.DMA,
        ],
        compiler_params=pltpu.CompilerParams(vmem_limit_bytes=scratch + SMALL),
        cost_estimate=pl.CostEstimate(
            flops=0, bytes_accessed=0, transcendentals=0
        ),
        name="correlate_add" if add else "correlate",
    )(where, *pieces, *more)


def swap(array, axis, k):
    return lax.ppermute(array, axis, [(i, i ^ k) for i in range(lax.axis_size(axis))])


def stack_kernel(*refs):
    out_ref = refs[-1]
    first = 0
    for block in refs[:-1]:
        out_ref[first:first + block.shape[0]] = block[...]
        first += block.shape[0]


def stack(blocks):
    depth = sum(block.shape[0] for block in blocks)
    return pl.pallas_call(
        stack_kernel,
        out_shape=jax.ShapeDtypeStruct((depth, *blocks[0].shape[1:]), blocks[0].dtype),
        in_specs=[VMEM] * len(blocks),
        out_specs=VMEM,
        compiler_params=pltpu.CompilerParams(vmem_limit_bytes=SMALL),
        name="stack",
    )(*blocks)


def halves(white):
    groups = lax.axis_size("tm")
    blocks = [white[None]] + [swap(white[None], "tm", k) for k in range(1, groups)]
    return [stack(blocks[first:first + groups // 2]) for first in (0, groups // 2)]


def between_devices(half):
    own = stack([half] + [swap(half, "chan", k) for k in range(CORES, lax.axis_size("chan"), CORES)])
    return own, swap(own, "chan", 1)


def per_device(spectra, bad_channels, tile_list):
    groups = lax.axis_size("tm")
    hours = spectra.shape[1] * groups
    tiles = tile_list.shape[0] // groups
    white = whiten(spectra, bad_channels)
    pairs = lax.dynamic_slice_in_dim(tile_list, lax.axis_index("tm") * tiles, tiles, axis=0)
    where = jnp.concatenate([lax.axis_index("chan").reshape(1), pairs.reshape(-1)]).astype(jnp.int32)
    near, far = [between_devices(half) for half in halves(white)]
    partial = correlate(near, groups // 2, where, tiles, hours)
    out = correlate(far, groups // 2, where, tiles, hours, partial)
    return out.reshape(tiles, LAGS, TILE, TILE)


def solution(mesh):
    placed = (P(None, "tm", None, "chan"), P("chan"), P("chan", None))
    return jax.shard_map(
        per_device,
        mesh=mesh,
        in_specs=placed,
        out_specs=P(("chan", "tm"), None, None, None),
        check_vma=False,
    )
```

```python
import math

import jax
import jax.numpy as jnp
from jax import lax
from jax.experimental import pallas as pl
from jax.experimental.pallas import tpu as pltpu
from jax.sharding import PartitionSpec as P

F = 64
LAGS = 32
TILE = 128
EPSILON = 1e-06
CORES = 2
SMALL = 4 * 1024 * 1024
VMEM = pl.BlockSpec(memory_space=pltpu.VMEM)
SMEM = pl.BlockSpec(memory_space=pltpu.SMEM)
COARSE = (-12, -4, 4, 12)
FINE_PAIRS = ((-4, 0), (-1, 1), (-2, 2), (-3, 3))


def whiten_kernel(spectra_hbm, bad_hbm, out_ref, spectra_ref, bad_ref, sems):
    copies = [
        pltpu.make_async_copy(spectra_hbm, spectra_ref, sems.at[0]),
        pltpu.make_async_copy(bad_hbm, bad_ref, sems.at[1]),
    ]
    for copy in copies:
        copy.start()
    bins, hours, _, chans = spectra_ref.shape
    rows = bins * hours * 2
    row = lax.broadcasted_iota(jnp.int32, (rows, chans), 0)
    hour = (row // 2) % hours
    src = lax.broadcasted_iota(jnp.int32, (rows, rows), 0)
    dst = lax.broadcasted_iota(jnp.int32, (rows, rows), 1)
    move = jnp.where((src % 2) * (rows // 2) + src // 2 == dst, 1.0, 0.0).astype(jnp.bfloat16)
    for copy in copies:
        copy.wait()
    values = spectra_ref[...].reshape(rows, chans).astype(jnp.float32)
    keep = (1 - bad_ref[...]).astype(jnp.float32)
    squares = values * values
    scale = jnp.zeros((rows, chans), jnp.float32)
    for h in range(hours):
        power = jnp.sum(jnp.where(hour == h, squares, 0.0), axis=0, keepdims=True) * (1.0 / (2 * bins))
        scale = jnp.where(hour == h, lax.rsqrt(power + EPSILON) * keep, scale)
    white = (values * scale).astype(jnp.bfloat16)
    out_ref[...] = lax.dot_general(
        white, move, (((0,), (0,)), ((), ())), preferred_element_type=jnp.float32
    ).astype(jnp.bfloat16)


def whiten(spectra, bad_channels):
    bins, hours, _, chans = spectra.shape
    spectra = pltpu.with_memory_space_constraint(spectra, pltpu.HBM)
    bad_channels = pltpu.with_memory_space_constraint(bad_channels.reshape(1, chans), pltpu.HBM)
    return pl.pallas_call(
        whiten_kernel,
        out_shape=jax.ShapeDtypeStruct((chans, bins * hours * 2), jnp.bfloat16),
        in_specs=[pl.BlockSpec(memory_space=pltpu.HBM)] * 2,
        out_specs=VMEM,
        scratch_shapes=[
            pltpu.VMEM(spectra.shape, spectra.dtype),
            pltpu.VMEM((1, chans), bad_channels.dtype),
            pltpu.SemaphoreType.DMA((2,)),
        ],
        compiler_params=pltpu.CompilerParams(vmem_limit_bytes=SMALL),
        name="whiten",
    )(spectra, bad_channels)


def turn_by(re, im, cos, sin, both):
    rc, rs, ic, is_ = re * cos, re * sin, im * cos, im * sin
    forward = (rc - is_, rs + ic)
    return (forward, (rc + is_, ic - rs)) if both else (forward,)


def correlate_kernel(norm, add, tiles, where_ref, *refs):
    pieces = refs[:-5 - add]
    out_ref, spectra, left_turned, right_turned, sem = refs[-5:]
    groups, _, lanes = spectra.shape
    half = lanes // 2
    hours_dev = half // F
    bin_number = lax.broadcasted_iota(jnp.int32, (8, half), 1) // hours_dev + 1
    step = lax.broadcasted_iota(jnp.int32, (8, half), 0)
    step = jnp.where(step == 6, 12, step)
    turn = (step * bin_number) % (2 * F)
    angle = jnp.where(turn >= F, turn - 2 * F, turn).astype(jnp.float32) * (math.pi / F)
    cos, sin = jnp.cos(angle), jnp.sin(angle)
    table = {k: (cos[i:i + 1], sin[i:i + 1]) for k, i in ((1, 1), (2, 2), (3, 3), (4, 4), (12, 6))}

    rows = pieces[0].shape[1]
    for core, piece in enumerate(pieces):
        for k in range(piece.shape[0] // groups):
            place = pl.multiple_of((where_ref[0] ^ (CORES * k + core)) * rows, 32)
            spectra[:, pl.ds(place, rows), :] = piece[k * groups:(k + 1) * groups]

    def load(block, g):
        whole = spectra[g, pl.ds(pl.multiple_of(block * TILE, TILE), TILE), :].astype(jnp.float32)
        return whole[:, :half], whole[:, half:]

    def store(ref, slot, index, g, value):
        rows_at = pl.ds(index * TILE, TILE)
        ref[slot, rows_at, g * lanes:g * lanes + half] = value[0].astype(jnp.bfloat16)
        ref[slot, rows_at, g * lanes + half:(g + 1) * lanes] = value[1].astype(jnp.bfloat16)

    def turn_left(t):
        for g in range(groups):
            re, im = load(where_ref[1 + 2 * t], g)
            for k in (4, 12):
                forward, backward = turn_by(re, im, *(norm * part for part in table[k]), True)
                store(left_turned, t % slots, COARSE.index(k), g, forward)
                store(left_turned, t % slots, COARSE.index(-k), g, backward)

    def turn_right(t, j):
        for g in range(groups):
            re, im = load(where_ref[2 + 2 * t], g)
            if j == 0:
                store(right_turned, t % slots, 0, g, turn_by(re, im, *table[4], False)[0])
                store(right_turned, t % slots, 1, g, (re, im))
            else:
                forward, backward = turn_by(re, im, *table[j], True)
                store(right_turned, t % slots, 2 * j, g, forward)
                store(right_turned, t % slots, 2 * j + 1, g, backward)

    slots = left_turned.shape[0]
    partial = refs[-6] if add else out_ref
    copies = []
    steps = [(t, j) for t in range(tiles) for j in range(len(FINE_PAIRS))]
    turn_left(0)
    turn_right(0, 0)
    for (t, j), after in zip(steps, steps[1:] + [None]):
        if after:
            if after[1] == 0:
                turn_left(after[0])
            turn_right(*after)
        total = lax.dot_general(
            left_turned[t % slots],
            right_turned[t % slots, 2 * j * TILE:2 * (j + 1) * TILE, :],
            (((1,), (1,)), ((), ())),
            preferred_element_type=jnp.float32,
        )
        for s in range(2):
            fine = FINE_PAIRS[j][s] + 4
            for u in range(len(COARSE)):
                value = total[u * TILE:(u + 1) * TILE, s * TILE:(s + 1) * TILE]
                partial[t, u, fine] = partial[t, u, fine] + value if add else value
            if add:
                copy = pltpu.make_async_copy(partial.at[t, :, fine], out_ref.at[t, :, fine], sem)
                copy.start()
                copies.append(copy)
    for copy in copies:
        copy.wait()


def correlate(pieces, groups, where, tiles, hours, partial=None):
    depth, rows, lanes = pieces[0].shape
    fine = 2 * len(FINE_PAIRS)
    shape = (tiles, len(COARSE), fine, TILE, TILE)
    norm = 1.0 / math.sqrt(F * hours)
    slots = min(tiles, 2)
    chans = len(pieces) * depth // groups * rows
    scratch = 2 * (groups * chans * lanes + slots * (len(COARSE) + fine) * TILE * groups * lanes)
    add = partial is not None
    more = (partial,) if add else ()
    return pl.pallas_call(
        lambda *refs: correlate_kernel(norm, add, tiles, *refs),
        out_shape=jax.ShapeDtypeStruct(shape, jnp.float32),
        in_specs=[SMEM] + [VMEM] * (len(pieces) + add),
        out_specs=pl.BlockSpec(memory_space=pl.ANY) if add else VMEM,
        scratch_shapes=[
            pltpu.VMEM((groups, chans, lanes), jnp.bfloat16),
            pltpu.VMEM((slots, len(COARSE) * TILE, groups * lanes), jnp.bfloat16),
            pltpu.VMEM((slots, fine * TILE, groups * lanes), jnp.bfloat16),
            pltpu.SemaphoreType.DMA,
        ],
        compiler_params=pltpu.CompilerParams(vmem_limit_bytes=scratch + SMALL),
        cost_estimate=pl.CostEstimate(
            flops=0, bytes_accessed=0, transcendentals=0
        ),
        name="correlate_add" if add else "correlate",
    )(where, *pieces, *more)


def swap(array, axis, k):
    return lax.ppermute(array, axis, [(i, i ^ k) for i in range(lax.axis_size(axis))])


def stack_kernel(*refs):
    out_ref = refs[-1]
    first = 0
    for block in refs[:-1]:
        out_ref[first:first + block.shape[0]] = block[...]
        first += block.shape[0]


def stack(blocks, flops=0):
    depth = sum(block.shape[0] for block in blocks)
    return pl.pallas_call(
        stack_kernel,
        out_shape=jax.ShapeDtypeStruct((depth, *blocks[0].shape[1:]), blocks[0].dtype),
        in_specs=[VMEM] * len(blocks),
        out_specs=VMEM,
        compiler_params=pltpu.CompilerParams(vmem_limit_bytes=SMALL),
        cost_estimate=pl.CostEstimate(flops=flops, bytes_accessed=0, transcendentals=0),
        name="stack",
    )(*blocks)


def halves(white):
    groups = lax.axis_size("tm")
    blocks = [white[None]] + [swap(white[None], "tm", k) for k in range(1, groups)]
    return stack(blocks[:groups // 2]), stack(blocks[groups // 2:], flops=10**9)


def between_devices(half):
    own = stack([half] + [swap(half, "chan", k) for k in range(CORES, lax.axis_size("chan"), CORES)])
    return own, swap(own, "chan", 1)


def per_device(spectra, bad_channels, tile_list):
    groups = lax.axis_size("tm")
    hours = spectra.shape[1] * groups
    tiles = tile_list.shape[0] // groups
    white = whiten(spectra, bad_channels)
    pairs = lax.dynamic_slice_in_dim(tile_list, lax.axis_index("tm") * tiles, tiles, axis=0)
    where = jnp.concatenate([lax.axis_index("chan").reshape(1), pairs.reshape(-1)]).astype(jnp.int32)
    near, far = [between_devices(half) for half in halves(white)]
    partial = correlate(near, groups // 2, where, tiles, hours)
    out = correlate(far, groups // 2, where, tiles, hours, partial)
    return out.reshape(tiles, LAGS, TILE, TILE)


def solution(mesh):
    placed = (P(None, "tm", None, "chan"), P("chan"), P("chan", None))
    return jax.shard_map(
        per_device,
        mesh=mesh,
        in_specs=placed,
        out_specs=P(("chan", "tm"), None, None, None),
        check_vma=False,
    )
```

```python
import math

import jax
import jax.numpy as jnp
from jax import lax
from jax.experimental import pallas as pl
from jax.experimental.pallas import tpu as pltpu
from jax.sharding import PartitionSpec as P

F = 64
LAGS = 32
TILE = 128
EPSILON = 1e-06
CORES = 2
SMALL = 4 * 1024 * 1024
VMEM = pl.BlockSpec(memory_space=pltpu.VMEM)
COARSE = (-12, -4, 4, 12)
FINE_PAIRS = ((-4, 0), (-1, 1), (-2, 2), (-3, 3))


def whiten_kernel(spectra_hbm, bad_hbm, out_ref, spectra_ref, bad_ref, sems):
    copies = [
        pltpu.make_async_copy(spectra_hbm, spectra_ref, sems.at[0]),
        pltpu.make_async_copy(bad_hbm, bad_ref, sems.at[1]),
    ]
    for copy in copies:
        copy.start()
    bins, hours, _, chans = spectra_ref.shape
    rows = bins * hours * 2
    row = lax.broadcasted_iota(jnp.int32, (rows, chans), 0)
    hour = (row // 2) % hours
    src = lax.broadcasted_iota(jnp.int32, (rows, rows), 0)
    dst = lax.broadcasted_iota(jnp.int32, (rows, rows), 1)
    move = jnp.where((src % 2) * (rows // 2) + src // 2 == dst, 1.0, 0.0).astype(jnp.bfloat16)
    for copy in copies:
        copy.wait()
    values = spectra_ref[...].reshape(rows, chans).astype(jnp.float32)
    keep = (1 - bad_ref[...]).astype(jnp.float32)
    squares = values * values
    scale = jnp.zeros((rows, chans), jnp.float32)
    for h in range(hours):
        power = jnp.sum(jnp.where(hour == h, squares, 0.0), axis=0, keepdims=True) * (1.0 / (2 * bins))
        scale = jnp.where(hour == h, lax.rsqrt(power + EPSILON) * keep, scale)
    white = (values * scale).astype(jnp.bfloat16)
    out_ref[...] = lax.dot_general(
        white, move, (((0,), (0,)), ((), ())), preferred_element_type=jnp.float32
    ).astype(jnp.bfloat16)


def whiten(spectra, bad_channels):
    bins, hours, _, chans = spectra.shape
    spectra = pltpu.with_memory_space_constraint(spectra, pltpu.HBM)
    bad_channels = pltpu.with_memory_space_constraint(bad_channels.reshape(1, chans), pltpu.HBM)
    return pl.pallas_call(
        whiten_kernel,
        out_shape=jax.ShapeDtypeStruct((chans, bins * hours * 2), jnp.bfloat16),
        in_specs=[pl.BlockSpec(memory_space=pltpu.HBM)] * 2,
        out_specs=VMEM,
        scratch_shapes=[
            pltpu.VMEM(spectra.shape, spectra.dtype),
            pltpu.VMEM((1, chans), bad_channels.dtype),
            pltpu.SemaphoreType.DMA((2,)),
        ],
        compiler_params=pltpu.CompilerParams(vmem_limit_bytes=SMALL),
        name="whiten",
    )(spectra, bad_channels)


def turn_by(re, im, cos, sin, both):
    rc, rs, ic, is_ = re * cos, re * sin, im * cos, im * sin
    forward = (rc - is_, rs + ic)
    return (forward, (rc + is_, ic - rs)) if both else (forward,)


def correlate_kernel(norm, picked, adds, where_ref, own_ref, sib_ref, *refs):
    partials = refs[:adds]
    out_ref = refs[adds]
    spectra, left_turned, right_turned, *more = refs[adds + 1:]
    groups, _, lanes = spectra.shape
    half = lanes // 2
    hours_dev = half // F
    bin_number = lax.broadcasted_iota(jnp.int32, (8, half), 1) // hours_dev + 1
    step = lax.broadcasted_iota(jnp.int32, (8, half), 0)
    step = jnp.where(step == 6, 12, step)
    turn = (step * bin_number) % (2 * F)
    angle = jnp.where(turn >= F, turn - 2 * F, turn).astype(jnp.float32) * (math.pi / F)
    cos, sin = jnp.cos(angle), jnp.sin(angle)
    table = {k: (cos[i:i + 1], sin[i:i + 1]) for k, i in ((1, 1), (2, 2), (3, 3), (4, 4), (12, 6))}

    chan = where_ref[0, 0]
    rows = own_ref.shape[1]
    for core, piece in enumerate((own_ref, sib_ref)):
        for k in range(piece.shape[0] // groups):
            place = pl.multiple_of((chan ^ (CORES * k + core)) * rows, 32)
            spectra[:, pl.ds(place, rows), :] = piece[k * groups:(k + 1) * groups]

    def load(block, g):
        whole = spectra[g, pl.ds(pl.multiple_of(block * TILE, TILE), TILE), :].astype(jnp.float32)
        return whole[:, :half], whole[:, half:]

    def store(ref, slot, index, g, value):
        rows_at = pl.ds(index * TILE, TILE)
        ref[slot, rows_at, g * lanes:g * lanes + half] = value[0].astype(jnp.bfloat16)
        ref[slot, rows_at, g * lanes + half:(g + 1) * lanes] = value[1].astype(jnp.bfloat16)

    copies = []
    for i, t in enumerate(picked):
        slot = i % left_turned.shape[0]
        left_block, right_block = where_ref[0, 1 + 2 * t], where_ref[0, 2 + 2 * t]
        for g in range(groups):
            re, im = load(left_block, g)
            for k in (4, 12):
                forward, backward = turn_by(re, im, *(norm * part for part in table[k]), True)
                store(left_turned, slot, COARSE.index(k), g, forward)
                store(left_turned, slot, COARSE.index(-k), g, backward)
        for j in range(len(FINE_PAIRS)):
            for g in range(groups):
                re, im = load(right_block, g)
                if j == 0:
                    store(right_turned, slot, 0, g, turn_by(re, im, *table[4], False)[0])
                    store(right_turned, slot, 1, g, (re, im))
                else:
                    forward, backward = turn_by(re, im, *table[j], True)
                    store(right_turned, slot, 2 * j, g, forward)
                    store(right_turned, slot, 2 * j + 1, g, backward)
            total = lax.dot_general(
                left_turned[slot],
                right_turned[slot, 2 * j * TILE:2 * (j + 1) * TILE, :],
                (((1,), (1,)), ((), ())),
                preferred_element_type=jnp.float32,
            )
            for s in range(2):
                fine = FINE_PAIRS[j][s] + 4
                for u in range(len(COARSE)):
                    value = total[u * TILE:(u + 1) * TILE, s * TILE:(s + 1) * TILE]
                    if adds:
                        each = len(picked) // adds
                        more[0][i, u, fine] = partials[i // each][i % each, u, fine] + value
                    else:
                        out_ref[i, u, fine] = value
                if adds:
                    copy = pltpu.make_async_copy(more[0].at[i, :, fine], out_ref.at[i, :, fine], more[1])
                    copy.start()
                    copies.append(copy)
    for copy in copies:
        copy.wait()


def correlate(pieces, groups, where, picked, hours, partials=()):
    depth, rows, lanes = pieces[0].shape
    fine = 2 * len(FINE_PAIRS)
    shape = (len(picked), len(COARSE), fine, TILE, TILE)
    norm = 1.0 / math.sqrt(F * hours)
    slots = min(len(picked), 2)
    chans = len(pieces) * depth // groups * rows
    scratch = 2 * (groups * chans * lanes + slots * (len(COARSE) + fine) * TILE * groups * lanes)
    adds = len(partials)
    more = []
    if adds:
        more = [pltpu.VMEM(shape, jnp.float32), pltpu.SemaphoreType.DMA]
        scratch += 4 * math.prod(shape)
    return pl.pallas_call(
        lambda *refs: correlate_kernel(norm, picked, adds, *refs),
        out_shape=jax.ShapeDtypeStruct(shape, jnp.float32),
        in_specs=[VMEM] * (1 + len(pieces) + adds),
        out_specs=pl.BlockSpec(memory_space=pl.ANY) if adds else VMEM,
        scratch_shapes=[
            pltpu.VMEM((groups, chans, lanes), jnp.bfloat16),
            pltpu.VMEM((slots, len(COARSE) * TILE, groups * lanes), jnp.bfloat16),
            pltpu.VMEM((slots, fine * TILE, groups * lanes), jnp.bfloat16),
            *more,
        ],
        compiler_params=pltpu.CompilerParams(vmem_limit_bytes=scratch + SMALL),
        cost_estimate=pl.CostEstimate(flops=0, bytes_accessed=0, transcendentals=0),
        name="correlate_add" if adds else "correlate",
    )(where, *pieces, *partials)


def swap(array, axis, k):
    return lax.ppermute(array, axis, [(i, i ^ k) for i in range(lax.axis_size(axis))])


def stack_kernel(blocks, *refs):
    out_ref = refs[-1]
    first = 0
    for block in refs[:blocks]:
        out_ref[first:first + block.shape[0]] = block[...]
        first += block.shape[0]


def stack(blocks, after=(), flops=0):
    depth = sum(block.shape[0] for block in blocks)
    return pl.pallas_call(
        lambda *refs: stack_kernel(len(blocks), *refs),
        out_shape=jax.ShapeDtypeStruct((depth, *blocks[0].shape[1:]), blocks[0].dtype),
        in_specs=[VMEM] * len(blocks) + [pl.BlockSpec(memory_space=pl.ANY)] * len(after),
        out_specs=VMEM,
        compiler_params=pltpu.CompilerParams(vmem_limit_bytes=SMALL),
        cost_estimate=pl.CostEstimate(flops=flops, bytes_accessed=0, transcendentals=0),
        name="stack",
    )(*blocks, *after)


def halves(white, where):
    groups = lax.axis_size("tm")
    blocks = [white[None]] + [swap(white[None], "tm", k) for k in range(1, groups)]
    return stack(blocks[:groups // 2], after=(where,)), stack(blocks[groups // 2:], flops=10**9)


def between_chips(half):
    return [half] + [swap(half, "chan", k) for k in range(CORES, lax.axis_size("chan"), CORES)]


def per_device(spectra, bad_channels, tile_list):
    groups = lax.axis_size("tm")
    hours = spectra.shape[1] * groups
    tiles = tile_list.shape[0] // groups
    white = whiten(spectra, bad_channels)
    pairs = lax.dynamic_slice_in_dim(tile_list, lax.axis_index("tm") * tiles, tiles, axis=0)
    where = jnp.concatenate([lax.axis_index("chan").reshape(1), pairs.reshape(-1)]).astype(jnp.int32).reshape(1, -1)
    near, far = [between_chips(half) for half in halves(white, where)]
    near = stack(near)
    near = (near, swap(near, "chan", 1))
    far = stack(far)
    far = (far, swap(far, "chan", 1))
    partial = correlate(near, groups // 2, where, range(tiles), hours)
    out = correlate(far, groups // 2, where, range(tiles), hours, [partial])
    return out.reshape(tiles, LAGS, TILE, TILE)


def solution(mesh):
    placed = (P(None, "tm", None, "chan"), P("chan"), P("chan", None))
    return jax.shard_map(
        per_device,
        mesh=mesh,
        in_specs=placed,
        out_specs=P(("chan", "tm"), None, None, None),
        check_vma=False,
    )
```

```python
import math

import jax
import jax.numpy as jnp
from jax import lax
from jax.experimental import pallas as pl
from jax.experimental.pallas import tpu as pltpu
from jax.sharding import PartitionSpec as P

F = 64
LAGS = 32
TILE = 128
EPSILON = 1e-06
CORES = 2
SMALL = 4 * 1024 * 1024
VMEM = pl.BlockSpec(memory_space=pltpu.VMEM)
COARSE = (-12, -4, 4, 12)
FINE_PAIRS = ((-4, 0), (-1, 1), (-2, 2), (-3, 3))


def whiten_kernel(spectra_hbm, bad_hbm, out_ref, spectra_ref, bad_ref, sems):
    copies = [
        pltpu.make_async_copy(spectra_hbm, spectra_ref, sems.at[0]),
        pltpu.make_async_copy(bad_hbm, bad_ref, sems.at[1]),
    ]
    for copy in copies:
        copy.start()
    bins, hours, _, chans = spectra_ref.shape
    rows = bins * hours * 2
    row = lax.broadcasted_iota(jnp.int32, (rows, chans), 0)
    hour = (row // 2) % hours
    src = lax.broadcasted_iota(jnp.int32, (rows, rows), 0)
    dst = lax.broadcasted_iota(jnp.int32, (rows, rows), 1)
    move = jnp.where((src % 2) * (rows // 2) + src // 2 == dst, 1.0, 0.0).astype(jnp.bfloat16)
    for copy in copies:
        copy.wait()
    values = spectra_ref[...].reshape(rows, chans).astype(jnp.float32)
    keep = (1 - bad_ref[...]).astype(jnp.float32)
    squares = values * values
    scale = jnp.zeros((rows, chans), jnp.float32)
    for h in range(hours):
        power = jnp.sum(jnp.where(hour == h, squares, 0.0), axis=0, keepdims=True) * (1.0 / (2 * bins))
        scale = jnp.where(hour == h, lax.rsqrt(power + EPSILON) * keep, scale)
    white = (values * scale).astype(jnp.bfloat16)
    out_ref[...] = lax.dot_general(
        white, move, (((0,), (0,)), ((), ())), preferred_element_type=jnp.float32
    ).astype(jnp.bfloat16)


def whiten(spectra, bad_channels):
    bins, hours, _, chans = spectra.shape
    spectra = pltpu.with_memory_space_constraint(spectra, pltpu.HBM)
    bad_channels = pltpu.with_memory_space_constraint(bad_channels.reshape(1, chans), pltpu.HBM)
    return pl.pallas_call(
        whiten_kernel,
        out_shape=jax.ShapeDtypeStruct((chans, bins * hours * 2), jnp.bfloat16),
        in_specs=[pl.BlockSpec(memory_space=pltpu.HBM)] * 2,
        out_specs=VMEM,
        scratch_shapes=[
            pltpu.VMEM(spectra.shape, spectra.dtype),
            pltpu.VMEM((1, chans), bad_channels.dtype),
            pltpu.SemaphoreType.DMA((2,)),
        ],
        compiler_params=pltpu.CompilerParams(vmem_limit_bytes=SMALL),
        name="whiten",
    )(spectra, bad_channels)


def cos_sin(turn):
    quarter = F // 2
    shifted = turn + quarter // 2
    x = (shifted % quarter - quarter // 2).astype(jnp.float32) * (math.pi / F)
    y = x * x
    cos = 1 - y * (1 / 2 - y * (1 / 24 - y * (1 / 720 - y * (1 / 40320 - y / 3628800))))
    sin = x * (1 - y * (1 / 6 - y * (1 / 120 - y * (1 / 5040 - y / 362880))))
    quadrant = shifted // quarter % 4
    odd = quadrant % 2 == 1
    cos, sin = jnp.where(odd, sin, cos), jnp.where(odd, cos, sin)
    return jnp.where((quadrant == 1) | (quadrant == 2), -cos, cos), jnp.where(quadrant >= 2, -sin, sin)


def turn_by(re, im, cos, sin, both):
    rc, rs, ic, is_ = re * cos, re * sin, im * cos, im * sin
    forward = (rc - is_, rs + ic)
    return (forward, (rc + is_, ic - rs)) if both else (forward,)


def correlate_kernel(norm, picked, adds, where_ref, own_ref, sib_ref, *refs):
    partials = refs[:adds]
    out_ref = refs[adds]
    spectra, left_turned, right_turned, *more = refs[adds + 1:]
    groups, _, lanes = spectra.shape
    half = lanes // 2
    hours_dev = half // F
    bin_number = lax.broadcasted_iota(jnp.int32, (8, half), 1) // hours_dev + 1
    step = lax.broadcasted_iota(jnp.int32, (8, half), 0)
    cos, sin = cos_sin(jnp.where(step == 6, 12, step) * bin_number)
    table = {k: (cos[i:i + 1], sin[i:i + 1]) for k, i in ((1, 1), (2, 2), (3, 3), (4, 4), (12, 6))}

    chan = where_ref[0, 0]
    rows = own_ref.shape[1]
    for core, piece in enumerate((own_ref, sib_ref)):
        for k in range(piece.shape[0] // groups):
            place = pl.multiple_of((chan ^ (CORES * k + core)) * rows, 32)
            spectra[:, pl.ds(place, rows), :] = piece[k * groups:(k + 1) * groups]

    def load(block, g):
        whole = spectra[g, pl.ds(pl.multiple_of(block * TILE, TILE), TILE), :].astype(jnp.float32)
        return whole[:, :half], whole[:, half:]

    def store(ref, slot, index, g, value):
        rows_at = pl.ds(index * TILE, TILE)
        ref[slot, rows_at, g * lanes:g * lanes + half] = value[0].astype(jnp.bfloat16)
        ref[slot, rows_at, g * lanes + half:(g + 1) * lanes] = value[1].astype(jnp.bfloat16)

    copies = []
    for i, t in enumerate(picked):
        slot = i % left_turned.shape[0]
        left_block, right_block = where_ref[0, 1 + 2 * t], where_ref[0, 2 + 2 * t]
        for g in range(groups):
            re, im = load(left_block, g)
            for k in (4, 12):
                forward, backward = turn_by(re, im, *(norm * part for part in table[k]), True)
                store(left_turned, slot, COARSE.index(k), g, forward)
                store(left_turned, slot, COARSE.index(-k), g, backward)
        for j in range(len(FINE_PAIRS)):
            for g in range(groups):
                re, im = load(right_block, g)
                if j == 0:
                    store(right_turned, slot, 0, g, turn_by(re, im, *table[4], False)[0])
                    store(right_turned, slot, 1, g, (re, im))
                else:
                    forward, backward = turn_by(re, im, *table[j], True)
                    store(right_turned, slot, 2 * j, g, forward)
                    store(right_turned, slot, 2 * j + 1, g, backward)
            total = lax.dot_general(
                left_turned[slot],
                right_turned[slot, 2 * j * TILE:2 * (j + 1) * TILE, :],
                (((1,), (1,)), ((), ())),
                preferred_element_type=jnp.float32,
            )
            for s in range(2):
                fine = FINE_PAIRS[j][s] + 4
                for u in range(len(COARSE)):
                    value = total[u * TILE:(u + 1) * TILE, s * TILE:(s + 1) * TILE]
                    if adds:
                        each = len(picked) // adds
                        more[0][i, u, fine] = partials[i // each][i % each, u, fine] + value
                    else:
                        out_ref[i, u, fine] = value
                if adds:
                    copy = pltpu.make_async_copy(more[0].at[i, :, fine], out_ref.at[i, :, fine], more[1])
                    copy.start(priority=s)
                    copies.append(copy)
    for copy in copies:
        copy.wait()


def correlate(pieces, groups, where, picked, hours, partials=()):
    depth, rows, lanes = pieces[0].shape
    fine = 2 * len(FINE_PAIRS)
    shape = (len(picked), len(COARSE), fine, TILE, TILE)
    norm = 1.0 / math.sqrt(F * hours)
    slots = min(len(picked), 2)
    chans = len(pieces) * depth // groups * rows
    scratch = 2 * (groups * chans * lanes + slots * (len(COARSE) + fine) * TILE * groups * lanes)
    adds = len(partials)
    more = []
    if adds:
        more = [pltpu.VMEM(shape, jnp.float32), pltpu.SemaphoreType.DMA]
        scratch += 4 * math.prod(shape)
    return pl.pallas_call(
        lambda *refs: correlate_kernel(norm, picked, adds, *refs),
        out_shape=jax.ShapeDtypeStruct(shape, jnp.float32),
        in_specs=[VMEM] * (1 + len(pieces) + adds),
        out_specs=pl.BlockSpec(memory_space=pl.ANY) if adds else VMEM,
        scratch_shapes=[
            pltpu.VMEM((groups, chans, lanes), jnp.bfloat16),
            pltpu.VMEM((slots, len(COARSE) * TILE, groups * lanes), jnp.bfloat16),
            pltpu.VMEM((slots, fine * TILE, groups * lanes), jnp.bfloat16),
            *more,
        ],
        compiler_params=pltpu.CompilerParams(vmem_limit_bytes=scratch + SMALL),
        cost_estimate=pl.CostEstimate(flops=0, bytes_accessed=0, transcendentals=0),
        name="correlate_add" if adds else "correlate",
    )(where, *pieces, *partials)


def swap(array, axis, k):
    return lax.ppermute(array, axis, [(i, i ^ k) for i in range(lax.axis_size(axis))])


def stack_kernel(blocks, *refs):
    out_ref = refs[-1]
    first = 0
    for block in refs[:blocks]:
        out_ref[first:first + block.shape[0]] = block[...]
        first += block.shape[0]


def stack(blocks, after=(), flops=0):
    depth = sum(block.shape[0] for block in blocks)
    return pl.pallas_call(
        lambda *refs: stack_kernel(len(blocks), *refs),
        out_shape=jax.ShapeDtypeStruct((depth, *blocks[0].shape[1:]), blocks[0].dtype),
        in_specs=[VMEM] * len(blocks) + [pl.BlockSpec(memory_space=pl.ANY)] * len(after),
        out_specs=VMEM,
        compiler_params=pltpu.CompilerParams(vmem_limit_bytes=SMALL),
        cost_estimate=pl.CostEstimate(flops=flops, bytes_accessed=0, transcendentals=0),
        name="stack",
    )(*blocks, *after)


def halves(white, where):
    groups = lax.axis_size("tm")
    blocks = [white[None]] + [swap(white[None], "tm", k) for k in range(1, groups)]
    return stack(blocks[:groups // 2], after=(where,)), stack(blocks[groups // 2:], flops=10**9)


def between_chips(half):
    return [half] + [swap(half, "chan", k) for k in range(CORES, lax.axis_size("chan"), CORES)]


def per_device(spectra, bad_channels, tile_list):
    groups = lax.axis_size("tm")
    hours = spectra.shape[1] * groups
    tiles = tile_list.shape[0] // groups
    white = whiten(spectra, bad_channels)
    pairs = lax.dynamic_slice_in_dim(tile_list, lax.axis_index("tm") * tiles, tiles, axis=0)
    where = jnp.concatenate([lax.axis_index("chan").reshape(1), pairs.reshape(-1)]).astype(jnp.int32).reshape(1, -1)
    near, far = [between_chips(half) for half in halves(white, where)]
    near = stack(near)
    near = (near, swap(near, "chan", 1))
    far = stack(far)
    far = (far, swap(far, "chan", 1))
    partial = correlate(near, groups // 2, where, range(tiles), hours)
    out = correlate(far, groups // 2, where, range(tiles), hours, [partial])
    return out.reshape(tiles, LAGS, TILE, TILE)


def solution(mesh):
    placed = (P(None, "tm", None, "chan"), P("chan"), P("chan", None))
    return jax.shard_map(
        per_device,
        mesh=mesh,
        in_specs=placed,
        out_specs=P(("chan", "tm"), None, None, None),
        check_vma=False,
    )
```

```python
import math

import jax
import jax.numpy as jnp
from jax import lax
from jax.experimental import pallas as pl
from jax.experimental.pallas import tpu as pltpu
from jax.sharding import PartitionSpec as P

F = 64
LAGS = 32
TILE = 128
EPSILON = 1e-06
CORES = 2
SMALL = 4 * 1024 * 1024
VMEM = pl.BlockSpec(memory_space=pltpu.VMEM)
COARSE = (-12, -4, 4, 12)
FINE_PAIRS = ((-4, 0), (-1, 1), (-2, 2), (-3, 3))


def whiten_kernel(spectra_hbm, bad_hbm, out_ref, spectra_ref, bad_ref, sems):
    copies = [
        pltpu.make_async_copy(spectra_hbm, spectra_ref, sems.at[0]),
        pltpu.make_async_copy(bad_hbm, bad_ref, sems.at[1]),
    ]
    for copy in copies:
        copy.start()
    bins, hours, _, chans = spectra_ref.shape
    rows = bins * hours * 2
    row = lax.broadcasted_iota(jnp.int32, (rows, chans), 0)
    hour = (row // 2) % hours
    src = lax.broadcasted_iota(jnp.int32, (rows, rows), 0)
    dst = lax.broadcasted_iota(jnp.int32, (rows, rows), 1)
    move = jnp.where((src % 2) * (rows // 2) + src // 2 == dst, 1.0, 0.0).astype(jnp.bfloat16)
    for copy in copies:
        copy.wait()
    values = spectra_ref[...].reshape(rows, chans).astype(jnp.float32)
    keep = (1 - bad_ref[...]).astype(jnp.float32)
    squares = values * values
    scale = jnp.zeros((rows, chans), jnp.float32)
    for h in range(hours):
        power = jnp.sum(jnp.where(hour == h, squares, 0.0), axis=0, keepdims=True) * (1.0 / (2 * bins))
        scale = jnp.where(hour == h, lax.rsqrt(power + EPSILON) * keep, scale)
    white = (values * scale).astype(jnp.bfloat16)
    out_ref[...] = lax.dot_general(
        white, move, (((0,), (0,)), ((), ())), preferred_element_type=jnp.float32
    ).astype(jnp.bfloat16)


def whiten(spectra, bad_channels):
    bins, hours, _, chans = spectra.shape
    spectra = pltpu.with_memory_space_constraint(spectra, pltpu.HBM)
    bad_channels = pltpu.with_memory_space_constraint(bad_channels.reshape(1, chans), pltpu.HBM)
    return pl.pallas_call(
        whiten_kernel,
        out_shape=jax.ShapeDtypeStruct((chans, bins * hours * 2), jnp.bfloat16),
        in_specs=[pl.BlockSpec(memory_space=pltpu.HBM)] * 2,
        out_specs=VMEM,
        scratch_shapes=[
            pltpu.VMEM(spectra.shape, spectra.dtype),
            pltpu.VMEM((1, chans), bad_channels.dtype),
            pltpu.SemaphoreType.DMA((2,)),
        ],
        compiler_params=pltpu.CompilerParams(vmem_limit_bytes=SMALL),
        name="whiten",
    )(spectra, bad_channels)


def cos_sin(turn):
    quarter = F // 2
    shifted = turn + quarter // 2
    x = (shifted % quarter - quarter // 2).astype(jnp.float32) * (math.pi / F)
    y = x * x
    cos = 1 - y * (1 / 2 - y * (1 / 24 - y * (1 / 720 - y * (1 / 40320 - y / 3628800))))
    sin = x * (1 - y * (1 / 6 - y * (1 / 120 - y * (1 / 5040 - y / 362880))))
    quadrant = shifted // quarter % 4
    odd = quadrant % 2 == 1
    cos, sin = jnp.where(odd, sin, cos), jnp.where(odd, cos, sin)
    return jnp.where((quadrant == 1) | (quadrant == 2), -cos, cos), jnp.where(quadrant >= 2, -sin, sin)


def turn_by(re, im, cos, sin, both):
    rc, rs, ic, is_ = re * cos, re * sin, im * cos, im * sin
    forward = (rc - is_, rs + ic)
    return (forward, (rc + is_, ic - rs)) if both else (forward,)


def correlate_kernel(norm, picked, adds, crossings, where_ref, own_ref, sib_ref, *refs):
    partials = refs[:adds]
    out_ref = refs[adds]
    spectra, left_turned, right_turned, *more = refs[adds + 1:]
    groups, _, lanes = spectra.shape
    half = lanes // 2
    hours_dev = half // F
    bin_number = lax.broadcasted_iota(jnp.int32, (8, half), 1) // hours_dev + 1
    step = lax.broadcasted_iota(jnp.int32, (8, half), 0)
    cos, sin = cos_sin(jnp.where(step == 6, 12, step) * bin_number)
    table = {k: (cos[i:i + 1], sin[i:i + 1]) for k, i in ((1, 1), (2, 2), (3, 3), (4, 4), (12, 6))}

    chan = where_ref[0, 0]
    rows = own_ref.shape[1]
    for core, piece in enumerate((own_ref, sib_ref)):
        for slot in range(piece.shape[0]):
            k, g = slot // groups, slot % groups
            crossed = core ^ (k > 0) ^ crossings[g]
            place = pl.multiple_of((chan ^ (CORES * k + crossed)) * rows, 32)
            spectra[g, pl.ds(place, rows), :] = piece[slot]

    def load(block, g):
        whole = spectra[g, pl.ds(pl.multiple_of(block * TILE, TILE), TILE), :].astype(jnp.float32)
        return whole[:, :half], whole[:, half:]

    def store(ref, slot, index, g, value):
        rows_at = pl.ds(index * TILE, TILE)
        ref[slot, rows_at, g * lanes:g * lanes + half] = value[0].astype(jnp.bfloat16)
        ref[slot, rows_at, g * lanes + half:(g + 1) * lanes] = value[1].astype(jnp.bfloat16)

    copies = []
    for i, t in enumerate(picked):
        slot = i % left_turned.shape[0]
        left_block, right_block = where_ref[0, 1 + 2 * t], where_ref[0, 2 + 2 * t]
        for g in range(groups):
            re, im = load(left_block, g)
            for k in (4, 12):
                forward, backward = turn_by(re, im, *(norm * part for part in table[k]), True)
                store(left_turned, slot, COARSE.index(k), g, forward)
                store(left_turned, slot, COARSE.index(-k), g, backward)
        for j in range(len(FINE_PAIRS)):
            for g in range(groups):
                re, im = load(right_block, g)
                if j == 0:
                    store(right_turned, slot, 0, g, turn_by(re, im, *table[4], False)[0])
                    store(right_turned, slot, 1, g, (re, im))
                else:
                    forward, backward = turn_by(re, im, *table[j], True)
                    store(right_turned, slot, 2 * j, g, forward)
                    store(right_turned, slot, 2 * j + 1, g, backward)
            total = lax.dot_general(
                left_turned[slot],
                right_turned[slot, 2 * j * TILE:2 * (j + 1) * TILE, :],
                (((1,), (1,)), ((), ())),
                preferred_element_type=jnp.float32,
            )
            for s in range(2):
                fine = FINE_PAIRS[j][s] + 4
                for u in range(len(COARSE)):
                    value = total[u * TILE:(u + 1) * TILE, s * TILE:(s + 1) * TILE]
                    if adds:
                        each = len(picked) // adds
                        more[0][i, u, fine] = partials[i // each][i % each, u, fine] + value
                    else:
                        out_ref[i, u, fine] = value
                if adds:
                    copy = pltpu.make_async_copy(more[0].at[i, :, fine], out_ref.at[i, :, fine], more[1])
                    copy.start(priority=s)
                    copies.append(copy)
    for copy in copies:
        copy.wait()


def correlate(pieces, crossings, where, picked, hours, partials=()):
    depth, rows, lanes = pieces[0].shape
    groups = len(crossings)
    fine = 2 * len(FINE_PAIRS)
    shape = (len(picked), len(COARSE), fine, TILE, TILE)
    norm = 1.0 / math.sqrt(F * hours)
    slots = min(len(picked), 2)
    chans = len(pieces) * depth // groups * rows
    scratch = 2 * (groups * chans * lanes + slots * (len(COARSE) + fine) * TILE * groups * lanes)
    adds = len(partials)
    more = []
    if adds:
        more = [pltpu.VMEM(shape, jnp.float32), pltpu.SemaphoreType.DMA]
        scratch += 4 * math.prod(shape)
    return pl.pallas_call(
        lambda *refs: correlate_kernel(norm, picked, adds, crossings, *refs),
        out_shape=jax.ShapeDtypeStruct(shape, jnp.float32),
        in_specs=[VMEM] * (1 + len(pieces) + adds),
        out_specs=pl.BlockSpec(memory_space=pl.ANY) if adds else VMEM,
        scratch_shapes=[
            pltpu.VMEM((groups, chans, lanes), jnp.bfloat16),
            pltpu.VMEM((slots, len(COARSE) * TILE, groups * lanes), jnp.bfloat16),
            pltpu.VMEM((slots, fine * TILE, groups * lanes), jnp.bfloat16),
            *more,
        ],
        compiler_params=pltpu.CompilerParams(vmem_limit_bytes=scratch + SMALL),
        cost_estimate=pl.CostEstimate(flops=0, bytes_accessed=0, transcendentals=0),
        name="correlate_add" if adds else "correlate",
    )(where, *pieces, *partials)


def swap(array, chan_k, tm_k):
    chans, groups = lax.axis_size("chan"), lax.axis_size("tm")
    pairs = [
        (chan * groups + tm, (chan ^ chan_k) * groups + (tm ^ tm_k)) for chan in range(chans) for tm in range(groups)
    ]
    return lax.ppermute(array, ("chan", "tm"), pairs)


def stack_kernel(blocks, *refs):
    out_ref = refs[-1]
    first = 0
    for block in refs[:blocks]:
        out_ref[first:first + block.shape[0]] = block[...]
        first += block.shape[0]


def stack(blocks, after=(), flops=0):
    depth = sum(block.shape[0] for block in blocks)
    return pl.pallas_call(
        lambda *refs: stack_kernel(len(blocks), *refs),
        out_shape=jax.ShapeDtypeStruct((depth, *blocks[0].shape[1:]), blocks[0].dtype),
        in_specs=[VMEM] * len(blocks) + [pl.BlockSpec(memory_space=pl.ANY)] * len(after),
        out_specs=VMEM,
        compiler_params=pltpu.CompilerParams(vmem_limit_bytes=SMALL),
        cost_estimate=pl.CostEstimate(flops=flops, bytes_accessed=0, transcendentals=0),
        name="stack",
    )(*blocks, *after)


def halves(white, where):
    groups = lax.axis_size("tm")
    blocks = [white[None]] + [swap(white[None], 1, k) for k in range(1, groups)]
    return stack(blocks[:groups // 2], after=(where,)), stack(blocks[groups // 2:], flops=10**9)


def between_chips(half):
    return [half] + [swap(half, k + 1, 0) for k in range(CORES, lax.axis_size("chan"), CORES)]


def per_device(spectra, bad_channels, tile_list):
    groups = lax.axis_size("tm")
    hours = spectra.shape[1] * groups
    tiles = tile_list.shape[0] // groups
    white = whiten(spectra, bad_channels)
    pairs = lax.dynamic_slice_in_dim(tile_list, lax.axis_index("tm") * tiles, tiles, axis=0)
    where = jnp.concatenate([lax.axis_index("chan").reshape(1), pairs.reshape(-1)]).astype(jnp.int32).reshape(1, -1)
    crossings = [0] + [1] * (groups - 1)
    near, far = [between_chips(half) for half in halves(white, where)]
    near = stack(near)
    near = (near, swap(near, 1, 0))
    far = stack(far)
    far = (far, swap(far, 1, 0))
    partial = correlate(near, crossings[:groups // 2], where, range(tiles), hours)
    out = correlate(far, crossings[groups // 2:], where, range(tiles), hours, [partial])
    return out.reshape(tiles, LAGS, TILE, TILE)


def solution(mesh):
    placed = (P(None, "tm", None, "chan"), P("chan"), P("chan", None))
    return jax.shard_map(
        per_device,
        mesh=mesh,
        in_specs=placed,
        out_specs=P(("chan", "tm"), None, None, None),
        check_vma=False,
    )
```

```python
import math

import jax
import jax.numpy as jnp
from jax import lax
from jax.experimental import pallas as pl
from jax.experimental.pallas import tpu as pltpu
from jax.sharding import PartitionSpec as P

F = 64
LAGS = 32
TILE = 128
EPSILON = 1e-06
CORES = 2
SMALL = 4 * 1024 * 1024
VMEM = pl.BlockSpec(memory_space=pltpu.VMEM)
COARSE = (-12, -4, 4, 12)
FINE_PAIRS = ((-4, 0), (-1, 1), (-2, 2), (-3, 3))


def whiten_kernel(spectra_hbm, bad_hbm, out_ref, spectra_ref, bad_ref, sems):
    copies = [
        pltpu.make_async_copy(spectra_hbm, spectra_ref, sems.at[0]),
        pltpu.make_async_copy(bad_hbm, bad_ref, sems.at[1]),
    ]
    for copy in copies:
        copy.start()
    bins, hours, _, chans = spectra_ref.shape
    rows = bins * hours * 2
    row = lax.broadcasted_iota(jnp.int32, (rows, chans), 0)
    hour = (row // 2) % hours
    src = lax.broadcasted_iota(jnp.int32, (rows, rows), 0)
    dst = lax.broadcasted_iota(jnp.int32, (rows, rows), 1)
    move = jnp.where((src % 2) * (rows // 2) + src // 2 == dst, 1.0, 0.0).astype(jnp.bfloat16)
    for copy in copies:
        copy.wait()
    values = spectra_ref[...].reshape(rows, chans).astype(jnp.float32)
    keep = (1 - bad_ref[...]).astype(jnp.float32)
    squares = values * values
    scale = jnp.zeros((rows, chans), jnp.float32)
    for h in range(hours):
        power = jnp.sum(jnp.where(hour == h, squares, 0.0), axis=0, keepdims=True) * (1.0 / (2 * bins))
        scale = jnp.where(hour == h, lax.rsqrt(power + EPSILON) * keep, scale)
    white = (values * scale).astype(jnp.bfloat16)
    out_ref[...] = lax.dot_general(
        white, move, (((0,), (0,)), ((), ())), preferred_element_type=jnp.float32
    ).astype(jnp.bfloat16)


def whiten(spectra, bad_channels):
    bins, hours, _, chans = spectra.shape
    spectra = pltpu.with_memory_space_constraint(spectra, pltpu.HBM)
    bad_channels = pltpu.with_memory_space_constraint(bad_channels.reshape(1, chans), pltpu.HBM)
    return pl.pallas_call(
        whiten_kernel,
        out_shape=jax.ShapeDtypeStruct((chans, bins * hours * 2), jnp.bfloat16),
        in_specs=[pl.BlockSpec(memory_space=pltpu.HBM)] * 2,
        out_specs=VMEM,
        scratch_shapes=[
            pltpu.VMEM(spectra.shape, spectra.dtype),
            pltpu.VMEM((1, chans), bad_channels.dtype),
            pltpu.SemaphoreType.DMA((2,)),
        ],
        compiler_params=pltpu.CompilerParams(vmem_limit_bytes=SMALL),
        name="whiten",
    )(spectra, bad_channels)


def cos_sin(turn):
    quarter = F // 2
    shifted = turn + quarter // 2
    x = (shifted % quarter - quarter // 2).astype(jnp.float32) * (math.pi / F)
    y = x * x
    cos = 1 - y * (1 / 2 - y * (1 / 24 - y * (1 / 720 - y * (1 / 40320 - y / 3628800))))
    sin = x * (1 - y * (1 / 6 - y * (1 / 120 - y * (1 / 5040 - y / 362880))))
    quadrant = shifted // quarter % 4
    odd = quadrant % 2 == 1
    cos, sin = jnp.where(odd, sin, cos), jnp.where(odd, cos, sin)
    return jnp.where((quadrant == 1) | (quadrant == 2), -cos, cos), jnp.where(quadrant >= 2, -sin, sin)


def turn_by(re, im, cos, sin, both):
    rc, rs, ic, is_ = re * cos, re * sin, im * cos, im * sin
    forward = (rc - is_, rs + ic)
    return (forward, (rc + is_, ic - rs)) if both else (forward,)


def correlate_kernel(norm, picked, adds, where_ref, own_ref, sib_ref, *refs):
    partials = refs[:adds]
    out_ref = refs[adds]
    spectra, left_turned, right_turned, *more = refs[adds + 1:]
    groups, _, lanes = spectra.shape
    half = lanes // 2
    hours_dev = half // F
    bin_number = lax.broadcasted_iota(jnp.int32, (8, half), 1) // hours_dev + 1
    step = lax.broadcasted_iota(jnp.int32, (8, half), 0)
    cos, sin = cos_sin(jnp.where(step == 6, 12, step) * bin_number)
    table = {k: (cos[i:i + 1], sin[i:i + 1]) for k, i in ((1, 1), (2, 2), (3, 3), (4, 4), (12, 6))}

    chan = where_ref[0, 0]
    rows = own_ref.shape[1]
    for core, piece in enumerate((own_ref, sib_ref)):
        for k in range(piece.shape[0] // groups):
            place = pl.multiple_of((chan ^ (CORES * k + core)) * rows, 32)
            spectra[:, pl.ds(place, rows), :] = piece[k * groups:(k + 1) * groups]

    def load(block, g):
        whole = spectra[g, pl.ds(pl.multiple_of(block * TILE, TILE), TILE), :].astype(jnp.float32)
        return whole[:, :half], whole[:, half:]

    def store(ref, slot, index, g, value):
        rows_at = pl.ds(index * TILE, TILE)
        ref[slot, rows_at, g * lanes:g * lanes + half] = value[0].astype(jnp.bfloat16)
        ref[slot, rows_at, g * lanes + half:(g + 1) * lanes] = value[1].astype(jnp.bfloat16)

    copies = []
    for i, t in enumerate(picked):
        slot = i % left_turned.shape[0]
        left_block, right_block = where_ref[0, 1 + 2 * t], where_ref[0, 2 + 2 * t]
        for g in range(groups):
            re, im = load(left_block, g)
            for k in (4, 12):
                forward, backward = turn_by(re, im, *(norm * part for part in table[k]), True)
                store(left_turned, slot, COARSE.index(k), g, forward)
                store(left_turned, slot, COARSE.index(-k), g, backward)
        for j in range(len(FINE_PAIRS)):
            for g in range(groups):
                re, im = load(right_block, g)
                if j == 0:
                    store(right_turned, slot, 0, g, turn_by(re, im, *table[4], False)[0])
                    store(right_turned, slot, 1, g, (re, im))
                else:
                    forward, backward = turn_by(re, im, *table[j], True)
                    store(right_turned, slot, 2 * j, g, forward)
                    store(right_turned, slot, 2 * j + 1, g, backward)
            for u in range(0, len(COARSE), 2):
                total = lax.dot_general(
                    left_turned[slot, u * TILE:(u + 2) * TILE, :],
                    right_turned[slot, 2 * j * TILE:2 * (j + 1) * TILE, :],
                    (((1,), (1,)), ((), ())),
                    preferred_element_type=jnp.float32,
                )
                for v, s in ((0, 0), (0, 1), (1, 0), (1, 1)):
                    fine = FINE_PAIRS[j][s] + 4
                    value = total[v * TILE:(v + 1) * TILE, s * TILE:(s + 1) * TILE]
                    if adds:
                        each = len(picked) // adds
                        more[0][i, u + v, fine] = partials[i // each][i % each, u + v, fine] + value
                    else:
                        out_ref[i, u + v, fine] = value
            for s in range(2 if adds else 0):
                fine = FINE_PAIRS[j][s] + 4
                copy = pltpu.make_async_copy(more[0].at[i, :, fine], out_ref.at[i, :, fine], more[1])
                copy.start(priority=s)
                copies.append(copy)
    for copy in copies:
        copy.wait()


def correlate(pieces, groups, where, picked, hours, partials=()):
    depth, rows, lanes = pieces[0].shape
    fine = 2 * len(FINE_PAIRS)
    shape = (len(picked), len(COARSE), fine, TILE, TILE)
    norm = 1.0 / math.sqrt(F * hours)
    slots = min(len(picked), 2)
    chans = len(pieces) * depth // groups * rows
    scratch = 2 * (groups * chans * lanes + slots * (len(COARSE) + fine) * TILE * groups * lanes)
    adds = len(partials)
    more = []
    if adds:
        more = [pltpu.VMEM(shape, jnp.float32), pltpu.SemaphoreType.DMA]
        scratch += 4 * math.prod(shape)
    return pl.pallas_call(
        lambda *refs: correlate_kernel(norm, picked, adds, *refs),
        out_shape=jax.ShapeDtypeStruct(shape, jnp.float32),
        in_specs=[VMEM] * (1 + len(pieces) + adds),
        out_specs=pl.BlockSpec(memory_space=pl.ANY) if adds else VMEM,
        scratch_shapes=[
            pltpu.VMEM((groups, chans, lanes), jnp.bfloat16),
            pltpu.VMEM((slots, len(COARSE) * TILE, groups * lanes), jnp.bfloat16),
            pltpu.VMEM((slots, fine * TILE, groups * lanes), jnp.bfloat16),
            *more,
        ],
        compiler_params=pltpu.CompilerParams(vmem_limit_bytes=scratch + SMALL),
        cost_estimate=pl.CostEstimate(flops=0, bytes_accessed=0, transcendentals=0),
        name="correlate_add" if adds else "correlate",
    )(where, *pieces, *partials)


def swap(array, axis, k):
    return lax.ppermute(array, axis, [(i, i ^ k) for i in range(lax.axis_size(axis))])


def stack_kernel(blocks, *refs):
    out_ref = refs[-1]
    first = 0
    for block in refs[:blocks]:
        out_ref[first:first + block.shape[0]] = block[...]
        first += block.shape[0]


def stack(blocks, after=(), flops=0):
    depth = sum(block.shape[0] for block in blocks)
    return pl.pallas_call(
        lambda *refs: stack_kernel(len(blocks), *refs),
        out_shape=jax.ShapeDtypeStruct((depth, *blocks[0].shape[1:]), blocks[0].dtype),
        in_specs=[VMEM] * len(blocks) + [pl.BlockSpec(memory_space=pl.ANY)] * len(after),
        out_specs=VMEM,
        compiler_params=pltpu.CompilerParams(vmem_limit_bytes=SMALL),
        cost_estimate=pl.CostEstimate(flops=flops, bytes_accessed=0, transcendentals=0),
        name="stack",
    )(*blocks, *after)


def halves(white, where):
    groups = lax.axis_size("tm")
    blocks = [white[None]] + [swap(white[None], "tm", k) for k in range(1, groups)]
    return stack(blocks[:groups // 2], after=(where,)), stack(blocks[groups // 2:], flops=10**9)


def between_chips(half):
    return [half] + [swap(half, "chan", k) for k in range(CORES, lax.axis_size("chan"), CORES)]


def per_device(spectra, bad_channels, tile_list):
    groups = lax.axis_size("tm")
    hours = spectra.shape[1] * groups
    tiles = tile_list.shape[0] // groups
    white = whiten(spectra, bad_channels)
    pairs = lax.dynamic_slice_in_dim(tile_list, lax.axis_index("tm") * tiles, tiles, axis=0)
    where = jnp.concatenate([lax.axis_index("chan").reshape(1), pairs.reshape(-1)]).astype(jnp.int32).reshape(1, -1)
    near, far = [between_chips(half) for half in halves(white, where)]
    near = stack(near)
    near = (near, swap(near, "chan", 1))
    far = stack(far)
    far = (far, swap(far, "chan", 1))
    partial = correlate(near, groups // 2, where, range(tiles), hours)
    out = correlate(far, groups // 2, where, range(tiles), hours, [partial])
    return out.reshape(tiles, LAGS, TILE, TILE)


def solution(mesh):
    placed = (P(None, "tm", None, "chan"), P("chan"), P("chan", None))
    return jax.shard_map(
        per_device,
        mesh=mesh,
        in_specs=placed,
        out_specs=P(("chan", "tm"), None, None, None),
        check_vma=False,
    )
```

```python
import math

import jax
import jax.numpy as jnp
from jax import lax
from jax.experimental import pallas as pl
from jax.experimental.pallas import tpu as pltpu
from jax.sharding import PartitionSpec as P

F = 64
LAGS = 32
TILE = 128
EPSILON = 1e-06
CORES = 2
SMALL = 4 * 1024 * 1024
VMEM = pl.BlockSpec(memory_space=pltpu.VMEM)
COARSE = (-12, -4, 4, 12)
FINE_PAIRS = ((-4, 0), (-1, 1), (-2, 2), (-3, 3))


def whiten_kernel(spectra_hbm, bad_hbm, out_ref, spectra_ref, bad_ref, sems):
    copies = [
        pltpu.make_async_copy(spectra_hbm, spectra_ref, sems.at[0]),
        pltpu.make_async_copy(bad_hbm, bad_ref, sems.at[1]),
    ]
    for copy in copies:
        copy.start()
    bins, hours, _, chans = spectra_ref.shape
    rows = bins * hours * 2
    row = lax.broadcasted_iota(jnp.int32, (rows, chans), 0)
    hour = (row // 2) % hours
    src = lax.broadcasted_iota(jnp.int32, (rows, rows), 0)
    dst = lax.broadcasted_iota(jnp.int32, (rows, rows), 1)
    move = jnp.where((src % 2) * (rows // 2) + src // 2 == dst, 1.0, 0.0).astype(jnp.bfloat16)
    for copy in copies:
        copy.wait()
    values = spectra_ref[...].reshape(rows, chans).astype(jnp.float32)
    keep = (1 - bad_ref[...]).astype(jnp.float32)
    squares = values * values
    scale = jnp.zeros((rows, chans), jnp.float32)
    for h in range(hours):
        power = jnp.sum(jnp.where(hour == h, squares, 0.0), axis=0, keepdims=True) * (1.0 / (2 * bins))
        scale = jnp.where(hour == h, lax.rsqrt(power + EPSILON) * keep, scale)
    white = (values * scale).astype(jnp.bfloat16)
    out_ref[...] = lax.dot_general(
        white, move, (((0,), (0,)), ((), ())), preferred_element_type=jnp.float32
    ).astype(jnp.bfloat16)


def whiten(spectra, bad_channels):
    bins, hours, _, chans = spectra.shape
    spectra = pltpu.with_memory_space_constraint(spectra, pltpu.HBM)
    bad_channels = pltpu.with_memory_space_constraint(bad_channels.reshape(1, chans), pltpu.HBM)
    return pl.pallas_call(
        whiten_kernel,
        out_shape=jax.ShapeDtypeStruct((chans, bins * hours * 2), jnp.bfloat16),
        in_specs=[pl.BlockSpec(memory_space=pltpu.HBM)] * 2,
        out_specs=VMEM,
        scratch_shapes=[
            pltpu.VMEM(spectra.shape, spectra.dtype),
            pltpu.VMEM((1, chans), bad_channels.dtype),
            pltpu.SemaphoreType.DMA((2,)),
        ],
        compiler_params=pltpu.CompilerParams(vmem_limit_bytes=SMALL),
        name="whiten",
    )(spectra, bad_channels)


def cos_sin(turn):
    quarter = F // 2
    shifted = turn + quarter // 2
    x = (shifted % quarter - quarter // 2).astype(jnp.float32) * (math.pi / F)
    y = x * x
    cos = 1 - y * (1 / 2 - y * (1 / 24 - y * (1 / 720 - y * (1 / 40320 - y / 3628800))))
    sin = x * (1 - y * (1 / 6 - y * (1 / 120 - y * (1 / 5040 - y / 362880))))
    quadrant = shifted // quarter % 4
    odd = quadrant % 2 == 1
    cos, sin = jnp.where(odd, sin, cos), jnp.where(odd, cos, sin)
    return jnp.where((quadrant == 1) | (quadrant == 2), -cos, cos), jnp.where(quadrant >= 2, -sin, sin)


def turn_by(re, im, cos, sin, both):
    rc, rs, ic, is_ = re * cos, re * sin, im * cos, im * sin
    forward = (rc - is_, rs + ic)
    return (forward, (rc + is_, ic - rs)) if both else (forward,)


def correlate_kernel(norm, picked, adds, places, where_ref, *refs):
    parts, refs = refs[:2 * len(places)], refs[2 * len(places):]
    partials = refs[:adds]
    out_ref = refs[adds]
    spectra, left_turned, right_turned, *more = refs[adds + 1:]
    groups, _, lanes = spectra.shape
    half = lanes // 2
    hours_dev = half // F
    bin_number = lax.broadcasted_iota(jnp.int32, (8, half), 1) // hours_dev + 1
    step = lax.broadcasted_iota(jnp.int32, (8, half), 0)
    cos, sin = cos_sin(jnp.where(step == 6, 12, step) * bin_number)
    table = {k: (cos[i:i + 1], sin[i:i + 1]) for k, i in ((1, 1), (2, 2), (3, 3), (4, 4), (12, 6))}

    chan = where_ref[0, 0]
    for i, piece in enumerate(parts):
        rows = piece.shape[1]
        for slot, k in enumerate(places[i // 2]):
            place = pl.multiple_of((chan ^ (CORES * k + i % 2)) * rows, 32)
            spectra[:, pl.ds(place, rows), :] = piece[slot * groups:(slot + 1) * groups]

    def load(block, g):
        whole = spectra[g, pl.ds(pl.multiple_of(block * TILE, TILE), TILE), :].astype(jnp.float32)
        return whole[:, :half], whole[:, half:]

    def store(ref, slot, index, g, value):
        rows_at = pl.ds(index * TILE, TILE)
        ref[slot, rows_at, g * lanes:g * lanes + half] = value[0].astype(jnp.bfloat16)
        ref[slot, rows_at, g * lanes + half:(g + 1) * lanes] = value[1].astype(jnp.bfloat16)

    copies = []
    for i, t in enumerate(picked):
        slot = i % left_turned.shape[0]
        left_block, right_block = where_ref[0, 1 + 2 * t], where_ref[0, 2 + 2 * t]
        for g in range(groups):
            re, im = load(left_block, g)
            for k in (4, 12):
                forward, backward = turn_by(re, im, *(norm * part for part in table[k]), True)
                store(left_turned, slot, COARSE.index(k), g, forward)
                store(left_turned, slot, COARSE.index(-k), g, backward)
        for j in range(len(FINE_PAIRS)):
            for g in range(groups):
                re, im = load(right_block, g)
                if j == 0:
                    store(right_turned, slot, 0, g, turn_by(re, im, *table[4], False)[0])
                    store(right_turned, slot, 1, g, (re, im))
                else:
                    forward, backward = turn_by(re, im, *table[j], True)
                    store(right_turned, slot, 2 * j, g, forward)
                    store(right_turned, slot, 2 * j + 1, g, backward)
            for u in range(0, len(COARSE), 2):
                total = lax.dot_general(
                    left_turned[slot, u * TILE:(u + 2) * TILE, :],
                    right_turned[slot, 2 * j * TILE:2 * (j + 1) * TILE, :],
                    (((1,), (1,)), ((), ())),
                    preferred_element_type=jnp.float32,
                )
                for v, s in ((0, 0), (0, 1), (1, 0), (1, 1)):
                    fine = FINE_PAIRS[j][s] + 4
                    value = total[v * TILE:(v + 1) * TILE, s * TILE:(s + 1) * TILE]
                    if adds:
                        each = len(picked) // adds
                        more[0][i, u + v, fine] = partials[i // each][i % each, u + v, fine] + value
                    else:
                        out_ref[i, u + v, fine] = value
                for s in range(2 if adds else 0):
                    done = (i, pl.ds(u, 2), FINE_PAIRS[j][s] + 4)
                    copy = pltpu.make_async_copy(more[0].at[done], out_ref.at[done], more[1])
                    copy.start(priority=s)
                    copies.append(copy)
    for copy in copies:
        copy.wait()


def correlate(parts, groups, where, picked, hours, partials=()):
    places = [part[0] for part in parts]
    pieces = [piece for part in parts for piece in part[1:]]
    _, rows, lanes = pieces[0].shape
    fine = 2 * len(FINE_PAIRS)
    shape = (len(picked), len(COARSE), fine, TILE, TILE)
    norm = 1.0 / math.sqrt(F * hours)
    slots = min(len(picked), 2)
    chans = CORES * sum(map(len, places)) * rows
    scratch = 2 * (groups * chans * lanes + slots * (len(COARSE) + fine) * TILE * groups * lanes)
    adds = len(partials)
    more = []
    if adds:
        more = [pltpu.VMEM(shape, jnp.float32), pltpu.SemaphoreType.DMA]
        scratch += 4 * math.prod(shape)
    return pl.pallas_call(
        lambda *refs: correlate_kernel(norm, picked, adds, places, *refs),
        out_shape=jax.ShapeDtypeStruct(shape, jnp.float32),
        in_specs=[VMEM] * (1 + len(pieces) + adds),
        out_specs=pl.BlockSpec(memory_space=pl.ANY) if adds else VMEM,
        scratch_shapes=[
            pltpu.VMEM((groups, chans, lanes), jnp.bfloat16),
            pltpu.VMEM((slots, len(COARSE) * TILE, groups * lanes), jnp.bfloat16),
            pltpu.VMEM((slots, fine * TILE, groups * lanes), jnp.bfloat16),
            *more,
        ],
        compiler_params=pltpu.CompilerParams(vmem_limit_bytes=scratch + SMALL),
        cost_estimate=pl.CostEstimate(flops=0, bytes_accessed=0, transcendentals=0),
        name="correlate_add" if adds else "correlate",
    )(where, *pieces, *partials)


def swap(array, axis, k):
    return lax.ppermute(array, axis, [(i, i ^ k) for i in range(lax.axis_size(axis))])


def stack_kernel(blocks, *refs):
    out_ref = refs[-1]
    first = 0
    for block in refs[:blocks]:
        out_ref[first:first + block.shape[0]] = block[...]
        first += block.shape[0]


def stack(blocks, after=(), flops=0):
    depth = sum(block.shape[0] for block in blocks)
    return pl.pallas_call(
        lambda *refs: stack_kernel(len(blocks), *refs),
        out_shape=jax.ShapeDtypeStruct((depth, *blocks[0].shape[1:]), blocks[0].dtype),
        in_specs=[VMEM] * len(blocks) + [pl.BlockSpec(memory_space=pl.ANY)] * len(after),
        out_specs=VMEM,
        compiler_params=pltpu.CompilerParams(vmem_limit_bytes=SMALL),
        cost_estimate=pl.CostEstimate(flops=flops, bytes_accessed=0, transcendentals=0),
        name="stack",
    )(*blocks, *after)


def halves(white, where):
    groups = lax.axis_size("tm")
    blocks = [white[None]] + [swap(white[None], "tm", k) for k in range(1, groups)]
    return stack(blocks[:groups // 2], after=(where,)), stack(blocks[groups // 2:], flops=10**9)


def between_chips(half, parts):
    chips = lax.axis_size("chan") // CORES
    places = [0, *range(chips - 1, 0, -1)]
    blocks = [swap(half, "chan", CORES * k) if k else half for k in places]
    each = chips // parts
    return [(places[i:i + each], blocks[i:i + each]) for i in range(0, chips, each)]


def between_cores(parts):
    collected = [(places, stack(blocks)) for places, blocks in parts]
    return [(places, own, swap(own, "chan", 1)) for places, own in collected]


def per_device(spectra, bad_channels, tile_list):
    groups = lax.axis_size("tm")
    hours = spectra.shape[1] * groups
    tiles = tile_list.shape[0] // groups
    white = whiten(spectra, bad_channels)
    pairs = lax.dynamic_slice_in_dim(tile_list, lax.axis_index("tm") * tiles, tiles, axis=0)
    where = jnp.concatenate([lax.axis_index("chan").reshape(1), pairs.reshape(-1)]).astype(jnp.int32).reshape(1, -1)
    near, far = halves(white, where)
    near, far = between_cores(between_chips(near, 2)), between_cores(between_chips(far, 2))
    partial = correlate(near, groups // 2, where, range(tiles), hours)
    out = correlate(far, groups // 2, where, range(tiles), hours, [partial])
    return out.reshape(tiles, LAGS, TILE, TILE)


def solution(mesh):
    placed = (P(None, "tm", None, "chan"), P("chan"), P("chan", None))
    return jax.shard_map(
        per_device,
        mesh=mesh,
        in_specs=placed,
        out_specs=P(("chan", "tm"), None, None, None),
        check_vma=False,
    )
```

```python
import math

import jax
import jax.numpy as jnp
from jax import lax
from jax.experimental import pallas as pl
from jax.experimental.pallas import tpu as pltpu
from jax.sharding import PartitionSpec as P

F = 64
LAGS = 32
TILE = 128
EPSILON = 1e-06
CORES = 2
SMALL = 4 * 1024 * 1024
VMEM = pl.BlockSpec(memory_space=pltpu.VMEM)
COARSE = (-12, -4, 4, 12)
FINE = (-4, -3, -2, -1, 0, 1, 2, 3)
LEFT_ORDER = (-4, 4, -12, 12)
STEPS = (0, -2, 2, -4)


def whiten_kernel(spectra_hbm, bad_hbm, out_ref, spectra_ref, bad_ref, sems):
    copies = [
        pltpu.make_async_copy(spectra_hbm, spectra_ref, sems.at[0]),
        pltpu.make_async_copy(bad_hbm, bad_ref, sems.at[1]),
    ]
    for copy in copies:
        copy.start()
    bins, hours, _, chans = spectra_ref.shape
    rows = bins * hours * 2
    row = lax.broadcasted_iota(jnp.int32, (rows, chans), 0)
    hour = (row // 2) % hours
    src = lax.broadcasted_iota(jnp.int32, (rows, rows), 0)
    dst = lax.broadcasted_iota(jnp.int32, (rows, rows), 1)
    move = jnp.where((src % 2) * (rows // 2) + src // 2 == dst, 1.0, 0.0).astype(jnp.bfloat16)
    for copy in copies:
        copy.wait()
    values = spectra_ref[...].reshape(rows, chans).astype(jnp.float32)
    keep = (1 - bad_ref[...]).astype(jnp.float32)
    squares = values * values
    scale = jnp.zeros((rows, chans), jnp.float32)
    for h in range(hours):
        power = jnp.sum(jnp.where(hour == h, squares, 0.0), axis=0, keepdims=True) * (1.0 / (2 * bins))
        scale = jnp.where(hour == h, lax.rsqrt(power + EPSILON) * keep, scale)
    white = (values * scale).astype(jnp.bfloat16)
    out_ref[...] = lax.dot_general(
        white, move, (((0,), (0,)), ((), ())), preferred_element_type=jnp.float32
    ).astype(jnp.bfloat16)


def whiten(spectra, bad_channels):
    bins, hours, _, chans = spectra.shape
    spectra = pltpu.with_memory_space_constraint(spectra, pltpu.HBM)
    bad_channels = pltpu.with_memory_space_constraint(bad_channels.reshape(1, chans), pltpu.HBM)
    return pl.pallas_call(
        whiten_kernel,
        out_shape=jax.ShapeDtypeStruct((chans, bins * hours * 2), jnp.bfloat16),
        in_specs=[pl.BlockSpec(memory_space=pltpu.HBM)] * 2,
        out_specs=VMEM,
        scratch_shapes=[
            pltpu.VMEM(spectra.shape, spectra.dtype),
            pltpu.VMEM((1, chans), bad_channels.dtype),
            pltpu.SemaphoreType.DMA((2,)),
        ],
        compiler_params=pltpu.CompilerParams(vmem_limit_bytes=SMALL),
        name="whiten",
    )(spectra, bad_channels)


def cos_sin(turn):
    quarter = F // 2
    shifted = turn + quarter // 2
    x = (shifted % quarter - quarter // 2).astype(jnp.float32) * (math.pi / F)
    y = x * x
    cos = 1 - y * (1 / 2 - y * (1 / 24 - y * (1 / 720 - y * (1 / 40320 - y / 3628800))))
    sin = x * (1 - y * (1 / 6 - y * (1 / 120 - y * (1 / 5040 - y / 362880))))
    quadrant = shifted // quarter % 4
    odd = quadrant % 2 == 1
    cos, sin = jnp.where(odd, sin, cos), jnp.where(odd, cos, sin)
    return jnp.where((quadrant == 1) | (quadrant == 2), -cos, cos), jnp.where(quadrant >= 2, -sin, sin)


def turn_by(re, im, cos, sin, both):
    rc, rs, ic, is_ = re * cos, re * sin, im * cos, im * sin
    forward = (rc - is_, rs + ic)
    return (forward, (rc + is_, ic - rs)) if both else (forward,)


def correlate_kernel(norm, picked, adds, places, where_ref, *refs):
    parts, refs = refs[:2 * len(places)], refs[2 * len(places):]
    partials = refs[:adds]
    out_ref = refs[adds]
    spectra, left_turned, right_turned, *more = refs[adds + 1:]
    groups, _, lanes = spectra.shape
    half = lanes // 2
    hours_dev = half // F
    bin_number = lax.broadcasted_iota(jnp.int32, (8, half), 1) // hours_dev + 1
    step = lax.broadcasted_iota(jnp.int32, (8, half), 0)
    cos, sin = cos_sin(jnp.where(step == 6, 12, step) * bin_number)
    table = {k: (cos[i:i + 1], sin[i:i + 1]) for k, i in ((1, 1), (2, 2), (3, 3), (4, 4), (12, 6))}

    chan = where_ref[0, 0]
    for i, piece in enumerate(parts):
        rows = piece.shape[1]
        for slot, k in enumerate(places[i // 2]):
            place = pl.multiple_of((chan ^ (CORES * k + i % 2)) * rows, 32)
            spectra[:, pl.ds(place, rows), :] = piece[slot * groups:(slot + 1) * groups]

    def load(block, g):
        whole = spectra[g, pl.ds(pl.multiple_of(block * TILE, TILE), TILE), :].astype(jnp.float32)
        return whole[:, :half], whole[:, half:]

    def store(ref, slot, index, g, value):
        rows_at = pl.ds(index * TILE, TILE)
        ref[slot, rows_at, g * lanes:g * lanes + half] = value[0].astype(jnp.bfloat16)
        ref[slot, rows_at, g * lanes + half:(g + 1) * lanes] = value[1].astype(jnp.bfloat16)

    def turn_left(slot, block, k):
        for g in range(groups):
            forward, backward = turn_by(*load(block, g), *(norm * part for part in table[k]), True)
            store(left_turned, slot, LEFT_ORDER.index(k), g, forward)
            store(left_turned, slot, LEFT_ORDER.index(-k), g, backward)

    def turn_right(slot, block, k):
        for g in range(groups):
            re, im = load(block, g)
            if k == 1:
                store(right_turned, slot, FINE.index(0), g, (re, im))
            turns = turn_by(re, im, *table[k], k in FINE)
            for lag, value in zip((-k, k), turns):
                store(right_turned, slot, FINE.index(lag), g, value)

    copies = []
    for i, t in enumerate(picked):
        slot = i % left_turned.shape[0]
        left_block, right_block = where_ref[0, 1 + 2 * t], where_ref[0, 2 + 2 * t]
        for j, lag in enumerate(STEPS):
            fine = FINE.index(lag)
            turn_right(slot, right_block, j + 1)
            for first in range(0, len(COARSE), 2):
                if j == 0:
                    turn_left(slot, left_block, LEFT_ORDER[first + 1])
                total = lax.dot_general(
                    left_turned[slot, first * TILE:(first + 2) * TILE, :],
                    right_turned[slot, fine * TILE:(fine + 2) * TILE, :],
                    (((1,), (1,)), ((), ())),
                    preferred_element_type=jnp.float32,
                )
                for v, s in ((0, 0), (0, 1), (1, 0), (1, 1)):
                    u = COARSE.index(LEFT_ORDER[first + v])
                    value = total[v * TILE:(v + 1) * TILE, s * TILE:(s + 1) * TILE]
                    if adds:
                        each = len(picked) // adds
                        more[0][i, u, fine + s] = partials[i // each][i % each, u, fine + s] + value
                    else:
                        out_ref[i, u, fine + s] = value
            if adds:
                done = (i, slice(None), pl.ds(fine, 2))
                copy = pltpu.make_async_copy(more[0].at[done], out_ref.at[done], more[1])
                copy.start(priority=j % 2)
                copies.append(copy)
    for copy in copies:
        copy.wait()


def correlate(parts, groups, where, picked, hours, partials=()):
    places = [part[0] for part in parts]
    pieces = [piece for part in parts for piece in part[1:]]
    _, rows, lanes = pieces[0].shape
    fine = len(FINE)
    shape = (len(picked), len(COARSE), fine, TILE, TILE)
    norm = 1.0 / math.sqrt(F * hours)
    slots = min(len(picked), 2)
    chans = CORES * sum(map(len, places)) * rows
    scratch = 2 * (groups * chans * lanes + slots * (len(COARSE) + fine) * TILE * groups * lanes)
    adds = len(partials)
    more = []
    if adds:
        more = [pltpu.VMEM(shape, jnp.float32), pltpu.SemaphoreType.DMA]
        scratch += 4 * math.prod(shape)
    return pl.pallas_call(
        lambda *refs: correlate_kernel(norm, picked, adds, places, *refs),
        out_shape=jax.ShapeDtypeStruct(shape, jnp.float32),
        in_specs=[VMEM] * (1 + len(pieces) + adds),
        out_specs=pl.BlockSpec(memory_space=pl.ANY) if adds else VMEM,
        scratch_shapes=[
            pltpu.VMEM((groups, chans, lanes), jnp.bfloat16),
            pltpu.VMEM((slots, len(COARSE) * TILE, groups * lanes), jnp.bfloat16),
            pltpu.VMEM((slots, fine * TILE, groups * lanes), jnp.bfloat16),
            *more,
        ],
        compiler_params=pltpu.CompilerParams(vmem_limit_bytes=scratch + SMALL),
        cost_estimate=pl.CostEstimate(flops=0, bytes_accessed=0, transcendentals=0),
        name="correlate_add" if adds else "correlate",
    )(where, *pieces, *partials)


def swap(array, axis, k):
    return lax.ppermute(array, axis, [(i, i ^ k) for i in range(lax.axis_size(axis))])


def stack_kernel(blocks, *refs):
    out_ref = refs[-1]
    first = 0
    for block in refs[:blocks]:
        out_ref[first:first + block.shape[0]] = block[...]
        first += block.shape[0]


def stack(blocks, after=(), flops=0):
    depth = sum(block.shape[0] for block in blocks)
    return pl.pallas_call(
        lambda *refs: stack_kernel(len(blocks), *refs),
        out_shape=jax.ShapeDtypeStruct((depth, *blocks[0].shape[1:]), blocks[0].dtype),
        in_specs=[VMEM] * len(blocks) + [pl.BlockSpec(memory_space=pl.ANY)] * len(after),
        out_specs=VMEM,
        compiler_params=pltpu.CompilerParams(vmem_limit_bytes=SMALL),
        cost_estimate=pl.CostEstimate(flops=flops, bytes_accessed=0, transcendentals=0),
        name="stack",
    )(*blocks, *after)


def halves(white, where):
    groups = lax.axis_size("tm")
    blocks = [white[None]] + [swap(white[None], "tm", k) for k in range(1, groups)]
    return stack(blocks[:groups // 2], after=(where,)), stack(blocks[groups // 2:], flops=10**9)


def between_chips(half, parts):
    chips = lax.axis_size("chan") // CORES
    places = [0, *range(chips - 1, 0, -1)]
    blocks = [swap(half, "chan", CORES * k) if k else half for k in places]
    each = chips // parts
    return [(places[i:i + each], blocks[i:i + each]) for i in range(0, chips, each)]


def between_cores(parts):
    collected = [(places, stack(blocks)) for places, blocks in parts]
    return [(places, own, swap(own, "chan", 1)) for places, own in collected]


def per_device(spectra, bad_channels, tile_list):
    groups = lax.axis_size("tm")
    hours = spectra.shape[1] * groups
    tiles = tile_list.shape[0] // groups
    white = whiten(spectra, bad_channels)
    pairs = lax.dynamic_slice_in_dim(tile_list, lax.axis_index("tm") * tiles, tiles, axis=0)
    where = jnp.concatenate([lax.axis_index("chan").reshape(1), pairs.reshape(-1)]).astype(jnp.int32).reshape(1, -1)
    near, far = halves(white, where)
    near, far = between_cores(between_chips(near, 2)), between_cores(between_chips(far, 2))
    partial = correlate(near, groups // 2, where, range(tiles), hours)
    out = correlate(far, groups // 2, where, range(tiles), hours, [partial])
    return out.reshape(tiles, LAGS, TILE, TILE)


def solution(mesh):
    placed = (P(None, "tm", None, "chan"), P("chan"), P("chan", None))
    return jax.shard_map(
        per_device,
        mesh=mesh,
        in_specs=placed,
        out_specs=P(("chan", "tm"), None, None, None),
        check_vma=False,
    )
```

```python
import math

import jax
import jax.numpy as jnp
from jax import lax
from jax.experimental import pallas as pl
from jax.experimental.pallas import tpu as pltpu
from jax.sharding import PartitionSpec as P

F = 64
LAGS = 32
TILE = 128
EPSILON = 1e-06
CORES = 2
SMALL = 4 * 1024 * 1024
VMEM = pl.BlockSpec(memory_space=pltpu.VMEM)
COARSE = (-12, -4, 4, 12)
FINE = (-4, -3, -2, -1, 0, 1, 2, 3)
LEFT_ORDER = (-4, 4, -12, 12)
STEPS = (0, -2, 2, -4)


def whiten_kernel(spectra_hbm, bad_hbm, out_ref, spectra_ref, bad_ref, sems):
    copies = [
        pltpu.make_async_copy(spectra_hbm, spectra_ref, sems.at[0]),
        pltpu.make_async_copy(bad_hbm, bad_ref, sems.at[1]),
    ]
    for copy in copies:
        copy.start()
    bins, hours, _, chans = spectra_ref.shape
    rows = bins * hours * 2
    row = lax.broadcasted_iota(jnp.int32, (rows, chans), 0)
    hour = (row // 2) % hours
    src = lax.broadcasted_iota(jnp.int32, (rows, rows), 0)
    dst = lax.broadcasted_iota(jnp.int32, (rows, rows), 1)
    move = jnp.where((src % 2) * (rows // 2) + src // 2 == dst, 1.0, 0.0).astype(jnp.bfloat16)
    for copy in copies:
        copy.wait()
    values = spectra_ref[...].reshape(rows, chans).astype(jnp.float32)
    keep = (1 - bad_ref[...]).astype(jnp.float32)
    squares = values * values
    scale = jnp.zeros((rows, chans), jnp.float32)
    for h in range(hours):
        power = jnp.sum(jnp.where(hour == h, squares, 0.0), axis=0, keepdims=True) * (1.0 / (2 * bins))
        scale = jnp.where(hour == h, lax.rsqrt(power + EPSILON) * keep, scale)
    white = (values * scale).astype(jnp.bfloat16)
    out_ref[...] = lax.dot_general(
        white, move, (((0,), (0,)), ((), ())), preferred_element_type=jnp.float32
    ).astype(jnp.bfloat16)


def whiten(spectra, bad_channels):
    bins, hours, _, chans = spectra.shape
    spectra = pltpu.with_memory_space_constraint(spectra, pltpu.HBM)
    bad_channels = pltpu.with_memory_space_constraint(bad_channels.reshape(1, chans), pltpu.HBM)
    return pl.pallas_call(
        whiten_kernel,
        out_shape=jax.ShapeDtypeStruct((chans, bins * hours * 2), jnp.bfloat16),
        in_specs=[pl.BlockSpec(memory_space=pltpu.HBM)] * 2,
        out_specs=VMEM,
        scratch_shapes=[
            pltpu.VMEM(spectra.shape, spectra.dtype),
            pltpu.VMEM((1, chans), bad_channels.dtype),
            pltpu.SemaphoreType.DMA((2,)),
        ],
        compiler_params=pltpu.CompilerParams(vmem_limit_bytes=SMALL),
        name="whiten",
    )(spectra, bad_channels)


def cos_sin(turn):
    quarter = F // 2
    shifted = turn + quarter // 2
    x = (shifted % quarter - quarter // 2).astype(jnp.float32) * (math.pi / F)
    y = x * x
    cos = 1 - y * (1 / 2 - y * (1 / 24 - y * (1 / 720 - y * (1 / 40320 - y / 3628800))))
    sin = x * (1 - y * (1 / 6 - y * (1 / 120 - y * (1 / 5040 - y / 362880))))
    quadrant = shifted // quarter % 4
    odd = quadrant % 2 == 1
    cos, sin = jnp.where(odd, sin, cos), jnp.where(odd, cos, sin)
    return jnp.where((quadrant == 1) | (quadrant == 2), -cos, cos), jnp.where(quadrant >= 2, -sin, sin)


def turn_by(re, im, cos, sin, both):
    rc, rs, ic, is_ = re * cos, re * sin, im * cos, im * sin
    forward = (rc - is_, rs + ic)
    return (forward, (rc + is_, ic - rs)) if both else (forward,)


def correlate_kernel(norm, picked, adds, slots_of, where_ref, *refs):
    partials, refs = refs[:adds], refs[adds:]
    parts, refs = refs[:2 * len(slots_of)], refs[2 * len(slots_of):]
    out_ref = refs[0]
    spectra, left_turned, right_turned, *more = refs[1:]
    groups, _, lanes = spectra.shape
    half = lanes // 2
    hours_dev = half // F
    bin_number = lax.broadcasted_iota(jnp.int32, (8, half), 1) // hours_dev + 1
    step = lax.broadcasted_iota(jnp.int32, (8, half), 0)
    cos, sin = cos_sin(jnp.where(step == 6, 12, step) * bin_number)
    table = {k: (cos[i:i + 1], sin[i:i + 1]) for k, i in ((1, 1), (2, 2), (3, 3), (4, 4), (12, 6))}

    chan = where_ref[0, 0]
    for i, piece in enumerate(parts):
        rows = piece.shape[1]
        for slot, (k, g) in enumerate(slots_of[i // 2]):
            place = pl.multiple_of((chan ^ (CORES * k + i % 2)) * rows, 32)
            spectra[g, pl.ds(place, rows), :] = piece[slot]

    def load(block, g):
        whole = spectra[g, pl.ds(pl.multiple_of(block * TILE, TILE), TILE), :].astype(jnp.float32)
        return whole[:, :half], whole[:, half:]

    def store(ref, slot, index, g, value):
        rows_at = pl.ds(index * TILE, TILE)
        ref[slot, rows_at, g * lanes:g * lanes + half] = value[0].astype(jnp.bfloat16)
        ref[slot, rows_at, g * lanes + half:(g + 1) * lanes] = value[1].astype(jnp.bfloat16)

    def turn_left(slot, block, k):
        for g in range(groups):
            forward, backward = turn_by(*load(block, g), *(norm * part for part in table[k]), True)
            store(left_turned, slot, LEFT_ORDER.index(k), g, forward)
            store(left_turned, slot, LEFT_ORDER.index(-k), g, backward)

    def turn_right(slot, block, k):
        for g in range(groups):
            re, im = load(block, g)
            if k == 1:
                store(right_turned, slot, FINE.index(0), g, (re, im))
            turns = turn_by(re, im, *table[k], k in FINE)
            for lag, value in zip((-k, k), turns):
                store(right_turned, slot, FINE.index(lag), g, value)

    copies = []
    for i, t in enumerate(picked):
        slot = i % left_turned.shape[0]
        left_block, right_block = where_ref[0, 1 + 2 * t], where_ref[0, 2 + 2 * t]
        for j, lag in enumerate(STEPS):
            fine = FINE.index(lag)
            turn_right(slot, right_block, j + 1)
            for first in range(0, len(COARSE), 2):
                if j == 0:
                    turn_left(slot, left_block, LEFT_ORDER[first + 1])
                total = lax.dot_general(
                    left_turned[slot, first * TILE:(first + 2) * TILE, :],
                    right_turned[slot, fine * TILE:(fine + 2) * TILE, :],
                    (((1,), (1,)), ((), ())),
                    preferred_element_type=jnp.float32,
                )
                for v, s in ((0, 0), (0, 1), (1, 0), (1, 1)):
                    u = COARSE.index(LEFT_ORDER[first + v])
                    value = total[v * TILE:(v + 1) * TILE, s * TILE:(s + 1) * TILE]
                    if adds:
                        each = len(picked) // adds
                        more[0][i, u, fine + s] = partials[i // each][i % each, u, fine + s] + value
                    else:
                        out_ref[i, u, fine + s] = value
            if adds:
                done = (i, slice(None), pl.ds(fine, 2))
                copy = pltpu.make_async_copy(more[0].at[done], out_ref.at[done], more[1])
                copy.start(priority=j % 2)
                copies.append(copy)
    for copy in copies:
        copy.wait()


def correlate(parts, groups, where, picked, hours, partials=()):
    slots_of = [part[0] for part in parts]
    pieces = [piece for part in parts for piece in part[1:]]
    _, rows, lanes = pieces[0].shape
    fine = len(FINE)
    shape = (len(picked), len(COARSE), fine, TILE, TILE)
    norm = 1.0 / math.sqrt(F * hours)
    slots = min(len(picked), 2)
    chans = lax.axis_size("chan") * rows
    scratch = 2 * (groups * chans * lanes + slots * (len(COARSE) + fine) * TILE * groups * lanes)
    adds = len(partials)
    more = []
    if adds:
        more = [pltpu.VMEM(shape, jnp.float32), pltpu.SemaphoreType.DMA]
        scratch += 4 * math.prod(shape)
    return pl.pallas_call(
        lambda *refs: correlate_kernel(norm, picked, adds, slots_of, *refs),
        out_shape=jax.ShapeDtypeStruct(shape, jnp.float32),
        in_specs=[VMEM] * (1 + len(pieces) + adds),
        out_specs=pl.BlockSpec(memory_space=pl.ANY) if adds else VMEM,
        scratch_shapes=[
            pltpu.VMEM((groups, chans, lanes), jnp.bfloat16),
            pltpu.VMEM((slots, len(COARSE) * TILE, groups * lanes), jnp.bfloat16),
            pltpu.VMEM((slots, fine * TILE, groups * lanes), jnp.bfloat16),
            *more,
        ],
        compiler_params=pltpu.CompilerParams(vmem_limit_bytes=scratch + SMALL),
        cost_estimate=pl.CostEstimate(flops=0, bytes_accessed=0, transcendentals=0),
        name="correlate_add" if adds else "correlate",
    )(where, *partials, *pieces)


def swap(array, axis, k):
    return lax.ppermute(array, axis, [(i, i ^ k) for i in range(lax.axis_size(axis))])


def stack_kernel(blocks, *refs):
    out_ref = refs[-1]
    first = 0
    for block in refs[:blocks]:
        out_ref[first:first + block.shape[0]] = block[...]
        first += block.shape[0]


def stack(blocks, after=(), flops=0):
    depth = sum(block.shape[0] for block in blocks)
    return pl.pallas_call(
        lambda *refs: stack_kernel(len(blocks), *refs),
        out_shape=jax.ShapeDtypeStruct((depth, *blocks[0].shape[1:]), blocks[0].dtype),
        in_specs=[VMEM] * len(blocks) + [pl.BlockSpec(memory_space=pl.ANY)] * len(after),
        out_specs=VMEM,
        compiler_params=pltpu.CompilerParams(vmem_limit_bytes=SMALL),
        cost_estimate=pl.CostEstimate(flops=flops, bytes_accessed=0, transcendentals=0),
        name="stack",
    )(*blocks, *after)


def between_chips(block):
    chips = lax.axis_size("chan") // CORES
    return [(k, swap(block, "chan", CORES * k) if k else block) for k in (0, *range(chips - 1, 0, -1))]


def both_cores(slots, own):
    return slots, own, swap(own, "chan", 1)


def per_device(spectra, bad_channels, tile_list):
    groups = lax.axis_size("tm")
    hours = spectra.shape[1] * groups
    tiles = tile_list.shape[0] // groups
    white = whiten(spectra, bad_channels)[None]
    pairs = lax.dynamic_slice_in_dim(tile_list, lax.axis_index("tm") * tiles, tiles, axis=0)
    where = jnp.concatenate([lax.axis_index("chan").reshape(1), pairs.reshape(-1)]).astype(jnp.int32).reshape(1, -1)
    far = stack([swap(white, "tm", k) for k in range(groups // 2, groups)])
    plane = between_chips(white)
    own = stack([block for _, block in plane], after=(where,))
    near = [own] + [swap(own, "tm", k) for k in range(1, groups // 2)]
    near = [both_cores([(k, g) for k, _ in plane], block) for g, block in enumerate(near)]
    plane = between_chips(far)
    far = []
    for part, flops in ((plane[:len(plane) // 2], 15 * 10**8), (plane[len(plane) // 2:], 0)):
        slots = [(k, g) for k, _ in part for g in range(groups // 2)]
        far.append(both_cores(slots, stack([block for _, block in part], flops=flops)))
    partial = correlate(near, groups // 2, where, range(tiles), hours)
    out = correlate(far, groups // 2, where, range(tiles), hours, [partial])
    return out.reshape(tiles, LAGS, TILE, TILE)


def solution(mesh):
    placed = (P(None, "tm", None, "chan"), P("chan"), P("chan", None))
    return jax.shard_map(
        per_device,
        mesh=mesh,
        in_specs=placed,
        out_specs=P(("chan", "tm"), None, None, None),
        check_vma=False,
    )
```

```python
import math

import jax
import jax.numpy as jnp
from jax import lax
from jax.experimental import pallas as pl
from jax.experimental.pallas import tpu as pltpu
from jax.sharding import PartitionSpec as P

F = 64
LAGS = 32
TILE = 128
EPSILON = 1e-06
CORES = 2
SMALL = 4 * 1024 * 1024
VMEM = pl.BlockSpec(memory_space=pltpu.VMEM)
COARSE = (-12, -4, 4, 12)
FINE = (-4, -3, -2, -1, 0, 1, 2, 3)
LEFT_ORDER = (-4, 4, -12, 12)
STEPS = (0, -2, 2, -4)


def whiten_kernel(spectra_hbm, bad_hbm, out_ref, spectra_ref, bad_ref, sems):
    copies = [
        pltpu.make_async_copy(spectra_hbm, spectra_ref, sems.at[0]),
        pltpu.make_async_copy(bad_hbm, bad_ref, sems.at[1]),
    ]
    for copy in copies:
        copy.start()
    bins, hours, _, chans = spectra_ref.shape
    rows = bins * hours * 2
    row = lax.broadcasted_iota(jnp.int32, (rows, chans), 0)
    hour = (row // 2) % hours
    src = lax.broadcasted_iota(jnp.int32, (rows, rows), 0)
    dst = lax.broadcasted_iota(jnp.int32, (rows, rows), 1)
    move = jnp.where((src % 2) * (rows // 2) + src // 2 == dst, 1.0, 0.0).astype(jnp.bfloat16)
    for copy in copies:
        copy.wait()
    values = spectra_ref[...].reshape(rows, chans).astype(jnp.float32)
    keep = (1 - bad_ref[...]).astype(jnp.float32)
    squares = values * values
    scale = jnp.zeros((rows, chans), jnp.float32)
    for h in range(hours):
        power = jnp.sum(jnp.where(hour == h, squares, 0.0), axis=0, keepdims=True) * (1.0 / (2 * bins))
        scale = jnp.where(hour == h, lax.rsqrt(power + EPSILON) * keep, scale)
    white = (values * scale).astype(jnp.bfloat16)
    out_ref[...] = lax.dot_general(
        white, move, (((0,), (0,)), ((), ())), preferred_element_type=jnp.float32
    ).astype(jnp.bfloat16)


def whiten(spectra, bad_channels):
    bins, hours, _, chans = spectra.shape
    spectra = pltpu.with_memory_space_constraint(spectra, pltpu.HBM)
    bad_channels = pltpu.with_memory_space_constraint(bad_channels.reshape(1, chans), pltpu.HBM)
    return pl.pallas_call(
        whiten_kernel,
        out_shape=jax.ShapeDtypeStruct((chans, bins * hours * 2), jnp.bfloat16),
        in_specs=[pl.BlockSpec(memory_space=pltpu.HBM)] * 2,
        out_specs=VMEM,
        scratch_shapes=[
            pltpu.VMEM(spectra.shape, spectra.dtype),
            pltpu.VMEM((1, chans), bad_channels.dtype),
            pltpu.SemaphoreType.DMA((2,)),
        ],
        compiler_params=pltpu.CompilerParams(vmem_limit_bytes=SMALL),
        name="whiten",
    )(spectra, bad_channels)


def cos_sin(turn):
    quarter = F // 2
    shifted = turn + quarter // 2
    x = (shifted % quarter - quarter // 2).astype(jnp.float32) * (math.pi / F)
    y = x * x
    cos = 1 - y * (1 / 2 - y * (1 / 24 - y * (1 / 720 - y * (1 / 40320 - y / 3628800))))
    sin = x * (1 - y * (1 / 6 - y * (1 / 120 - y * (1 / 5040 - y / 362880))))
    quadrant = shifted // quarter % 4
    odd = quadrant % 2 == 1
    cos, sin = jnp.where(odd, sin, cos), jnp.where(odd, cos, sin)
    return jnp.where((quadrant == 1) | (quadrant == 2), -cos, cos), jnp.where(quadrant >= 2, -sin, sin)


def turn_by(re, im, cos, sin, both):
    rc, rs, ic, is_ = re * cos, re * sin, im * cos, im * sin
    forward = (rc - is_, rs + ic)
    return (forward, (rc + is_, ic - rs)) if both else (forward,)


def correlate_kernel(norm, picked, adds, places, where_ref, *refs):
    parts, refs = refs[:2 * len(places)], refs[2 * len(places):]
    partials = refs[:adds]
    out_ref = refs[adds]
    spectra, left_turned, right_turned, *more = refs[adds + 1:]
    groups, _, lanes = spectra.shape
    half = lanes // 2
    hours_dev = half // F
    bin_number = lax.broadcasted_iota(jnp.int32, (8, half), 1) // hours_dev + 1
    step = lax.broadcasted_iota(jnp.int32, (8, half), 0)
    cos, sin = cos_sin(jnp.where(step == 6, 12, step) * bin_number)
    table = {k: (cos[i:i + 1], sin[i:i + 1]) for k, i in ((1, 1), (2, 2), (3, 3), (4, 4), (12, 6))}

    chan = where_ref[0, 0]
    for i, piece in enumerate(parts):
        rows = piece.shape[1]
        for slot, k in enumerate(places[i // 2]):
            place = pl.multiple_of((chan ^ (CORES * k + i % 2)) * rows, 32)
            spectra[:, pl.ds(place, rows), :] = piece[slot * groups:(slot + 1) * groups]

    def load(block, g):
        whole = spectra[g, pl.ds(pl.multiple_of(block * TILE, TILE), TILE), :].astype(jnp.float32)
        return whole[:, :half], whole[:, half:]

    def store(ref, slot, index, g, value):
        rows_at = pl.ds(index * TILE, TILE)
        ref[slot, rows_at, g * lanes:g * lanes + half] = value[0].astype(jnp.bfloat16)
        ref[slot, rows_at, g * lanes + half:(g + 1) * lanes] = value[1].astype(jnp.bfloat16)

    def turn_left(slot, block, k):
        for g in range(groups):
            forward, backward = turn_by(*load(block, g), *(norm * part for part in table[k]), True)
            store(left_turned, slot, LEFT_ORDER.index(k), g, forward)
            store(left_turned, slot, LEFT_ORDER.index(-k), g, backward)

    def turn_right(slot, block, k):
        for g in range(groups):
            re, im = load(block, g)
            if k == 1:
                store(right_turned, slot, FINE.index(0), g, (re, im))
            turns = turn_by(re, im, *table[k], k in FINE)
            for lag, value in zip((-k, k), turns):
                store(right_turned, slot, FINE.index(lag), g, value)

    copies = []
    for i, t in enumerate(picked):
        slot = i % left_turned.shape[0]
        left_block, right_block = where_ref[0, 1 + 2 * t], where_ref[0, 2 + 2 * t]
        for j, lag in enumerate(STEPS):
            fine = FINE.index(lag)
            turn_right(slot, right_block, j + 1)
            for first in range(0, len(COARSE), 2):
                if j == 0:
                    turn_left(slot, left_block, LEFT_ORDER[first + 1])
                total = lax.dot_general(
                    left_turned[slot, first * TILE:(first + 2) * TILE, :],
                    right_turned[slot, fine * TILE:(fine + 2) * TILE, :],
                    (((1,), (1,)), ((), ())),
                    preferred_element_type=jnp.float32,
                )
                for v, s in ((0, 0), (0, 1), (1, 0), (1, 1)):
                    u = COARSE.index(LEFT_ORDER[first + v])
                    value = total[v * TILE:(v + 1) * TILE, s * TILE:(s + 1) * TILE]
                    if adds:
                        each = len(picked) // adds
                        more[0][i, u, fine + s] = partials[i // each][i % each, u, fine + s] + value
                    else:
                        out_ref[i, u, fine + s] = value
            if adds:
                done = (i, slice(None), pl.ds(fine, 2))
                copy = pltpu.make_async_copy(more[0].at[done], out_ref.at[done], more[1])
                copy.start(priority=j % 2)
                copies.append(copy)
    for copy in copies:
        copy.wait()


def correlate(parts, groups, where, picked, hours, partials=()):
    places = [part[0] for part in parts]
    pieces = [piece for part in parts for piece in part[1:]]
    _, rows, lanes = pieces[0].shape
    fine = len(FINE)
    shape = (len(picked), len(COARSE), fine, TILE, TILE)
    norm = 1.0 / math.sqrt(F * hours)
    slots = min(len(picked), 2)
    chans = CORES * sum(map(len, places)) * rows
    scratch = 2 * (groups * chans * lanes + slots * (len(COARSE) + fine) * TILE * groups * lanes)
    adds = len(partials)
    more = []
    if adds:
        more = [pltpu.VMEM(shape, jnp.float32), pltpu.SemaphoreType.DMA]
        scratch += 4 * math.prod(shape)
    return pl.pallas_call(
        lambda *refs: correlate_kernel(norm, picked, adds, places, *refs),
        out_shape=jax.ShapeDtypeStruct(shape, jnp.float32),
        in_specs=[VMEM] * (1 + len(pieces) + adds),
        out_specs=pl.BlockSpec(memory_space=pl.ANY) if adds else VMEM,
        scratch_shapes=[
            pltpu.VMEM((groups, chans, lanes), jnp.bfloat16),
            pltpu.VMEM((slots, len(COARSE) * TILE, groups * lanes), jnp.bfloat16),
            pltpu.VMEM((slots, fine * TILE, groups * lanes), jnp.bfloat16),
            *more,
        ],
        compiler_params=pltpu.CompilerParams(vmem_limit_bytes=scratch + SMALL),
        cost_estimate=pl.CostEstimate(flops=0, bytes_accessed=0, transcendentals=0),
        name="correlate_add" if adds else "correlate",
    )(where, *pieces, *partials)


def swap(array, axis, k):
    return lax.ppermute(array, axis, [(i, i ^ k) for i in range(lax.axis_size(axis))])


def stack_kernel(blocks, *refs):
    out_ref = refs[-1]
    first = 0
    for block in refs[:blocks]:
        out_ref[first:first + block.shape[0]] = block[...]
        first += block.shape[0]


def stack(blocks, after=(), flops=0):
    depth = sum(block.shape[0] for block in blocks)
    return pl.pallas_call(
        lambda *refs: stack_kernel(len(blocks), *refs),
        out_shape=jax.ShapeDtypeStruct((depth, *blocks[0].shape[1:]), blocks[0].dtype),
        in_specs=[VMEM] * len(blocks) + [pl.BlockSpec(memory_space=pl.ANY)] * len(after),
        out_specs=VMEM,
        compiler_params=pltpu.CompilerParams(vmem_limit_bytes=SMALL),
        cost_estimate=pl.CostEstimate(flops=flops, bytes_accessed=0, transcendentals=0),
        name="stack",
    )(*blocks, *after)


def halves(white, where):
    groups = lax.axis_size("tm")
    blocks = [white[None]] + [swap(white[None], "tm", k) for k in range(1, groups)]
    return stack(blocks[:groups // 2], after=(where,)), stack(blocks[groups // 2:], flops=10**9)


def between_chips(half, parts, places):
    blocks = [swap(half, "chan", CORES * k) if k else half for k in places]
    each = len(places) // parts
    return [(places[i:i + each], blocks[i:i + each]) for i in range(0, len(places), each)]


def between_cores(part, after=(), flops=0):
    places, blocks = part
    own = stack(blocks, after, flops)
    return places, own, swap(own, "chan", 1)


def per_device(spectra, bad_channels, tile_list):
    groups = lax.axis_size("tm")
    hours = spectra.shape[1] * groups
    tiles = tile_list.shape[0] // groups
    white = whiten(spectra, bad_channels)
    pairs = lax.dynamic_slice_in_dim(tile_list, lax.axis_index("tm") * tiles, tiles, axis=0)
    where = jnp.concatenate([lax.axis_index("chan").reshape(1), pairs.reshape(-1)]).astype(jnp.int32).reshape(1, -1)
    near, far = halves(white, where)
    chips = lax.axis_size("chan") // CORES
    near = [between_cores(part) for part in between_chips(near, 2, range(chips))]
    *first, last = between_chips(far, 2, [0, *range(chips - 1, 0, -1)])
    partial = correlate(near, groups // 2, where, range(tiles), hours)
    far = [between_cores(part, flops=3 * 10**9) for part in first]
    far.append(between_cores(last, (partial,)))
    out = correlate(far, groups // 2, where, range(tiles), hours, [partial])
    return out.reshape(tiles, LAGS, TILE, TILE)


def solution(mesh):
    placed = (P(None, "tm", None, "chan"), P("chan"), P("chan", None))
    return jax.shard_map(
        per_device,
        mesh=mesh,
        in_specs=placed,
        out_specs=P(("chan", "tm"), None, None, None),
        check_vma=False,
    )
```

```python
import math

import jax
import jax.numpy as jnp
from jax import lax
from jax.experimental import pallas as pl
from jax.experimental.pallas import tpu as pltpu
from jax.sharding import PartitionSpec as P

F = 64
LAGS = 32
TILE = 128
EPSILON = 1e-06
CORES = 2
SMALL = 4 * 1024 * 1024
VMEM = pl.BlockSpec(memory_space=pltpu.VMEM)
COARSE = (-12, -4, 4, 12)
FINE = (-4, -3, -2, -1, 0, 1, 2, 3)
LEFT_ORDER = (-4, 4, -12, 12)
STEPS = (0, -2, 2, -4)


def whiten_kernel(spectra_hbm, bad_hbm, out_ref, spectra_ref, bad_ref, sems):
    copies = [
        pltpu.make_async_copy(spectra_hbm, spectra_ref, sems.at[0]),
        pltpu.make_async_copy(bad_hbm, bad_ref, sems.at[1]),
    ]
    for copy in copies:
        copy.start()
    bins, hours, _, chans = spectra_ref.shape
    rows = bins * hours * 2
    row = lax.broadcasted_iota(jnp.int32, (rows, chans), 0)
    hour = (row // 2) % hours
    src = lax.broadcasted_iota(jnp.int32, (rows, rows), 0)
    dst = lax.broadcasted_iota(jnp.int32, (rows, rows), 1)
    move = jnp.where((src % 2) * (rows // 2) + src // 2 == dst, 1.0, 0.0).astype(jnp.bfloat16)
    for copy in copies:
        copy.wait()
    values = spectra_ref[...].reshape(rows, chans).astype(jnp.float32)
    keep = (1 - bad_ref[...]).astype(jnp.float32)
    squares = values * values
    scale = jnp.zeros((rows, chans), jnp.float32)
    for h in range(hours):
        power = jnp.sum(jnp.where(hour == h, squares, 0.0), axis=0, keepdims=True) * (1.0 / (2 * bins))
        scale = jnp.where(hour == h, lax.rsqrt(power + EPSILON) * keep, scale)
    white = (values * scale).astype(jnp.bfloat16)
    out_ref[...] = lax.dot_general(
        white, move, (((0,), (0,)), ((), ())), preferred_element_type=jnp.float32
    ).astype(jnp.bfloat16)


def whiten(spectra, bad_channels):
    bins, hours, _, chans = spectra.shape
    spectra = pltpu.with_memory_space_constraint(spectra, pltpu.HBM)
    bad_channels = pltpu.with_memory_space_constraint(bad_channels.reshape(1, chans), pltpu.HBM)
    return pl.pallas_call(
        whiten_kernel,
        out_shape=jax.ShapeDtypeStruct((chans, bins * hours * 2), jnp.bfloat16),
        in_specs=[pl.BlockSpec(memory_space=pltpu.HBM)] * 2,
        out_specs=VMEM,
        scratch_shapes=[
            pltpu.VMEM(spectra.shape, spectra.dtype),
            pltpu.VMEM((1, chans), bad_channels.dtype),
            pltpu.SemaphoreType.DMA((2,)),
        ],
        compiler_params=pltpu.CompilerParams(vmem_limit_bytes=SMALL),
        name="whiten",
    )(spectra, bad_channels)


def cos_sin(turn):
    quarter = F // 2
    shifted = turn + quarter // 2
    x = (shifted % quarter - quarter // 2).astype(jnp.float32) * (math.pi / F)
    y = x * x
    cos = 1 - y * (1 / 2 - y * (1 / 24 - y * (1 / 720 - y * (1 / 40320 - y / 3628800))))
    sin = x * (1 - y * (1 / 6 - y * (1 / 120 - y * (1 / 5040 - y / 362880))))
    quadrant = shifted // quarter % 4
    odd = quadrant % 2 == 1
    cos, sin = jnp.where(odd, sin, cos), jnp.where(odd, cos, sin)
    return jnp.where((quadrant == 1) | (quadrant == 2), -cos, cos), jnp.where(quadrant >= 2, -sin, sin)


def turn_by(re, im, cos, sin, both):
    rc, rs, ic, is_ = re * cos, re * sin, im * cos, im * sin
    forward = (rc - is_, rs + ic)
    return (forward, (rc + is_, ic - rs)) if both else (forward,)


def correlate_kernel(norm, picked, adds, places, where_ref, *refs):
    parts, refs = refs[:2 * len(places)], refs[2 * len(places):]
    partials = refs[:adds]
    out_ref = refs[adds]
    spectra, left_turned, right_turned, *more = refs[adds + 1:]
    groups, _, lanes = spectra.shape
    half = lanes // 2
    hours_dev = half // F
    bin_number = lax.broadcasted_iota(jnp.int32, (8, half), 1) // hours_dev + 1
    step = lax.broadcasted_iota(jnp.int32, (8, half), 0)
    cos, sin = cos_sin(jnp.where(step == 6, 12, step) * bin_number)
    table = {k: (cos[i:i + 1], sin[i:i + 1]) for k, i in ((1, 1), (2, 2), (3, 3), (4, 4), (12, 6))}

    chan = where_ref[0, 0]
    for i, piece in enumerate(parts):
        rows = piece.shape[1]
        for slot, k in enumerate(places[i // 2]):
            place = pl.multiple_of((chan ^ (CORES * k + i % 2)) * rows, 32)
            spectra[:, pl.ds(place, rows), :] = piece[slot * groups:(slot + 1) * groups]

    def load(block, g):
        whole = spectra[g, pl.ds(pl.multiple_of(block * TILE, TILE), TILE), :].astype(jnp.float32)
        return whole[:, :half], whole[:, half:]

    def store(ref, slot, index, g, value):
        rows_at = pl.ds(index * TILE, TILE)
        ref[slot, rows_at, g * lanes:g * lanes + half] = value[0].astype(jnp.bfloat16)
        ref[slot, rows_at, g * lanes + half:(g + 1) * lanes] = value[1].astype(jnp.bfloat16)

    def turn_left(slot, block, k):
        for g in range(groups):
            forward, backward = turn_by(*load(block, g), *(norm * part for part in table[k]), True)
            store(left_turned, slot, LEFT_ORDER.index(k), g, forward)
            store(left_turned, slot, LEFT_ORDER.index(-k), g, backward)

    def turn_right(slot, block, k):
        for g in range(groups):
            re, im = load(block, g)
            if k == 1:
                store(right_turned, slot, FINE.index(0), g, (re, im))
            turns = turn_by(re, im, *table[k], k in FINE)
            for lag, value in zip((-k, k), turns):
                store(right_turned, slot, FINE.index(lag), g, value)

    copies = []
    for i, t in enumerate(picked):
        slot = i % left_turned.shape[0]
        left_block, right_block = where_ref[0, 1 + 2 * t], where_ref[0, 2 + 2 * t]
        for j, lag in enumerate(STEPS):
            fine = FINE.index(lag)
            turn_right(slot, right_block, j + 1)
            for first in range(len(COARSE)):
                if j == 0 and first % 2 == 0:
                    turn_left(slot, left_block, LEFT_ORDER[first + 1])
                total = lax.dot_general(
                    left_turned[slot, first * TILE:(first + 1) * TILE, :],
                    right_turned[slot, fine * TILE:(fine + 2) * TILE, :],
                    (((1,), (1,)), ((), ())),
                    preferred_element_type=jnp.float32,
                )
                u = COARSE.index(LEFT_ORDER[first])
                for s in range(2):
                    value = total[:, s * TILE:(s + 1) * TILE]
                    if adds:
                        each = len(picked) // adds
                        more[0][i, u, fine + s] = partials[i // each][i % each, u, fine + s] + value
                    else:
                        out_ref[i, u, fine + s] = value
            if adds:
                done = (i, slice(None), pl.ds(fine, 2))
                copy = pltpu.make_async_copy(more[0].at[done], out_ref.at[done], more[1])
                copy.start(priority=j % 2)
                copies.append(copy)
    for copy in copies:
        copy.wait()


def correlate(parts, groups, where, picked, hours, partials=()):
    places = [part[0] for part in parts]
    pieces = [piece for part in parts for piece in part[1:]]
    _, rows, lanes = pieces[0].shape
    fine = len(FINE)
    shape = (len(picked), len(COARSE), fine, TILE, TILE)
    norm = 1.0 / math.sqrt(F * hours)
    slots = min(len(picked), 2)
    chans = CORES * sum(map(len, places)) * rows
    scratch = 2 * (groups * chans * lanes + slots * (len(COARSE) + fine) * TILE * groups * lanes)
    adds = len(partials)
    more = []
    if adds:
        more = [pltpu.VMEM(shape, jnp.float32), pltpu.SemaphoreType.DMA]
        scratch += 4 * math.prod(shape)
    return pl.pallas_call(
        lambda *refs: correlate_kernel(norm, picked, adds, places, *refs),
        out_shape=jax.ShapeDtypeStruct(shape, jnp.float32),
        in_specs=[VMEM] * (1 + len(pieces) + adds),
        out_specs=pl.BlockSpec(memory_space=pl.ANY) if adds else VMEM,
        scratch_shapes=[
            pltpu.VMEM((groups, chans, lanes), jnp.bfloat16),
            pltpu.VMEM((slots, len(COARSE) * TILE, groups * lanes), jnp.bfloat16),
            pltpu.VMEM((slots, fine * TILE, groups * lanes), jnp.bfloat16),
            *more,
        ],
        compiler_params=pltpu.CompilerParams(vmem_limit_bytes=scratch + SMALL),
        cost_estimate=pl.CostEstimate(flops=0, bytes_accessed=0, transcendentals=0),
        name="correlate_add" if adds else "correlate",
    )(where, *pieces, *partials)


def swap(array, axis, k):
    return lax.ppermute(array, axis, [(i, i ^ k) for i in range(lax.axis_size(axis))])


def stack_kernel(blocks, *refs):
    out_ref = refs[-1]
    first = 0
    for block in refs[:blocks]:
        out_ref[first:first + block.shape[0]] = block[...]
        first += block.shape[0]


def stack(blocks, after=(), flops=0):
    depth = sum(block.shape[0] for block in blocks)
    return pl.pallas_call(
        lambda *refs: stack_kernel(len(blocks), *refs),
        out_shape=jax.ShapeDtypeStruct((depth, *blocks[0].shape[1:]), blocks[0].dtype),
        in_specs=[VMEM] * len(blocks) + [pl.BlockSpec(memory_space=pl.ANY)] * len(after),
        out_specs=VMEM,
        compiler_params=pltpu.CompilerParams(vmem_limit_bytes=SMALL),
        cost_estimate=pl.CostEstimate(flops=flops, bytes_accessed=0, transcendentals=0),
        name="stack",
    )(*blocks, *after)


def halves(white, where):
    groups = lax.axis_size("tm")
    blocks = [white[None]] + [swap(white[None], "tm", k) for k in range(1, groups)]
    return stack(blocks[:groups // 2], after=(where,)), stack(blocks[groups // 2:], flops=10**9)


def between_chips(half, parts):
    chips = lax.axis_size("chan") // CORES
    places = [0, *range(chips - 1, 0, -1)]
    blocks = [swap(half, "chan", CORES * k) if k else half for k in places]
    each = chips // parts
    return [(places[i:i + each], blocks[i:i + each]) for i in range(0, chips, each)]


def between_cores(parts):
    collected = [(places, stack(blocks)) for places, blocks in parts]
    return [(places, own, swap(own, "chan", 1)) for places, own in collected]


def per_device(spectra, bad_channels, tile_list):
    groups = lax.axis_size("tm")
    hours = spectra.shape[1] * groups
    tiles = tile_list.shape[0] // groups
    white = whiten(spectra, bad_channels)
    pairs = lax.dynamic_slice_in_dim(tile_list, lax.axis_index("tm") * tiles, tiles, axis=0)
    where = jnp.concatenate([lax.axis_index("chan").reshape(1), pairs.reshape(-1)]).astype(jnp.int32).reshape(1, -1)
    near, far = halves(white, where)
    near, far = between_cores(between_chips(near, 2)), between_cores(between_chips(far, 2))
    partial = correlate(near, groups // 2, where, range(tiles), hours)
    out = correlate(far, groups // 2, where, range(tiles), hours, [partial])
    return out.reshape(tiles, LAGS, TILE, TILE)


def solution(mesh):
    placed = (P(None, "tm", None, "chan"), P("chan"), P("chan", None))
    return jax.shard_map(
        per_device,
        mesh=mesh,
        in_specs=placed,
        out_specs=P(("chan", "tm"), None, None, None),
        check_vma=False,
    )
```

```python
import math

import jax
import jax.numpy as jnp
from jax import lax
from jax.experimental import pallas as pl
from jax.experimental.pallas import tpu as pltpu
from jax.sharding import PartitionSpec as P

F = 64
LAGS = 32
TILE = 128
EPSILON = 1e-06
CORES = 2
SMALL = 4 * 1024 * 1024
VMEM = pl.BlockSpec(memory_space=pltpu.VMEM)
COARSE = (-12, -4, 4, 12)
FINE = (-4, -3, -2, -1, 0, 1, 2, 3)
LEFT_ORDER = (-4, 4, -12, 12)
STEPS = (0, -2, 2, -4)


def whiten_kernel(spectra_hbm, bad_hbm, out_ref, spectra_ref, bad_ref, sems):
    copies = [
        pltpu.make_async_copy(spectra_hbm, spectra_ref, sems.at[0]),
        pltpu.make_async_copy(bad_hbm, bad_ref, sems.at[1]),
    ]
    for copy in copies:
        copy.start()
    bins, hours, _, chans = spectra_ref.shape
    rows = bins * hours * 2
    row = lax.broadcasted_iota(jnp.int32, (rows, chans), 0)
    hour = (row // 2) % hours
    src = lax.broadcasted_iota(jnp.int32, (rows, rows), 0)
    dst = lax.broadcasted_iota(jnp.int32, (rows, rows), 1)
    move = jnp.where((src % 2) * (rows // 2) + src // 2 == dst, 1.0, 0.0).astype(jnp.bfloat16)
    for copy in copies:
        copy.wait()
    values = spectra_ref[...].reshape(rows, chans).astype(jnp.float32)
    keep = (1 - bad_ref[...]).astype(jnp.float32)
    squares = values * values
    scale = jnp.zeros((rows, chans), jnp.float32)
    for h in range(hours):
        power = jnp.sum(jnp.where(hour == h, squares, 0.0), axis=0, keepdims=True) * (1.0 / (2 * bins))
        scale = jnp.where(hour == h, lax.rsqrt(power + EPSILON) * keep, scale)
    white = (values * scale).astype(jnp.bfloat16)
    out_ref[...] = lax.dot_general(
        white, move, (((0,), (0,)), ((), ())), preferred_element_type=jnp.float32
    ).astype(jnp.bfloat16)


def whiten(spectra, bad_channels):
    bins, hours, _, chans = spectra.shape
    spectra = pltpu.with_memory_space_constraint(spectra, pltpu.HBM)
    bad_channels = pltpu.with_memory_space_constraint(bad_channels.reshape(1, chans), pltpu.HBM)
    return pl.pallas_call(
        whiten_kernel,
        out_shape=jax.ShapeDtypeStruct((chans, bins * hours * 2), jnp.bfloat16),
        in_specs=[pl.BlockSpec(memory_space=pltpu.HBM)] * 2,
        out_specs=VMEM,
        scratch_shapes=[
            pltpu.VMEM(spectra.shape, spectra.dtype),
            pltpu.VMEM((1, chans), bad_channels.dtype),
            pltpu.SemaphoreType.DMA((2,)),
        ],
        compiler_params=pltpu.CompilerParams(vmem_limit_bytes=SMALL),
        name="whiten",
    )(spectra, bad_channels)


def cos_sin(turn):
    quarter = F // 2
    shifted = turn + quarter // 2
    x = (shifted % quarter - quarter // 2).astype(jnp.float32) * (math.pi / F)
    y = x * x
    cos = 1 - y * (1 / 2 - y * (1 / 24 - y * (1 / 720 - y * (1 / 40320 - y / 3628800))))
    sin = x * (1 - y * (1 / 6 - y * (1 / 120 - y * (1 / 5040 - y / 362880))))
    quadrant = shifted // quarter % 4
    odd = quadrant % 2 == 1
    cos, sin = jnp.where(odd, sin, cos), jnp.where(odd, cos, sin)
    return jnp.where((quadrant == 1) | (quadrant == 2), -cos, cos), jnp.where(quadrant >= 2, -sin, sin)


def turn_by(re, im, cos, sin, both):
    rc, rs, ic, is_ = re * cos, re * sin, im * cos, im * sin
    forward = (rc - is_, rs + ic)
    return (forward, (rc + is_, ic - rs)) if both else (forward,)


def correlate_kernel(norm, picked, adds, places, where_ref, *refs):
    parts, refs = refs[:2 * len(places)], refs[2 * len(places):]
    partials = refs[:adds]
    out_ref = refs[adds]
    spectra, left_turned, right_turned, *more = refs[adds + 1:]
    groups, _, lanes = spectra.shape
    half = lanes // 2
    hours_dev = half // F
    bin_number = lax.broadcasted_iota(jnp.int32, (8, half), 1) // hours_dev + 1
    step = lax.broadcasted_iota(jnp.int32, (8, half), 0)
    cos, sin = cos_sin(jnp.where(step == 6, 12, step) * bin_number)
    table = {k: (cos[i:i + 1], sin[i:i + 1]) for k, i in ((4, 4), (12, 6))}
    bin_number = lax.broadcasted_iota(jnp.int32, (half, 8), 0) // hours_dev + 1
    cos, sin = cos_sin(lax.broadcasted_iota(jnp.int32, (half, 8), 1) * bin_number)
    columns = {
        k: tuple(jnp.broadcast_to(part[:, k:k + 1], (half, TILE)) for part in (cos, sin)) for k in range(1, len(STEPS) + 1)
    }

    chan = where_ref[0, 0]
    for i, piece in enumerate(parts):
        rows = piece.shape[1]
        for slot, k in enumerate(places[i // 2]):
            place = pl.multiple_of((chan ^ (CORES * k + i % 2)) * rows, 32)
            spectra[:, pl.ds(place, rows), :] = piece[slot * groups:(slot + 1) * groups]

    def load(block, g):
        whole = spectra[g, pl.ds(pl.multiple_of(block * TILE, TILE), TILE), :].astype(jnp.float32)
        return whole[:, :half], whole[:, half:]

    def turn_left(slot, block, k):
        turns = [turn_by(*load(block, g), *(norm * part for part in table[k]), True) for g in range(groups)]
        for g, turn in enumerate(turns):
            for lag, value in zip((k, -k), turn):
                rows_at = pl.ds(LEFT_ORDER.index(lag) * TILE, TILE)
                for part in range(2):
                    at = g * lanes + part * half
                    left_turned[slot, rows_at, at:at + half] = value[part].astype(jnp.bfloat16)

    def turn_right(slot, block, k):
        for g in range(groups):
            at = [pl.ds(g * lanes + part * half, half) for part in range(2)]
            plain = pl.ds(FINE.index(0) * TILE, TILE)
            if k == 1:
                for part, value in enumerate(load(block, g)):
                    right_turned[slot, at[part], plain] = value.T.astype(jnp.bfloat16)
            re, im = (right_turned[slot, rows_at, plain].astype(jnp.float32) for rows_at in at)
            for lag, value in zip((-k, k), turn_by(re, im, *columns[k], k in FINE)):
                for part in range(2):
                    column = pl.ds(FINE.index(lag) * TILE, TILE)
                    right_turned[slot, at[part], column] = value[part].astype(jnp.bfloat16)

    copies = []
    for i, t in enumerate(picked):
        slot = i % left_turned.shape[0]
        left_block, right_block = where_ref[0, 1 + 2 * t], where_ref[0, 2 + 2 * t]
        for j, lag in enumerate(STEPS):
            fine = FINE.index(lag)
            turn_right(slot, right_block, j + 1)
            for first in range(0, len(COARSE), 2):
                if j == 0:
                    turn_left(slot, left_block, LEFT_ORDER[first + 1])
                total = lax.dot_general(
                    left_turned[slot, first * TILE:(first + 2) * TILE, :],
                    right_turned[slot, :, fine * TILE:(fine + 2) * TILE],
                    (((1,), (0,)), ((), ())),
                    preferred_element_type=jnp.float32,
                )
                for v, s in ((0, 0), (0, 1), (1, 0), (1, 1)):
                    u = COARSE.index(LEFT_ORDER[first + v])
                    value = total[v * TILE:(v + 1) * TILE, s * TILE:(s + 1) * TILE]
                    if adds:
                        each = len(picked) // adds
                        more[0][i, u, fine + s] = partials[i // each][i % each, u, fine + s] + value
                    else:
                        out_ref[i, u, fine + s] = value
            if adds:
                done = (i, slice(None), pl.ds(fine, 2))
                copy = pltpu.make_async_copy(more[0].at[done], out_ref.at[done], more[1])
                copy.start(priority=j % 2)
                copies.append(copy)
    for copy in copies:
        copy.wait()


def correlate(parts, groups, where, picked, hours, partials=()):
    places = [part[0] for part in parts]
    pieces = [piece for part in parts for piece in part[1:]]
    _, rows, lanes = pieces[0].shape
    fine = len(FINE)
    shape = (len(picked), len(COARSE), fine, TILE, TILE)
    norm = 1.0 / math.sqrt(F * hours)
    slots = min(len(picked), 2)
    chans = CORES * sum(map(len, places)) * rows
    scratch = 2 * (groups * chans * lanes + slots * (len(COARSE) + fine) * TILE * groups * lanes)
    adds = len(partials)
    more = []
    if adds:
        more = [pltpu.VMEM(shape, jnp.float32), pltpu.SemaphoreType.DMA]
        scratch += 4 * math.prod(shape)
    return pl.pallas_call(
        lambda *refs: correlate_kernel(norm, picked, adds, places, *refs),
        out_shape=jax.ShapeDtypeStruct(shape, jnp.float32),
        in_specs=[VMEM] * (1 + len(pieces) + adds),
        out_specs=pl.BlockSpec(memory_space=pl.ANY) if adds else VMEM,
        scratch_shapes=[
            pltpu.VMEM((groups, chans, lanes), jnp.bfloat16),
            pltpu.VMEM((slots, len(COARSE) * TILE, groups * lanes), jnp.bfloat16),
            pltpu.VMEM((slots, groups * lanes, fine * TILE), jnp.bfloat16),
            *more,
        ],
        compiler_params=pltpu.CompilerParams(vmem_limit_bytes=scratch + SMALL),
        cost_estimate=pl.CostEstimate(flops=0, bytes_accessed=0, transcendentals=0),
        name="correlate_add" if adds else "correlate",
    )(where, *pieces, *partials)


def swap(array, axis, k):
    return lax.ppermute(array, axis, [(i, i ^ k) for i in range(lax.axis_size(axis))])


def stack_kernel(blocks, *refs):
    out_ref = refs[-1]
    first = 0
    for block in refs[:blocks]:
        out_ref[first:first + block.shape[0]] = block[...]
        first += block.shape[0]


def stack(blocks, after=(), flops=0):
    depth = sum(block.shape[0] for block in blocks)
    return pl.pallas_call(
        lambda *refs: stack_kernel(len(blocks), *refs),
        out_shape=jax.ShapeDtypeStruct((depth, *blocks[0].shape[1:]), blocks[0].dtype),
        in_specs=[VMEM] * len(blocks) + [pl.BlockSpec(memory_space=pl.ANY)] * len(after),
        out_specs=VMEM,
        compiler_params=pltpu.CompilerParams(vmem_limit_bytes=SMALL),
        cost_estimate=pl.CostEstimate(flops=flops, bytes_accessed=0, transcendentals=0),
        name="stack",
    )(*blocks, *after)


def halves(white, where):
    groups = lax.axis_size("tm")
    blocks = [white[None]] + [swap(white[None], "tm", k) for k in range(1, groups)]
    return stack(blocks[:groups // 2], after=(where,)), stack(blocks[groups // 2:], flops=10**9)


def between_chips(half, parts):
    chips = lax.axis_size("chan") // CORES
    places = [0, *range(chips - 1, 0, -1)]
    blocks = [swap(half, "chan", CORES * k) if k else half for k in places]
    each = chips // parts
    return [(places[i:i + each], blocks[i:i + each]) for i in range(0, chips, each)]


def between_cores(parts):
    collected = [(places, stack(blocks)) for places, blocks in parts]
    return [(places, own, swap(own, "chan", 1)) for places, own in collected]


def per_device(spectra, bad_channels, tile_list):
    groups = lax.axis_size("tm")
    hours = spectra.shape[1] * groups
    tiles = tile_list.shape[0] // groups
    white = whiten(spectra, bad_channels)
    pairs = lax.dynamic_slice_in_dim(tile_list, lax.axis_index("tm") * tiles, tiles, axis=0)
    where = jnp.concatenate([lax.axis_index("chan").reshape(1), pairs.reshape(-1)]).astype(jnp.int32).reshape(1, -1)
    near, far = halves(white, where)
    near, far = between_cores(between_chips(near, 2)), between_cores(between_chips(far, 2))
    partial = correlate(near, groups // 2, where, range(tiles), hours)
    out = correlate(far, groups // 2, where, range(tiles), hours, [partial])
    return out.reshape(tiles, LAGS, TILE, TILE)


def solution(mesh):
    placed = (P(None, "tm", None, "chan"), P("chan"), P("chan", None))
    return jax.shard_map(
        per_device,
        mesh=mesh,
        in_specs=placed,
        out_specs=P(("chan", "tm"), None, None, None),
        check_vma=False,
    )
```

```python
import math

import jax
import jax.numpy as jnp
from jax import lax
from jax.experimental import pallas as pl
from jax.experimental.pallas import tpu as pltpu
from jax.sharding import PartitionSpec as P

F = 64
LAGS = 32
TILE = 128
EPSILON = 1e-06
CORES = 2
SMALL = 4 * 1024 * 1024
VMEM = pl.BlockSpec(memory_space=pltpu.VMEM)
COARSE = (-12, -4, 4, 12)
FINE = (-4, -3, -2, -1, 0, 1, 2, 3)
LEFT_ORDER = (-4, 4, -12, 12)
STEPS = (0, -2, 2, -4)


def whiten_kernel(spectra_hbm, bad_hbm, out_ref, spectra_ref, bad_ref, sems):
    copies = [
        pltpu.make_async_copy(spectra_hbm, spectra_ref, sems.at[0]),
        pltpu.make_async_copy(bad_hbm, bad_ref, sems.at[1]),
    ]
    for copy in copies:
        copy.start()
    rows, chans = spectra_ref.shape
    bins = F
    hours = rows // (2 * bins)
    row = lax.broadcasted_iota(jnp.int32, (rows, chans), 0)
    hour = (row // 2) % hours
    src = lax.broadcasted_iota(jnp.int32, (rows, rows), 0)
    dst = lax.broadcasted_iota(jnp.int32, (rows, rows), 1)
    move = jnp.where((src % 2) * (rows // 2) + src // 2 == dst, 1.0, 0.0).astype(jnp.bfloat16)
    for copy in copies:
        copy.wait()
    values = spectra_ref[...].astype(jnp.float32)
    keep = (1 - bad_ref[...]).astype(jnp.float32)
    squares = values * values
    scale = jnp.zeros((rows, chans), jnp.float32)
    for h in range(hours):
        power = jnp.sum(jnp.where(hour == h, squares, 0.0), axis=0, keepdims=True) * (1.0 / (2 * bins))
        scale = jnp.where(hour == h, lax.rsqrt(power + EPSILON) * keep, scale)
    white = (values * scale).astype(jnp.bfloat16)
    out_ref[...] = lax.dot_general(
        white, move, (((0,), (0,)), ((), ())), preferred_element_type=jnp.float32
    ).astype(jnp.bfloat16)


def whiten(spectra, bad_channels):
    chans = spectra.shape[-1]
    spectra = spectra.reshape(-1, chans)
    spectra = pltpu.with_memory_space_constraint(spectra, pltpu.HBM)
    bad_channels = pltpu.with_memory_space_constraint(bad_channels.reshape(1, chans), pltpu.HBM)
    return pl.pallas_call(
        whiten_kernel,
        out_shape=jax.ShapeDtypeStruct((chans, spectra.shape[0]), jnp.bfloat16),
        in_specs=[pl.BlockSpec(memory_space=pltpu.HBM)] * 2,
        out_specs=VMEM,
        scratch_shapes=[
            pltpu.VMEM(spectra.shape, spectra.dtype),
            pltpu.VMEM((1, chans), bad_channels.dtype),
            pltpu.SemaphoreType.DMA((2,)),
        ],
        compiler_params=pltpu.CompilerParams(vmem_limit_bytes=SMALL),
        name="whiten",
    )(spectra, bad_channels)


def cos_sin(turn):
    quarter = F // 2
    shifted = turn + quarter // 2
    x = (shifted % quarter - quarter // 2).astype(jnp.float32) * (math.pi / F)
    y = x * x
    cos = 1 - y * (1 / 2 - y * (1 / 24 - y * (1 / 720 - y * (1 / 40320 - y / 3628800))))
    sin = x * (1 - y * (1 / 6 - y * (1 / 120 - y * (1 / 5040 - y / 362880))))
    quadrant = shifted // quarter % 4
    odd = quadrant % 2 == 1
    cos, sin = jnp.where(odd, sin, cos), jnp.where(odd, cos, sin)
    return jnp.where((quadrant == 1) | (quadrant == 2), -cos, cos), jnp.where(quadrant >= 2, -sin, sin)


def turn_by(re, im, cos, sin, both):
    rc, rs, ic, is_ = re * cos, re * sin, im * cos, im * sin
    forward = (rc - is_, rs + ic)
    return (forward, (rc + is_, ic - rs)) if both else (forward,)


def correlate_kernel(norm, picked, adds, places, where_ref, *refs):
    parts, refs = refs[:2 * len(places)], refs[2 * len(places):]
    partials = refs[:adds]
    out_ref = refs[adds]
    spectra, left_turned, right_turned, *more = refs[adds + 1:]
    groups, _, lanes = spectra.shape
    half = lanes // 2
    hours_dev = half // F
    bin_number = lax.broadcasted_iota(jnp.int32, (8, half), 1) // hours_dev + 1
    step = lax.broadcasted_iota(jnp.int32, (8, half), 0)
    cos, sin = cos_sin(jnp.where(step == 6, 12, step) * bin_number)
    table = {k: (cos[i:i + 1], sin[i:i + 1]) for k, i in ((1, 1), (2, 2), (3, 3), (4, 4), (12, 6))}

    chan = where_ref[0, 0]
    for i, piece in enumerate(parts):
        rows = piece.shape[1]
        for slot, k in enumerate(places[i // 2]):
            place = pl.multiple_of((chan ^ (CORES * k + i % 2)) * rows, 32)
            spectra[:, pl.ds(place, rows), :] = piece[slot * groups:(slot + 1) * groups]

    def load(block, g):
        whole = spectra[g, pl.ds(pl.multiple_of(block * TILE, TILE), TILE), :].astype(jnp.float32)
        return whole[:, :half], whole[:, half:]

    def store(ref, slot, index, g, value):
        rows_at = pl.ds(index * TILE, TILE)
        ref[slot, rows_at, g * lanes:g * lanes + half] = value[0].astype(jnp.bfloat16)
        ref[slot, rows_at, g * lanes + half:(g + 1) * lanes] = value[1].astype(jnp.bfloat16)

    def turn_left(slot, block, k):
        for g in range(groups):
            forward, backward = turn_by(*load(block, g), *(norm * part for part in table[k]), True)
            store(left_turned, slot, LEFT_ORDER.index(k), g, forward)
            store(left_turned, slot, LEFT_ORDER.index(-k), g, backward)

    def turn_right(slot, block, k):
        for g in range(groups):
            re, im = load(block, g)
            if k == 1:
                store(right_turned, slot, FINE.index(0), g, (re, im))
            turns = turn_by(re, im, *table[k], k in FINE)
            for lag, value in zip((-k, k), turns):
                store(right_turned, slot, FINE.index(lag), g, value)

    copies = []
    for i, t in enumerate(picked):
        slot = i % left_turned.shape[0]
        left_block, right_block = where_ref[0, 1 + 2 * t], where_ref[0, 2 + 2 * t]
        for j, lag in enumerate(STEPS):
            fine = FINE.index(lag)
            turn_right(slot, right_block, j + 1)
            for first in range(0, len(COARSE), 2):
                if j == 0:
                    turn_left(slot, left_block, LEFT_ORDER[first + 1])
                total = lax.dot_general(
                    left_turned[slot, first * TILE:(first + 2) * TILE, :],
                    right_turned[slot, fine * TILE:(fine + 2) * TILE, :],
                    (((1,), (1,)), ((), ())),
                    preferred_element_type=jnp.float32,
                )
                for v, s in ((0, 0), (0, 1), (1, 0), (1, 1)):
                    u = COARSE.index(LEFT_ORDER[first + v])
                    value = total[v * TILE:(v + 1) * TILE, s * TILE:(s + 1) * TILE]
                    if adds:
                        each = len(picked) // adds
                        more[0][i, u, fine + s] = partials[i // each][i % each, u, fine + s] + value
                    else:
                        out_ref[i, u, fine + s] = value
            if adds:
                done = (i, slice(None), pl.ds(fine, 2))
                copy = pltpu.make_async_copy(more[0].at[done], out_ref.at[done], more[1])
                copy.start(priority=j % 2)
                copies.append(copy)
    for copy in copies:
        copy.wait()


def correlate(parts, groups, where, picked, hours, partials=()):
    places = [part[0] for part in parts]
    pieces = [piece for part in parts for piece in part[1:]]
    _, rows, lanes = pieces[0].shape
    fine = len(FINE)
    shape = (len(picked), len(COARSE), fine, TILE, TILE)
    norm = 1.0 / math.sqrt(F * hours)
    slots = min(len(picked), 2)
    chans = CORES * sum(map(len, places)) * rows
    scratch = 2 * (groups * chans * lanes + slots * (len(COARSE) + fine) * TILE * groups * lanes)
    adds = len(partials)
    more = []
    if adds:
        more = [pltpu.VMEM(shape, jnp.float32), pltpu.SemaphoreType.DMA]
        scratch += 4 * math.prod(shape)
    return pl.pallas_call(
        lambda *refs: correlate_kernel(norm, picked, adds, places, *refs),
        out_shape=jax.ShapeDtypeStruct(shape, jnp.float32),
        in_specs=[VMEM] * (1 + len(pieces) + adds),
        out_specs=pl.BlockSpec(memory_space=pl.ANY) if adds else VMEM,
        scratch_shapes=[
            pltpu.VMEM((groups, chans, lanes), jnp.bfloat16),
            pltpu.VMEM((slots, len(COARSE) * TILE, groups * lanes), jnp.bfloat16),
            pltpu.VMEM((slots, fine * TILE, groups * lanes), jnp.bfloat16),
            *more,
        ],
        compiler_params=pltpu.CompilerParams(vmem_limit_bytes=scratch + SMALL),
        cost_estimate=pl.CostEstimate(flops=0, bytes_accessed=0, transcendentals=0),
        name="correlate_add" if adds else "correlate",
    )(where, *pieces, *partials)


def swap(array, axis, k):
    return lax.ppermute(array, axis, [(i, i ^ k) for i in range(lax.axis_size(axis))])


def stack_kernel(blocks, *refs):
    out_ref = refs[-1]
    first = 0
    for block in refs[:blocks]:
        out_ref[first:first + block.shape[0]] = block[...]
        first += block.shape[0]


def stack(blocks, after=(), flops=0):
    depth = sum(block.shape[0] for block in blocks)
    return pl.pallas_call(
        lambda *refs: stack_kernel(len(blocks), *refs),
        out_shape=jax.ShapeDtypeStruct((depth, *blocks[0].shape[1:]), blocks[0].dtype),
        in_specs=[VMEM] * len(blocks) + [pl.BlockSpec(memory_space=pl.ANY)] * len(after),
        out_specs=VMEM,
        compiler_params=pltpu.CompilerParams(vmem_limit_bytes=SMALL),
        cost_estimate=pl.CostEstimate(flops=flops, bytes_accessed=0, transcendentals=0),
        name="stack",
    )(*blocks, *after)


def halves(white, where):
    groups = lax.axis_size("tm")
    blocks = [white[None]] + [swap(white[None], "tm", k) for k in range(1, groups)]
    return stack(blocks[:groups // 2], after=(where,)), stack(blocks[groups // 2:], flops=10**9)


def between_chips(half, parts):
    chips = lax.axis_size("chan") // CORES
    places = [0, *range(chips - 1, 0, -1)]
    blocks = [swap(half, "chan", CORES * k) if k else half for k in places]
    each = chips // parts
    return [(places[i:i + each], blocks[i:i + each]) for i in range(0, chips, each)]


def between_cores(parts):
    collected = [(places, stack(blocks)) for places, blocks in parts]
    return [(places, own, swap(own, "chan", 1)) for places, own in collected]


def per_device(spectra, bad_channels, tile_list):
    groups = lax.axis_size("tm")
    hours = spectra.shape[1] * groups
    tiles = tile_list.shape[0] // groups
    white = whiten(spectra, bad_channels)
    pairs = lax.dynamic_slice_in_dim(tile_list, lax.axis_index("tm") * tiles, tiles, axis=0)
    where = jnp.concatenate([lax.axis_index("chan").reshape(1), pairs.reshape(-1)]).astype(jnp.int32).reshape(1, -1)
    near, far = halves(white, where)
    near, far = between_cores(between_chips(near, 2)), between_cores(between_chips(far, 2))
    partial = correlate(near, groups // 2, where, range(tiles), hours)
    out = correlate(far, groups // 2, where, range(tiles), hours, [partial])
    return out.reshape(tiles, LAGS, TILE, TILE)


def solution(mesh):
    placed = (P(None, "tm", None, "chan"), P("chan"), P("chan", None))
    return jax.shard_map(
        per_device,
        mesh=mesh,
        in_specs=placed,
        out_specs=P(("chan", "tm"), None, None, None),
        check_vma=False,
    )
```

```python
import math

import jax
import jax.numpy as jnp
from jax import lax
from jax.experimental import pallas as pl
from jax.experimental.pallas import tpu as pltpu
from jax.sharding import PartitionSpec as P

F = 64
LAGS = 32
TILE = 128
EPSILON = 1e-06
CORES = 2
SMALL = 4 * 1024 * 1024
VMEM = pl.BlockSpec(memory_space=pltpu.VMEM)
COARSE = (-12, -4, 4, 12)
FINE_PAIRS = ((-4, 0), (-1, 1), (-2, 2), (-3, 3))


def whiten_kernel(spectra_hbm, bad_hbm, out_ref, spectra_ref, bad_ref, sems):
    copies = [
        pltpu.make_async_copy(spectra_hbm, spectra_ref, sems.at[0]),
        pltpu.make_async_copy(bad_hbm, bad_ref, sems.at[1]),
    ]
    for copy in copies:
        copy.start()
    rows, chans = spectra_ref.shape
    bins = F
    hours = rows // (2 * bins)
    row = lax.broadcasted_iota(jnp.int32, (rows, chans), 0)
    hour = (row // 2) % hours
    src = lax.broadcasted_iota(jnp.int32, (rows, rows), 0)
    dst = lax.broadcasted_iota(jnp.int32, (rows, rows), 1)
    move = jnp.where((src % 2) * (rows // 2) + src // 2 == dst, 1.0, 0.0).astype(jnp.bfloat16)
    for copy in copies:
        copy.wait()
    values = spectra_ref[...].astype(jnp.float32)
    keep = (1 - bad_ref[...]).astype(jnp.float32)
    squares = values * values
    scale = jnp.zeros((rows, chans), jnp.float32)
    for h in range(hours):
        power = jnp.sum(jnp.where(hour == h, squares, 0.0), axis=0, keepdims=True) * (1.0 / (2 * bins))
        scale = jnp.where(hour == h, lax.rsqrt(power + EPSILON) * keep, scale)
    white = (values * scale).astype(jnp.bfloat16)
    out_ref[...] = lax.dot_general(
        white, move, (((0,), (0,)), ((), ())), preferred_element_type=jnp.float32
    ).astype(jnp.bfloat16)


def whiten(spectra, bad_channels):
    chans = spectra.shape[-1]
    spectra = spectra.reshape(-1, chans)
    spectra = pltpu.with_memory_space_constraint(spectra, pltpu.HBM)
    bad_channels = pltpu.with_memory_space_constraint(bad_channels.reshape(1, chans), pltpu.HBM)
    return pl.pallas_call(
        whiten_kernel,
        out_shape=jax.ShapeDtypeStruct((chans, spectra.shape[0]), jnp.bfloat16),
        in_specs=[pl.BlockSpec(memory_space=pltpu.HBM)] * 2,
        out_specs=VMEM,
        scratch_shapes=[
            pltpu.VMEM(spectra.shape, spectra.dtype),
            pltpu.VMEM((1, chans), bad_channels.dtype),
            pltpu.SemaphoreType.DMA((2,)),
        ],
        compiler_params=pltpu.CompilerParams(vmem_limit_bytes=SMALL),
        name="whiten",
    )(spectra, bad_channels)


def cos_sin(turn):
    quarter = F // 2
    shifted = turn + quarter // 2
    x = (shifted % quarter - quarter // 2).astype(jnp.float32) * (math.pi / F)
    y = x * x
    cos = 1 - y * (1 / 2 - y * (1 / 24 - y * (1 / 720 - y * (1 / 40320 - y / 3628800))))
    sin = x * (1 - y * (1 / 6 - y * (1 / 120 - y * (1 / 5040 - y / 362880))))
    quadrant = shifted // quarter % 4
    odd = quadrant % 2 == 1
    cos, sin = jnp.where(odd, sin, cos), jnp.where(odd, cos, sin)
    return jnp.where((quadrant == 1) | (quadrant == 2), -cos, cos), jnp.where(quadrant >= 2, -sin, sin)


def turn_by(re, im, cos, sin, both):
    rc, rs, ic, is_ = re * cos, re * sin, im * cos, im * sin
    forward = (rc - is_, rs + ic)
    return (forward, (rc + is_, ic - rs)) if both else (forward,)


def correlate_kernel(norm, picked, adds, places, where_ref, *refs):
    parts, refs = refs[:2 * len(places)], refs[2 * len(places):]
    partials = refs[:adds]
    out_ref = refs[adds]
    spectra, left_turned, right_turned, *more = refs[adds + 1:]
    groups, _, lanes = spectra.shape
    half = lanes // 2
    hours_dev = half // F
    bin_number = lax.broadcasted_iota(jnp.int32, (8, half), 1) // hours_dev + 1
    step = lax.broadcasted_iota(jnp.int32, (8, half), 0)
    cos, sin = cos_sin(jnp.where(step == 6, 12, step) * bin_number)
    table = {k: (cos[i:i + 1], sin[i:i + 1]) for k, i in ((1, 1), (2, 2), (3, 3), (4, 4), (12, 6))}

    chan = where_ref[0, 0]
    for i, piece in enumerate(parts):
        rows = piece.shape[1]
        for slot, k in enumerate(places[i // 2]):
            place = pl.multiple_of((chan ^ (CORES * k + i % 2)) * rows, 32)
            spectra[:, pl.ds(place, rows), :] = piece[slot * groups:(slot + 1) * groups]

    def load(block, g):
        whole = spectra[g, pl.ds(pl.multiple_of(block * TILE, TILE), TILE), :].astype(jnp.float32)
        return whole[:, :half], whole[:, half:]

    def store(ref, slot, index, g, value):
        rows_at = pl.ds(index * TILE, TILE)
        ref[slot, rows_at, g * lanes:g * lanes + half] = value[0].astype(jnp.bfloat16)
        ref[slot, rows_at, g * lanes + half:(g + 1) * lanes] = value[1].astype(jnp.bfloat16)

    copies = []
    for i, t in enumerate(picked):
        slot = i % left_turned.shape[0]
        left_block, right_block = where_ref[0, 1 + 2 * t], where_ref[0, 2 + 2 * t]
        for g in range(groups):
            re, im = load(left_block, g)
            for k in (4, 12):
                forward, backward = turn_by(re, im, *(norm * part for part in table[k]), True)
                store(left_turned, slot, COARSE.index(k), g, forward)
                store(left_turned, slot, COARSE.index(-k), g, backward)
        for j in range(len(FINE_PAIRS)):
            for g in range(groups):
                re, im = load(right_block, g)
                if j == 0:
                    store(right_turned, slot, 0, g, turn_by(re, im, *table[4], False)[0])
                    store(right_turned, slot, 1, g, (re, im))
                else:
                    forward, backward = turn_by(re, im, *table[j], True)
                    store(right_turned, slot, 2 * j, g, forward)
                    store(right_turned, slot, 2 * j + 1, g, backward)
            for u in range(0, len(COARSE), 2):
                total = lax.dot_general(
                    left_turned[slot, u * TILE:(u + 2) * TILE, :],
                    right_turned[slot, 2 * j * TILE:2 * (j + 1) * TILE, :],
                    (((1,), (1,)), ((), ())),
                    preferred_element_type=jnp.float32,
                )
                for v, s in ((0, 0), (0, 1), (1, 0), (1, 1)):
                    fine = FINE_PAIRS[j][s] + 4
                    value = total[v * TILE:(v + 1) * TILE, s * TILE:(s + 1) * TILE]
                    if adds:
                        each = len(picked) // adds
                        more[0][i, u + v, fine] = partials[i // each][i % each, u + v, fine] + value
                    else:
                        out_ref[i, u + v, fine] = value
            for s in range(2 if adds else 0):
                done = (i, slice(None), FINE_PAIRS[j][s] + 4)
                copy = pltpu.make_async_copy(more[0].at[done], out_ref.at[done], more[1])
                copy.start(priority=s)
                copies.append(copy)
    for copy in copies:
        copy.wait()


def correlate(parts, groups, where, picked, hours, partials=()):
    places = [part[0] for part in parts]
    pieces = [piece for part in parts for piece in part[1:]]
    _, rows, lanes = pieces[0].shape
    fine = 2 * len(FINE_PAIRS)
    shape = (len(picked), len(COARSE), fine, TILE, TILE)
    norm = 1.0 / math.sqrt(F * hours)
    slots = min(len(picked), 2)
    chans = CORES * sum(map(len, places)) * rows
    scratch = 2 * (groups * chans * lanes + slots * (len(COARSE) + fine) * TILE * groups * lanes)
    adds = len(partials)
    more = []
    if adds:
        more = [pltpu.VMEM(shape, jnp.float32), pltpu.SemaphoreType.DMA]
        scratch += 4 * math.prod(shape)
    return pl.pallas_call(
        lambda *refs: correlate_kernel(norm, picked, adds, places, *refs),
        out_shape=jax.ShapeDtypeStruct(shape, jnp.float32),
        in_specs=[VMEM] * (1 + len(pieces) + adds),
        out_specs=pl.BlockSpec(memory_space=pl.ANY) if adds else VMEM,
        scratch_shapes=[
            pltpu.VMEM((groups, chans, lanes), jnp.bfloat16),
            pltpu.VMEM((slots, len(COARSE) * TILE, groups * lanes), jnp.bfloat16),
            pltpu.VMEM((slots, fine * TILE, groups * lanes), jnp.bfloat16),
            *more,
        ],
        compiler_params=pltpu.CompilerParams(vmem_limit_bytes=scratch + SMALL),
        cost_estimate=pl.CostEstimate(flops=0, bytes_accessed=0, transcendentals=0),
        name="correlate_add" if adds else "correlate",
    )(where, *pieces, *partials)


def swap(array, axis, k):
    return lax.ppermute(array, axis, [(i, i ^ k) for i in range(lax.axis_size(axis))])


def stack_kernel(blocks, *refs):
    out_ref = refs[-1]
    first = 0
    for block in refs[:blocks]:
        out_ref[first:first + block.shape[0]] = block[...]
        first += block.shape[0]


def stack(blocks, after=(), flops=0):
    depth = sum(block.shape[0] for block in blocks)
    return pl.pallas_call(
        lambda *refs: stack_kernel(len(blocks), *refs),
        out_shape=jax.ShapeDtypeStruct((depth, *blocks[0].shape[1:]), blocks[0].dtype),
        in_specs=[VMEM] * len(blocks) + [pl.BlockSpec(memory_space=pl.ANY)] * len(after),
        out_specs=VMEM,
        compiler_params=pltpu.CompilerParams(vmem_limit_bytes=SMALL),
        cost_estimate=pl.CostEstimate(flops=flops, bytes_accessed=0, transcendentals=0),
        name="stack",
    )(*blocks, *after)


def halves(white, where):
    groups = lax.axis_size("tm")
    blocks = [white[None]] + [swap(white[None], "tm", k) for k in range(1, groups)]
    return stack(blocks[:groups // 2]), stack(blocks[groups // 2:], after=(where,), flops=10**9)


def between_chips(half, parts):
    chips = lax.axis_size("chan") // CORES
    places = [0, *range(chips - 1, 0, -1)]
    blocks = [swap(half, "chan", CORES * k) if k else half for k in places]
    each = chips // parts
    return [(places[i:i + each], blocks[i:i + each]) for i in range(0, chips, each)]


def between_cores(parts):
    collected = [(places, stack(blocks)) for places, blocks in parts]
    return [(places, own, swap(own, "chan", 1)) for places, own in collected]


def per_device(spectra, bad_channels, tile_list):
    groups = lax.axis_size("tm")
    hours = spectra.shape[1] * groups
    tiles = tile_list.shape[0] // groups
    white = whiten(spectra, bad_channels)
    pairs = lax.dynamic_slice_in_dim(tile_list, lax.axis_index("tm") * tiles, tiles, axis=0)
    where = jnp.concatenate([lax.axis_index("chan").reshape(1), pairs.reshape(-1)]).astype(jnp.int32).reshape(1, -1)
    near, far = halves(white, where)
    near, far = between_cores(between_chips(near, 2)), between_cores(between_chips(far, 2))
    partial = correlate(near, groups // 2, where, range(tiles), hours)
    out = correlate(far, groups // 2, where, range(tiles), hours, [partial])
    return out.reshape(tiles, LAGS, TILE, TILE)


def solution(mesh):
    placed = (P(None, "tm", None, "chan"), P("chan"), P("chan", None))
    return jax.shard_map(
        per_device,
        mesh=mesh,
        in_specs=placed,
        out_specs=P(("chan", "tm"), None, None, None),
        check_vma=False,
    )
```

```python
import math

import jax
import jax.numpy as jnp
from jax import lax
from jax.experimental import pallas as pl
from jax.experimental.pallas import tpu as pltpu
from jax.sharding import PartitionSpec as P

F = 64
LAGS = 32
TILE = 128
EPSILON = 1e-06
CORES = 2
SMALL = 4 * 1024 * 1024
VMEM = pl.BlockSpec(memory_space=pltpu.VMEM)
COARSE = (-12, -4, 4, 12)
FINE_PAIRS = ((-4, 0), (-1, 1), (-2, 2), (-3, 3))


def whiten_kernel(spectra_hbm, bad_hbm, out_ref, spectra_ref, bad_ref, sems):
    copies = [
        pltpu.make_async_copy(spectra_hbm, spectra_ref, sems.at[0]),
        pltpu.make_async_copy(bad_hbm, bad_ref, sems.at[1]),
    ]
    for copy in copies:
        copy.start()
    rows, chans = spectra_ref.shape
    bins = F
    hours = rows // (2 * bins)
    row = lax.broadcasted_iota(jnp.int32, (rows, chans), 0)
    hour = (row // 2) % hours
    src = lax.broadcasted_iota(jnp.int32, (rows, rows), 0)
    dst = lax.broadcasted_iota(jnp.int32, (rows, rows), 1)
    move = jnp.where((src % 2) * (rows // 2) + src // 2 == dst, 1.0, 0.0).astype(jnp.bfloat16)
    for copy in copies:
        copy.wait()
    values = spectra_ref[...].astype(jnp.float32)
    keep = (1 - bad_ref[...]).astype(jnp.float32)
    squares = values * values
    scale = jnp.zeros((rows, chans), jnp.float32)
    for h in range(hours):
        power = jnp.sum(jnp.where(hour == h, squares, 0.0), axis=0, keepdims=True) * (1.0 / (2 * bins))
        scale = jnp.where(hour == h, lax.rsqrt(power + EPSILON) * keep, scale)
    white = (values * scale).astype(jnp.bfloat16)
    out_ref[...] = lax.dot_general(
        white, move, (((0,), (0,)), ((), ())), preferred_element_type=jnp.float32
    ).astype(jnp.bfloat16)


def whiten(spectra, bad_channels):
    chans = spectra.shape[-1]
    spectra = spectra.reshape(-1, chans)
    spectra = pltpu.with_memory_space_constraint(spectra, pltpu.HBM)
    bad_channels = pltpu.with_memory_space_constraint(bad_channels.reshape(1, chans), pltpu.HBM)
    return pl.pallas_call(
        whiten_kernel,
        out_shape=jax.ShapeDtypeStruct((chans, spectra.shape[0]), jnp.bfloat16),
        in_specs=[pl.BlockSpec(memory_space=pltpu.HBM)] * 2,
        out_specs=VMEM,
        scratch_shapes=[
            pltpu.VMEM(spectra.shape, spectra.dtype),
            pltpu.VMEM((1, chans), bad_channels.dtype),
            pltpu.SemaphoreType.DMA((2,)),
        ],
        compiler_params=pltpu.CompilerParams(vmem_limit_bytes=SMALL),
        name="whiten",
    )(spectra, bad_channels)


def cos_sin(turn):
    quarter = F // 2
    shifted = turn + quarter // 2
    x = (shifted % quarter - quarter // 2).astype(jnp.float32) * (math.pi / F)
    y = x * x
    cos = 1 - y * (1 / 2 - y * (1 / 24 - y * (1 / 720 - y * (1 / 40320 - y / 3628800))))
    sin = x * (1 - y * (1 / 6 - y * (1 / 120 - y * (1 / 5040 - y / 362880))))
    quadrant = shifted // quarter % 4
    odd = quadrant % 2 == 1
    cos, sin = jnp.where(odd, sin, cos), jnp.where(odd, cos, sin)
    return jnp.where((quadrant == 1) | (quadrant == 2), -cos, cos), jnp.where(quadrant >= 2, -sin, sin)


def turn_by(re, im, cos, sin, both):
    rc, rs, ic, is_ = re * cos, re * sin, im * cos, im * sin
    forward = (rc - is_, rs + ic)
    return (forward, (rc + is_, ic - rs)) if both else (forward,)


def correlate_kernel(norm, picked, adds, places, where_ref, *refs):
    parts, refs = refs[:2 * len(places)], refs[2 * len(places):]
    partials = refs[:adds]
    out_ref = refs[adds]
    spectra, left_turned, right_turned, *more = refs[adds + 1:]
    groups, _, lanes = spectra.shape
    half = lanes // 2
    hours_dev = half // F
    bin_number = lax.broadcasted_iota(jnp.int32, (8, half), 1) // hours_dev + 1
    step = lax.broadcasted_iota(jnp.int32, (8, half), 0)
    cos, sin = cos_sin(jnp.where(step == 6, 12, step) * bin_number)
    table = {k: (cos[i:i + 1], sin[i:i + 1]) for k, i in ((1, 1), (2, 2), (3, 3), (4, 4), (12, 6))}

    chan = where_ref[0, 0]
    for i, piece in enumerate(parts):
        rows = piece.shape[1]
        for slot, k in enumerate(places[i // 2]):
            place = pl.multiple_of((chan ^ (CORES * k + i % 2)) * rows, 32)
            spectra[:, pl.ds(place, rows), :] = piece[slot * groups:(slot + 1) * groups]

    def load(block, g):
        whole = spectra[g, pl.ds(pl.multiple_of(block * TILE, TILE), TILE), :].astype(jnp.float32)
        return whole[:, :half], whole[:, half:]

    def store(ref, slot, index, g, value):
        rows_at = pl.ds(index * TILE, TILE)
        ref[slot, rows_at, g * lanes:g * lanes + half] = value[0].astype(jnp.bfloat16)
        ref[slot, rows_at, g * lanes + half:(g + 1) * lanes] = value[1].astype(jnp.bfloat16)

    copies = []
    for i, t in enumerate(picked):
        slot = i % left_turned.shape[0]
        left_block, right_block = where_ref[0, 1 + 2 * t], where_ref[0, 2 + 2 * t]
        for g in range(groups):
            re, im = load(left_block, g)
            for k in (4, 12):
                forward, backward = turn_by(re, im, *(norm * part for part in table[k]), True)
                store(left_turned, slot, COARSE.index(k), g, forward)
                store(left_turned, slot, COARSE.index(-k), g, backward)
        for j in range(0, len(FINE_PAIRS), 2):
            for g in range(groups):
                re, im = load(right_block, g)
                for pair in (j, j + 1):
                    if pair == 0:
                        turns = (turn_by(re, im, *table[4], False)[0], (re, im))
                    else:
                        turns = turn_by(re, im, *table[pair], True)
                    for s in range(2):
                        store(right_turned, slot, 2 * pair + s, g, turns[s])
            for u in range(0, len(COARSE), 2):
                total = lax.dot_general(
                    left_turned[slot, u * TILE:(u + 2) * TILE, :],
                    right_turned[slot, 2 * j * TILE:2 * (j + 2) * TILE, :],
                    (((1,), (1,)), ((), ())),
                    preferred_element_type=jnp.float32,
                )
                for v in range(2):
                    for s in range(4):
                        fine = FINE_PAIRS[j + s // 2][s % 2] + 4
                        value = total[v * TILE:(v + 1) * TILE, s * TILE:(s + 1) * TILE]
                        if adds:
                            each = len(picked) // adds
                            more[0][i, u + v, fine] = partials[i // each][i % each, u + v, fine] + value
                        else:
                            out_ref[i, u + v, fine] = value
            for s in range(4 if adds else 0):
                done = (i, slice(None), FINE_PAIRS[j + s // 2][s % 2] + 4)
                copy = pltpu.make_async_copy(more[0].at[done], out_ref.at[done], more[1])
                copy.start(priority=s % 2)
                copies.append(copy)
    for copy in copies:
        copy.wait()


def correlate(parts, groups, where, picked, hours, partials=()):
    places = [part[0] for part in parts]
    pieces = [piece for part in parts for piece in part[1:]]
    _, rows, lanes = pieces[0].shape
    fine = 2 * len(FINE_PAIRS)
    shape = (len(picked), len(COARSE), fine, TILE, TILE)
    norm = 1.0 / math.sqrt(F * hours)
    slots = min(len(picked), 2)
    chans = CORES * sum(map(len, places)) * rows
    scratch = 2 * (groups * chans * lanes + slots * (len(COARSE) + fine) * TILE * groups * lanes)
    adds = len(partials)
    more = []
    if adds:
        more = [pltpu.VMEM(shape, jnp.float32), pltpu.SemaphoreType.DMA]
        scratch += 4 * math.prod(shape)
    return pl.pallas_call(
        lambda *refs: correlate_kernel(norm, picked, adds, places, *refs),
        out_shape=jax.ShapeDtypeStruct(shape, jnp.float32),
        in_specs=[VMEM] * (1 + len(pieces) + adds),
        out_specs=pl.BlockSpec(memory_space=pl.ANY) if adds else VMEM,
        scratch_shapes=[
            pltpu.VMEM((groups, chans, lanes), jnp.bfloat16),
            pltpu.VMEM((slots, len(COARSE) * TILE, groups * lanes), jnp.bfloat16),
            pltpu.VMEM((slots, fine * TILE, groups * lanes), jnp.bfloat16),
            *more,
        ],
        compiler_params=pltpu.CompilerParams(vmem_limit_bytes=scratch + SMALL),
        cost_estimate=pl.CostEstimate(flops=0, bytes_accessed=0, transcendentals=0),
        name="correlate_add" if adds else "correlate",
    )(where, *pieces, *partials)


def swap(array, axis, k):
    return lax.ppermute(array, axis, [(i, i ^ k) for i in range(lax.axis_size(axis))])


def stack_kernel(blocks, *refs):
    out_ref = refs[-1]
    first = 0
    for block in refs[:blocks]:
        out_ref[first:first + block.shape[0]] = block[...]
        first += block.shape[0]


def stack(blocks, after=(), flops=0):
    depth = sum(block.shape[0] for block in blocks)
    return pl.pallas_call(
        lambda *refs: stack_kernel(len(blocks), *refs),
        out_shape=jax.ShapeDtypeStruct((depth, *blocks[0].shape[1:]), blocks[0].dtype),
        in_specs=[VMEM] * len(blocks) + [pl.BlockSpec(memory_space=pl.ANY)] * len(after),
        out_specs=VMEM,
        compiler_params=pltpu.CompilerParams(vmem_limit_bytes=SMALL),
        cost_estimate=pl.CostEstimate(flops=flops, bytes_accessed=0, transcendentals=0),
        name="stack",
    )(*blocks, *after)


def halves(white, where):
    groups = lax.axis_size("tm")
    blocks = [white[None]] + [swap(white[None], "tm", k) for k in range(1, groups)]
    return stack(blocks[:groups // 2]), stack(blocks[groups // 2:], after=(where,), flops=10**9)


def between_chips(half, parts):
    chips = lax.axis_size("chan") // CORES
    places = [0, *range(chips - 1, 0, -1)]
    blocks = [swap(half, "chan", CORES * k) if k else half for k in places]
    each = chips // parts
    return [(places[i:i + each], blocks[i:i + each]) for i in range(0, chips, each)]


def between_cores(parts):
    collected = [(places, stack(blocks)) for places, blocks in parts]
    return [(places, own, swap(own, "chan", 1)) for places, own in collected]


def per_device(spectra, bad_channels, tile_list):
    groups = lax.axis_size("tm")
    hours = spectra.shape[1] * groups
    tiles = tile_list.shape[0] // groups
    white = whiten(spectra, bad_channels)
    pairs = lax.dynamic_slice_in_dim(tile_list, lax.axis_index("tm") * tiles, tiles, axis=0)
    where = jnp.concatenate([lax.axis_index("chan").reshape(1), pairs.reshape(-1)]).astype(jnp.int32).reshape(1, -1)
    near, far = halves(white, where)
    near, far = between_cores(between_chips(near, 2)), between_cores(between_chips(far, 2))
    partial = correlate(near, groups // 2, where, range(tiles), hours)
    out = correlate(far, groups // 2, where, range(tiles), hours, [partial])
    return out.reshape(tiles, LAGS, TILE, TILE)


def solution(mesh):
    placed = (P(None, "tm", None, "chan"), P("chan"), P("chan", None))
    return jax.shard_map(
        per_device,
        mesh=mesh,
        in_specs=placed,
        out_specs=P(("chan", "tm"), None, None, None),
        check_vma=False,
    )
```

```python
import math

import jax
import jax.numpy as jnp
from jax import lax
from jax.experimental import pallas as pl
from jax.experimental.pallas import tpu as pltpu
from jax.sharding import PartitionSpec as P

F = 64
LAGS = 32
TILE = 128
EPSILON = 1e-06
CORES = 2
SMALL = 4 * 1024 * 1024
VMEM = pl.BlockSpec(memory_space=pltpu.VMEM)
COARSE = (-12, -4, 4, 12)
FINE_PAIRS = ((-4, 0), (-1, 1), (-2, 2), (-3, 3))


def whiten_kernel(spectra_hbm, bad_hbm, out_ref, spectra_ref, bad_ref, sems):
    copies = [
        pltpu.make_async_copy(spectra_hbm, spectra_ref, sems.at[0]),
        pltpu.make_async_copy(bad_hbm, bad_ref, sems.at[1]),
    ]
    for copy in copies:
        copy.start()
    rows, chans = spectra_ref.shape
    bins = F
    hours = rows // (2 * bins)
    row = lax.broadcasted_iota(jnp.int32, (rows, chans), 0)
    hour = (row // 2) % hours
    src = lax.broadcasted_iota(jnp.int32, (rows, rows), 0)
    dst = lax.broadcasted_iota(jnp.int32, (rows, rows), 1)
    move = jnp.where((src % 2) * (rows // 2) + src // 2 == dst, 1.0, 0.0).astype(jnp.bfloat16)
    for copy in copies:
        copy.wait()
    values = spectra_ref[...].astype(jnp.float32)
    keep = (1 - bad_ref[...]).astype(jnp.float32)
    squares = values * values
    scale = jnp.zeros((rows, chans), jnp.float32)
    for h in range(hours):
        power = jnp.sum(jnp.where(hour == h, squares, 0.0), axis=0, keepdims=True) * (1.0 / (2 * bins))
        scale = jnp.where(hour == h, lax.rsqrt(power + EPSILON) * keep, scale)
    white = (values * scale).astype(jnp.bfloat16)
    out_ref[...] = lax.dot_general(
        white, move, (((0,), (0,)), ((), ())), preferred_element_type=jnp.float32
    ).astype(jnp.bfloat16)


def whiten(spectra, bad_channels):
    chans = spectra.shape[-1]
    spectra = spectra.reshape(-1, chans)
    spectra = pltpu.with_memory_space_constraint(spectra, pltpu.HBM)
    bad_channels = pltpu.with_memory_space_constraint(bad_channels.reshape(1, chans), pltpu.HBM)
    return pl.pallas_call(
        whiten_kernel,
        out_shape=jax.ShapeDtypeStruct((chans, spectra.shape[0]), jnp.bfloat16),
        in_specs=[pl.BlockSpec(memory_space=pltpu.HBM)] * 2,
        out_specs=VMEM,
        scratch_shapes=[
            pltpu.VMEM(spectra.shape, spectra.dtype),
            pltpu.VMEM((1, chans), bad_channels.dtype),
            pltpu.SemaphoreType.DMA((2,)),
        ],
        compiler_params=pltpu.CompilerParams(vmem_limit_bytes=SMALL),
        name="whiten",
    )(spectra, bad_channels)


def cos_sin(turn):
    quarter = F // 2
    shifted = turn + quarter // 2
    x = (shifted % quarter - quarter // 2).astype(jnp.float32) * (math.pi / F)
    y = x * x
    cos = 1 - y * (1 / 2 - y * (1 / 24 - y * (1 / 720 - y * (1 / 40320 - y / 3628800))))
    sin = x * (1 - y * (1 / 6 - y * (1 / 120 - y * (1 / 5040 - y / 362880))))
    quadrant = shifted // quarter % 4
    odd = quadrant % 2 == 1
    cos, sin = jnp.where(odd, sin, cos), jnp.where(odd, cos, sin)
    return jnp.where((quadrant == 1) | (quadrant == 2), -cos, cos), jnp.where(quadrant >= 2, -sin, sin)


def turn_by(re, im, cos, sin, both):
    rc, rs, ic, is_ = re * cos, re * sin, im * cos, im * sin
    forward = (rc - is_, rs + ic)
    return (forward, (rc + is_, ic - rs)) if both else (forward,)


def correlate_kernel(norm, picked, adds, places, where_ref, *refs):
    parts, refs = refs[:2 * len(places)], refs[2 * len(places):]
    partials = refs[:adds]
    out_ref = refs[adds]
    spectra, left_turned, right_turned, *more = refs[adds + 1:]
    groups, _, lanes = spectra.shape
    half = lanes // 2
    hours_dev = half // F
    bin_number = lax.broadcasted_iota(jnp.int32, (8, half), 1) // hours_dev + 1
    step = lax.broadcasted_iota(jnp.int32, (8, half), 0)
    cos, sin = cos_sin(jnp.where(step == 6, 12, step) * bin_number)
    table = {k: (cos[i:i + 1], sin[i:i + 1]) for k, i in ((1, 1), (2, 2), (3, 3), (4, 4), (12, 6))}

    chan = where_ref[0, 0]
    for i, piece in enumerate(parts):
        rows = piece.shape[1]
        for slot, k in enumerate(places[i // 2]):
            place = pl.multiple_of((chan ^ (CORES * k + i % 2)) * rows, 32)
            spectra[:, pl.ds(place, rows), :] = piece[slot * groups:(slot + 1) * groups]

    def load(block, g):
        whole = spectra[g, pl.ds(pl.multiple_of(block * TILE, TILE), TILE), :].astype(jnp.float32)
        return whole[:, :half], whole[:, half:]

    def store(ref, slot, index, g, value):
        rows_at = pl.ds(index * TILE, TILE)
        ref[slot, rows_at, g * lanes:g * lanes + half] = value[0].astype(jnp.bfloat16)
        ref[slot, rows_at, g * lanes + half:(g + 1) * lanes] = value[1].astype(jnp.bfloat16)

    def turn_left(i):
        for g in range(groups):
            re, im = load(where_ref[0, 1 + 2 * picked[i]], g)
            for k in (4, 12):
                forward, backward = turn_by(re, im, *(norm * part for part in table[k]), True)
                store(left_turned, i % slots, COARSE.index(k), g, forward)
                store(left_turned, i % slots, COARSE.index(-k), g, backward)

    def turn_right(i, j):
        for g in range(groups):
            re, im = load(where_ref[0, 2 + 2 * picked[i]], g)
            if j == 0:
                turns = (turn_by(re, im, *table[4], False)[0], (re, im))
            else:
                turns = turn_by(re, im, *table[j], True)
            for s in range(2):
                store(right_turned, i % slots, 2 * j + s, g, turns[s])

    slots = left_turned.shape[0]
    copies = []
    steps = [(i, j) for i in range(len(picked)) for j in range(len(FINE_PAIRS))]
    turn_left(0)
    turn_right(0, 0)
    for (i, j), after in zip(steps, steps[1:] + [None]):
        for u in range(0, len(COARSE), 2):
            if u and after:
                if after[1] == 0:
                    turn_left(after[0])
                turn_right(*after)
            total = lax.dot_general(
                left_turned[i % slots, u * TILE:(u + 2) * TILE, :],
                right_turned[i % slots, 2 * j * TILE:2 * (j + 1) * TILE, :],
                (((1,), (1,)), ((), ())),
                preferred_element_type=jnp.float32,
            )
            for v, s in ((0, 0), (0, 1), (1, 0), (1, 1)):
                fine = FINE_PAIRS[j][s] + 4
                value = total[v * TILE:(v + 1) * TILE, s * TILE:(s + 1) * TILE]
                if adds:
                    each = len(picked) // adds
                    more[0][i, u + v, fine] = partials[i // each][i % each, u + v, fine] + value
                else:
                    out_ref[i, u + v, fine] = value
        for s in range(2 if adds else 0):
            done = (i, slice(None), FINE_PAIRS[j][s] + 4)
            copy = pltpu.make_async_copy(more[0].at[done], out_ref.at[done], more[1])
            copy.start(priority=s)
            copies.append(copy)
    for copy in copies:
        copy.wait()


def correlate(parts, groups, where, picked, hours, partials=()):
    places = [part[0] for part in parts]
    pieces = [piece for part in parts for piece in part[1:]]
    _, rows, lanes = pieces[0].shape
    fine = 2 * len(FINE_PAIRS)
    shape = (len(picked), len(COARSE), fine, TILE, TILE)
    norm = 1.0 / math.sqrt(F * hours)
    slots = min(len(picked), 2)
    chans = CORES * sum(map(len, places)) * rows
    scratch = 2 * (groups * chans * lanes + slots * (len(COARSE) + fine) * TILE * groups * lanes)
    adds = len(partials)
    more = []
    if adds:
        more = [pltpu.VMEM(shape, jnp.float32), pltpu.SemaphoreType.DMA]
        scratch += 4 * math.prod(shape)
    return pl.pallas_call(
        lambda *refs: correlate_kernel(norm, picked, adds, places, *refs),
        out_shape=jax.ShapeDtypeStruct(shape, jnp.float32),
        in_specs=[VMEM] * (1 + len(pieces) + adds),
        out_specs=pl.BlockSpec(memory_space=pl.ANY) if adds else VMEM,
        scratch_shapes=[
            pltpu.VMEM((groups, chans, lanes), jnp.bfloat16),
            pltpu.VMEM((slots, len(COARSE) * TILE, groups * lanes), jnp.bfloat16),
            pltpu.VMEM((slots, fine * TILE, groups * lanes), jnp.bfloat16),
            *more,
        ],
        compiler_params=pltpu.CompilerParams(vmem_limit_bytes=scratch + SMALL),
        cost_estimate=pl.CostEstimate(flops=0, bytes_accessed=0, transcendentals=0),
        name="correlate_add" if adds else "correlate",
    )(where, *pieces, *partials)


def swap(array, axis, k):
    return lax.ppermute(array, axis, [(i, i ^ k) for i in range(lax.axis_size(axis))])


def stack_kernel(blocks, *refs):
    out_ref = refs[-1]
    first = 0
    for block in refs[:blocks]:
        out_ref[first:first + block.shape[0]] = block[...]
        first += block.shape[0]


def stack(blocks, after=(), flops=0):
    depth = sum(block.shape[0] for block in blocks)
    return pl.pallas_call(
        lambda *refs: stack_kernel(len(blocks), *refs),
        out_shape=jax.ShapeDtypeStruct((depth, *blocks[0].shape[1:]), blocks[0].dtype),
        in_specs=[VMEM] * len(blocks) + [pl.BlockSpec(memory_space=pl.ANY)] * len(after),
        out_specs=VMEM,
        compiler_params=pltpu.CompilerParams(vmem_limit_bytes=SMALL),
        cost_estimate=pl.CostEstimate(flops=flops, bytes_accessed=0, transcendentals=0),
        name="stack",
    )(*blocks, *after)


def halves(white, where):
    groups = lax.axis_size("tm")
    blocks = [white[None]] + [swap(white[None], "tm", k) for k in range(1, groups)]
    return stack(blocks[:groups // 2]), stack(blocks[groups // 2:], after=(where,), flops=10**9)


def between_chips(half, parts):
    chips = lax.axis_size("chan") // CORES
    places = [0, *range(chips - 1, 0, -1)]
    blocks = [swap(half, "chan", CORES * k) if k else half for k in places]
    each = chips // parts
    return [(places[i:i + each], blocks[i:i + each]) for i in range(0, chips, each)]


def between_cores(parts):
    collected = [(places, stack(blocks)) for places, blocks in parts]
    return [(places, own, swap(own, "chan", 1)) for places, own in collected]


def per_device(spectra, bad_channels, tile_list):
    groups = lax.axis_size("tm")
    hours = spectra.shape[1] * groups
    tiles = tile_list.shape[0] // groups
    white = whiten(spectra, bad_channels)
    pairs = lax.dynamic_slice_in_dim(tile_list, lax.axis_index("tm") * tiles, tiles, axis=0)
    where = jnp.concatenate([lax.axis_index("chan").reshape(1), pairs.reshape(-1)]).astype(jnp.int32).reshape(1, -1)
    near, far = halves(white, where)
    near, far = between_cores(between_chips(near, 2)), between_cores(between_chips(far, 2))
    partial = correlate(near, groups // 2, where, range(tiles), hours)
    out = correlate(far, groups // 2, where, range(tiles), hours, [partial])
    return out.reshape(tiles, LAGS, TILE, TILE)


def solution(mesh):
    placed = (P(None, "tm", None, "chan"), P("chan"), P("chan", None))
    return jax.shard_map(
        per_device,
        mesh=mesh,
        in_specs=placed,
        out_specs=P(("chan", "tm"), None, None, None),
        check_vma=False,
    )
```

```python
import math

import jax
import jax.numpy as jnp
from jax import lax
from jax.experimental import pallas as pl
from jax.experimental.pallas import tpu as pltpu
from jax.sharding import PartitionSpec as P

F = 64
LAGS = 32
TILE = 128
EPSILON = 1e-06
CORES = 2
SMALL = 4 * 1024 * 1024
VMEM = pl.BlockSpec(memory_space=pltpu.VMEM)
COARSE = (-12, -4, 4, 12)
FINE_PAIRS = ((-4, 0), (-1, 1), (-2, 2), (-3, 3))


def whiten_kernel(spectra_hbm, bad_hbm, out_ref, spectra_ref, bad_ref, sems):
    copies = [
        pltpu.make_async_copy(spectra_hbm, spectra_ref, sems.at[0]),
        pltpu.make_async_copy(bad_hbm, bad_ref, sems.at[1]),
    ]
    for copy in copies:
        copy.start()
    rows, chans = spectra_ref.shape
    bins = F
    hours = rows // (2 * bins)
    row = lax.broadcasted_iota(jnp.int32, (rows, chans), 0)
    hour = (row // 2) % hours
    src = lax.broadcasted_iota(jnp.int32, (rows, rows), 0)
    dst = lax.broadcasted_iota(jnp.int32, (rows, rows), 1)
    move = jnp.where((src % 2) * (rows // 2) + src // 2 == dst, 1.0, 0.0).astype(jnp.bfloat16)
    for copy in copies:
        copy.wait()
    values = spectra_ref[...].astype(jnp.float32)
    keep = (1 - bad_ref[...]).astype(jnp.float32)
    squares = values * values
    scale = jnp.zeros((rows, chans), jnp.float32)
    for h in range(hours):
        power = jnp.sum(jnp.where(hour == h, squares, 0.0), axis=0, keepdims=True) * (1.0 / (2 * bins))
        scale = jnp.where(hour == h, lax.rsqrt(power + EPSILON) * keep, scale)
    white = (values * scale).astype(jnp.bfloat16)
    out_ref[...] = lax.dot_general(
        white, move, (((0,), (0,)), ((), ())), preferred_element_type=jnp.float32
    ).astype(jnp.bfloat16)


def whiten(spectra, bad_channels):
    chans = spectra.shape[-1]
    spectra = spectra.reshape(-1, chans)
    spectra = pltpu.with_memory_space_constraint(spectra, pltpu.HBM)
    bad_channels = pltpu.with_memory_space_constraint(bad_channels.reshape(1, chans), pltpu.HBM)
    return pl.pallas_call(
        whiten_kernel,
        out_shape=jax.ShapeDtypeStruct((chans, spectra.shape[0]), jnp.bfloat16),
        in_specs=[pl.BlockSpec(memory_space=pltpu.HBM)] * 2,
        out_specs=VMEM,
        scratch_shapes=[
            pltpu.VMEM(spectra.shape, spectra.dtype),
            pltpu.VMEM((1, chans), bad_channels.dtype),
            pltpu.SemaphoreType.DMA((2,)),
        ],
        compiler_params=pltpu.CompilerParams(vmem_limit_bytes=SMALL),
        name="whiten",
    )(spectra, bad_channels)


def cos_sin(turn):
    quarter = F // 2
    shifted = turn + quarter // 2
    x = (shifted % quarter - quarter // 2).astype(jnp.float32) * (math.pi / F)
    y = x * x
    cos = 1 - y * (1 / 2 - y * (1 / 24 - y * (1 / 720 - y * (1 / 40320 - y / 3628800))))
    sin = x * (1 - y * (1 / 6 - y * (1 / 120 - y * (1 / 5040 - y / 362880))))
    quadrant = shifted // quarter % 4
    odd = quadrant % 2 == 1
    cos, sin = jnp.where(odd, sin, cos), jnp.where(odd, cos, sin)
    return jnp.where((quadrant == 1) | (quadrant == 2), -cos, cos), jnp.where(quadrant >= 2, -sin, sin)


def turn_by(re, im, cos, sin, both):
    rc, rs, ic, is_ = re * cos, re * sin, im * cos, im * sin
    forward = (rc - is_, rs + ic)
    return (forward, (rc + is_, ic - rs)) if both else (forward,)


def correlate_kernel(norm, picked, adds, places, where_ref, *refs):
    parts, refs = refs[:2 * len(places)], refs[2 * len(places):]
    partials = refs[:adds]
    out_ref = refs[adds]
    spectra, left_turned, right_turned, *more = refs[adds + 1:]
    groups, _, lanes = spectra.shape
    half = lanes // 2
    hours_dev = half // F
    bin_number = lax.broadcasted_iota(jnp.int32, (8, half), 1) // hours_dev + 1
    step = lax.broadcasted_iota(jnp.int32, (8, half), 0)
    cos, sin = cos_sin(jnp.where(step == 6, 12, step) * bin_number)
    table = {k: (cos[i:i + 1], sin[i:i + 1]) for k, i in ((1, 1), (2, 2), (3, 3), (4, 4), (12, 6))}

    chan = where_ref[0, 0]
    for i, piece in enumerate(parts):
        rows = piece.shape[1]
        for slot, k in enumerate(places[i // 2]):
            place = pl.multiple_of((chan ^ (CORES * k + i % 2)) * rows, 32)
            spectra[:, pl.ds(place, rows), :] = piece[slot * groups:(slot + 1) * groups]

    def load(block, g):
        whole = spectra[g, pl.ds(pl.multiple_of(block * TILE, TILE), TILE), :].astype(jnp.float32)
        return whole[:, :half], whole[:, half:]

    def store(ref, slot, index, g, value):
        rows_at = pl.ds(index * TILE, TILE)
        ref[slot, rows_at, g * lanes:g * lanes + half] = value[0].astype(jnp.bfloat16)
        ref[slot, rows_at, g * lanes + half:(g + 1) * lanes] = value[1].astype(jnp.bfloat16)

    def turn_left(i):
        for g in range(groups):
            re, im = load(where_ref[0, 1 + 2 * picked[i]], g)
            for k in (4, 12):
                forward, backward = turn_by(re, im, *(norm * part for part in table[k]), True)
                store(left_turned, i % slots, COARSE.index(k), g, forward)
                store(left_turned, i % slots, COARSE.index(-k), g, backward)

    def turn_right(i, j):
        for g in range(groups):
            re, im = load(where_ref[0, 2 + 2 * picked[i]], g)
            if j == 0:
                turns = (turn_by(re, im, *table[4], False)[0], (re, im))
            else:
                turns = turn_by(re, im, *table[j], True)
            for s in range(2):
                store(right_turned, i % slots, 2 * j + s, g, turns[s])

    slots = left_turned.shape[0]
    copies = []
    steps = [(i, j) for i in range(len(picked)) for j in range(len(FINE_PAIRS))]
    turn_left(0)
    turn_right(0, 0)
    for (i, j), after in zip(steps, steps[1:] + [None]):
        for u in range(0, len(COARSE), 2):
            if u and after:
                if after[1] == 0:
                    turn_left(after[0])
                turn_right(*after)
            total = lax.dot_general(
                left_turned[i % slots, u * TILE:(u + 2) * TILE, :],
                right_turned[i % slots, 2 * j * TILE:2 * (j + 1) * TILE, :],
                (((1,), (1,)), ((), ())),
                preferred_element_type=jnp.float32,
            )
            for v, s in ((0, 0), (0, 1), (1, 0), (1, 1)):
                fine = FINE_PAIRS[j][s] + 4
                value = total[v * TILE:(v + 1) * TILE, s * TILE:(s + 1) * TILE]
                if adds:
                    each = len(picked) // adds
                    more[0][i, u + v, fine] = partials[i // each][i % each, u + v, fine] + value
                else:
                    out_ref[i, u + v, fine] = value
        for s in range(2 if adds else 0):
            done = (i, slice(None), FINE_PAIRS[j][s] + 4)
            copy = pltpu.make_async_copy(more[0].at[done], out_ref.at[done], more[1])
            copy.start(priority=s)
            copies.append(copy)
    for copy in copies:
        copy.wait()


def correlate(parts, groups, where, picked, hours, partials=()):
    places = [part[0] for part in parts]
    pieces = [piece for part in parts for piece in part[1:]]
    _, rows, lanes = pieces[0].shape
    fine = 2 * len(FINE_PAIRS)
    shape = (len(picked), len(COARSE), fine, TILE, TILE)
    norm = 1.0 / math.sqrt(F * hours)
    slots = min(len(picked), 2)
    chans = CORES * sum(map(len, places)) * rows
    scratch = 2 * (groups * chans * lanes + slots * (len(COARSE) + fine) * TILE * groups * lanes)
    adds = len(partials)
    more = []
    if adds:
        more = [pltpu.VMEM(shape, jnp.float32), pltpu.SemaphoreType.DMA]
        scratch += 4 * math.prod(shape)
    return pl.pallas_call(
        lambda *refs: correlate_kernel(norm, picked, adds, places, *refs),
        out_shape=jax.ShapeDtypeStruct(shape, jnp.float32),
        in_specs=[VMEM] * (1 + len(pieces) + adds),
        out_specs=pl.BlockSpec(memory_space=pl.ANY) if adds else VMEM,
        scratch_shapes=[
            pltpu.VMEM((groups, chans, lanes), jnp.bfloat16),
            pltpu.VMEM((slots, len(COARSE) * TILE, groups * lanes), jnp.bfloat16),
            pltpu.VMEM((slots, fine * TILE, groups * lanes), jnp.bfloat16),
            *more,
        ],
        compiler_params=pltpu.CompilerParams(vmem_limit_bytes=scratch + SMALL),
        cost_estimate=pl.CostEstimate(flops=0, bytes_accessed=0, transcendentals=0),
        name="correlate_add" if adds else "correlate",
    )(where, *pieces, *partials)


def swap(array, axis, k):
    return lax.ppermute(array, axis, [(i, i ^ k) for i in range(lax.axis_size(axis))])


def stack_kernel(blocks, *refs):
    out_ref = refs[-1]
    first = 0
    for block in refs[:blocks]:
        out_ref[first:first + block.shape[0]] = block[...]
        first += block.shape[0]


def stack(blocks, after=(), flops=0):
    depth = sum(block.shape[0] for block in blocks)
    return pl.pallas_call(
        lambda *refs: stack_kernel(len(blocks), *refs),
        out_shape=jax.ShapeDtypeStruct((depth, *blocks[0].shape[1:]), blocks[0].dtype),
        in_specs=[VMEM] * len(blocks) + [pl.BlockSpec(memory_space=pl.ANY)] * len(after),
        out_specs=VMEM,
        compiler_params=pltpu.CompilerParams(vmem_limit_bytes=SMALL),
        cost_estimate=pl.CostEstimate(flops=flops, bytes_accessed=0, transcendentals=0),
        name="stack",
    )(*blocks, *after)


def halves(white, where):
    groups = lax.axis_size("tm")
    near_ks, far_ks = range(1, groups // 2), range(groups - 1, groups // 2 - 1, -1)
    blocks = [white[None]] + [swap(white[None], "tm", k) for k in (*near_ks, *far_ks)]
    return stack(blocks[:groups // 2]), stack(blocks[groups // 2:], after=(where,), flops=10**9)


def between_chips(half, parts):
    chips = lax.axis_size("chan") // CORES
    places = [0, *range(chips - 1, 0, -1)]
    blocks = [swap(half, "chan", CORES * k) if k else half for k in places]
    each = chips // parts
    return [(places[i:i + each], blocks[i:i + each]) for i in range(0, chips, each)]


def between_cores(parts):
    collected = [(places, stack(blocks)) for places, blocks in parts]
    return [(places, own, swap(own, "chan", 1)) for places, own in collected]


def per_device(spectra, bad_channels, tile_list):
    groups = lax.axis_size("tm")
    hours = spectra.shape[1] * groups
    tiles = tile_list.shape[0] // groups
    white = whiten(spectra, bad_channels)
    pairs = lax.dynamic_slice_in_dim(tile_list, lax.axis_index("tm") * tiles, tiles, axis=0)
    where = jnp.concatenate([lax.axis_index("chan").reshape(1), pairs.reshape(-1)]).astype(jnp.int32).reshape(1, -1)
    near, far = halves(white, where)
    near, far = between_cores(between_chips(near, 2)), between_cores(between_chips(far, 2))
    partial = correlate(near, groups // 2, where, range(tiles), hours)
    out = correlate(far, groups // 2, where, range(tiles), hours, [partial])
    return out.reshape(tiles, LAGS, TILE, TILE)


def solution(mesh):
    placed = (P(None, "tm", None, "chan"), P("chan"), P("chan", None))
    return jax.shard_map(
        per_device,
        mesh=mesh,
        in_specs=placed,
        out_specs=P(("chan", "tm"), None, None, None),
        check_vma=False,
    )
```

```python
import math

import jax
import jax.numpy as jnp
from jax import lax
from jax.experimental import pallas as pl
from jax.experimental.pallas import tpu as pltpu
from jax.sharding import PartitionSpec as P

F = 64
LAGS = 32
TILE = 128
EPSILON = 1e-06
CORES = 2
SMALL = 4 * 1024 * 1024
VMEM = pl.BlockSpec(memory_space=pltpu.VMEM)
COARSE = (-12, -4, 4, 12)
FINE_PAIRS = ((-4, 0), (-1, 1), (-2, 2), (-3, 3))


def whiten_kernel(spectra_hbm, bad_hbm, out_ref, spectra_ref, bad_ref, sems):
    rows, chans = spectra_ref.shape
    parts = 4
    slices = [pl.ds(i * rows // parts, rows // parts) for i in range(parts)]
    copies = [pltpu.make_async_copy(spectra_hbm.at[at], spectra_ref.at[at], sems.at[i]) for i, at in enumerate(slices)]
    copies.append(pltpu.make_async_copy(bad_hbm, bad_ref, sems.at[parts]))
    for copy in copies:
        copy.start()
    bins = F
    hours = rows // (2 * bins)
    row = lax.broadcasted_iota(jnp.int32, (rows, chans), 0)
    hour = (row // 2) % hours
    src = lax.broadcasted_iota(jnp.int32, (rows, rows), 0)
    dst = lax.broadcasted_iota(jnp.int32, (rows, rows), 1)
    move = jnp.where((src % 2) * (rows // 2) + src // 2 == dst, 1.0, 0.0).astype(jnp.bfloat16)
    for copy in copies:
        copy.wait()
    values = spectra_ref[...].astype(jnp.float32)
    keep = (1 - bad_ref[...]).astype(jnp.float32)
    squares = values * values
    scale = jnp.zeros((rows, chans), jnp.float32)
    for h in range(hours):
        power = jnp.sum(jnp.where(hour == h, squares, 0.0), axis=0, keepdims=True) * (1.0 / (2 * bins))
        scale = jnp.where(hour == h, lax.rsqrt(power + EPSILON) * keep, scale)
    white = (values * scale).astype(jnp.bfloat16)
    out_ref[...] = lax.dot_general(
        white, move, (((0,), (0,)), ((), ())), preferred_element_type=jnp.float32
    ).astype(jnp.bfloat16)


def whiten(spectra, bad_channels):
    chans = spectra.shape[-1]
    spectra = spectra.reshape(-1, chans)
    spectra = pltpu.with_memory_space_constraint(spectra, pltpu.HBM)
    bad_channels = pltpu.with_memory_space_constraint(bad_channels.reshape(1, chans), pltpu.HBM)
    return pl.pallas_call(
        whiten_kernel,
        out_shape=jax.ShapeDtypeStruct((chans, spectra.shape[0]), jnp.bfloat16),
        in_specs=[pl.BlockSpec(memory_space=pltpu.HBM)] * 2,
        out_specs=VMEM,
        scratch_shapes=[
            pltpu.VMEM(spectra.shape, spectra.dtype),
            pltpu.VMEM((1, chans), bad_channels.dtype),
            pltpu.SemaphoreType.DMA((5,)),
        ],
        compiler_params=pltpu.CompilerParams(vmem_limit_bytes=SMALL),
        name="whiten",
    )(spectra, bad_channels)


def cos_sin(turn):
    quarter = F // 2
    shifted = turn + quarter // 2
    x = (shifted % quarter - quarter // 2).astype(jnp.float32) * (math.pi / F)
    y = x * x
    cos = 1 - y * (1 / 2 - y * (1 / 24 - y * (1 / 720 - y * (1 / 40320 - y / 3628800))))
    sin = x * (1 - y * (1 / 6 - y * (1 / 120 - y * (1 / 5040 - y / 362880))))
    quadrant = shifted // quarter % 4
    odd = quadrant % 2 == 1
    cos, sin = jnp.where(odd, sin, cos), jnp.where(odd, cos, sin)
    return jnp.where((quadrant == 1) | (quadrant == 2), -cos, cos), jnp.where(quadrant >= 2, -sin, sin)


def turn_by(re, im, cos, sin, both):
    rc, rs, ic, is_ = re * cos, re * sin, im * cos, im * sin
    forward = (rc - is_, rs + ic)
    return (forward, (rc + is_, ic - rs)) if both else (forward,)


def correlate_kernel(norm, picked, adds, places, where_ref, *refs):
    parts, refs = refs[:2 * len(places)], refs[2 * len(places):]
    partials = refs[:adds]
    out_ref = refs[adds]
    spectra, left_turned, right_turned, *more = refs[adds + 1:]
    groups, _, lanes = spectra.shape
    half = lanes // 2
    hours_dev = half // F
    bin_number = lax.broadcasted_iota(jnp.int32, (8, half), 1) // hours_dev + 1
    step = lax.broadcasted_iota(jnp.int32, (8, half), 0)
    cos, sin = cos_sin(jnp.where(step == 6, 12, step) * bin_number)
    table = {k: (cos[i:i + 1], sin[i:i + 1]) for k, i in ((1, 1), (2, 2), (3, 3), (4, 4), (12, 6))}

    chan = where_ref[0, 0]
    for i, piece in enumerate(parts):
        rows = piece.shape[1]
        for slot, k in enumerate(places[i // 2]):
            place = pl.multiple_of((chan ^ (CORES * k + i % 2)) * rows, 32)
            spectra[:, pl.ds(place, rows), :] = piece[slot * groups:(slot + 1) * groups]

    def load(block, g):
        whole = spectra[g, pl.ds(pl.multiple_of(block * TILE, TILE), TILE), :].astype(jnp.float32)
        return whole[:, :half], whole[:, half:]

    def store(ref, slot, index, g, value):
        rows_at = pl.ds(index * TILE, TILE)
        ref[slot, rows_at, g * lanes:g * lanes + half] = value[0].astype(jnp.bfloat16)
        ref[slot, rows_at, g * lanes + half:(g + 1) * lanes] = value[1].astype(jnp.bfloat16)

    def turn_left(i):
        for g in range(groups):
            re, im = load(where_ref[0, 1 + 2 * picked[i]], g)
            for k in (4, 12):
                forward, backward = turn_by(re, im, *(norm * part for part in table[k]), True)
                store(left_turned, i % slots, COARSE.index(k), g, forward)
                store(left_turned, i % slots, COARSE.index(-k), g, backward)

    def turn_right(i, j):
        for g in range(groups):
            re, im = load(where_ref[0, 2 + 2 * picked[i]], g)
            if j == 0:
                turns = (turn_by(re, im, *table[4], False)[0], (re, im))
            else:
                turns = turn_by(re, im, *table[j], True)
            for s in range(2):
                store(right_turned, i % slots, 2 * j + s, g, turns[s])

    slots = left_turned.shape[0]
    copies = []
    steps = [(i, j) for i in range(len(picked)) for j in range(len(FINE_PAIRS))]
    turn_left(0)
    turn_right(0, 0)
    for (i, j), after in zip(steps, steps[1:] + [None]):
        for u in range(0, len(COARSE), 2):
            if u and after:
                if after[1] == 0:
                    turn_left(after[0])
                turn_right(*after)
            total = lax.dot_general(
                left_turned[i % slots, u * TILE:(u + 2) * TILE, :],
                right_turned[i % slots, 2 * j * TILE:2 * (j + 1) * TILE, :],
                (((1,), (1,)), ((), ())),
                preferred_element_type=jnp.float32,
            )
            for v, s in ((0, 0), (0, 1), (1, 0), (1, 1)):
                fine = FINE_PAIRS[j][s] + 4
                value = total[v * TILE:(v + 1) * TILE, s * TILE:(s + 1) * TILE]
                if adds:
                    each = len(picked) // adds
                    more[0][i, u + v, fine] = partials[i // each][i % each, u + v, fine] + value
                else:
                    out_ref[i, u + v, fine] = value
        for s in range(2 if adds else 0):
            done = (i, slice(None), FINE_PAIRS[j][s] + 4)
            copy = pltpu.make_async_copy(more[0].at[done], out_ref.at[done], more[1])
            copy.start(priority=s)
            copies.append(copy)
    for copy in copies:
        copy.wait()


def correlate(parts, groups, where, picked, hours, partials=()):
    places = [part[0] for part in parts]
    pieces = [piece for part in parts for piece in part[1:]]
    _, rows, lanes = pieces[0].shape
    fine = 2 * len(FINE_PAIRS)
    shape = (len(picked), len(COARSE), fine, TILE, TILE)
    norm = 1.0 / math.sqrt(F * hours)
    slots = min(len(picked), 2)
    chans = CORES * sum(map(len, places)) * rows
    scratch = 2 * (groups * chans * lanes + slots * (len(COARSE) + fine) * TILE * groups * lanes)
    adds = len(partials)
    more = []
    if adds:
        more = [pltpu.VMEM(shape, jnp.float32), pltpu.SemaphoreType.DMA]
        scratch += 4 * math.prod(shape)
    return pl.pallas_call(
        lambda *refs: correlate_kernel(norm, picked, adds, places, *refs),
        out_shape=jax.ShapeDtypeStruct(shape, jnp.float32),
        in_specs=[VMEM] * (1 + len(pieces) + adds),
        out_specs=pl.BlockSpec(memory_space=pl.ANY) if adds else VMEM,
        scratch_shapes=[
            pltpu.VMEM((groups, chans, lanes), jnp.bfloat16),
            pltpu.VMEM((slots, len(COARSE) * TILE, groups * lanes), jnp.bfloat16),
            pltpu.VMEM((slots, fine * TILE, groups * lanes), jnp.bfloat16),
            *more,
        ],
        compiler_params=pltpu.CompilerParams(vmem_limit_bytes=scratch + SMALL),
        cost_estimate=pl.CostEstimate(flops=0, bytes_accessed=0, transcendentals=0),
        name="correlate_add" if adds else "correlate",
    )(where, *pieces, *partials)


def swap(array, axis, k):
    return lax.ppermute(array, axis, [(i, i ^ k) for i in range(lax.axis_size(axis))])


def stack_kernel(blocks, *refs):
    out_ref = refs[-1]
    first = 0
    for block in refs[:blocks]:
        out_ref[first:first + block.shape[0]] = block[...]
        first += block.shape[0]


def stack(blocks, after=(), flops=0):
    depth = sum(block.shape[0] for block in blocks)
    return pl.pallas_call(
        lambda *refs: stack_kernel(len(blocks), *refs),
        out_shape=jax.ShapeDtypeStruct((depth, *blocks[0].shape[1:]), blocks[0].dtype),
        in_specs=[VMEM] * len(blocks) + [pl.BlockSpec(memory_space=pl.ANY)] * len(after),
        out_specs=VMEM,
        compiler_params=pltpu.CompilerParams(vmem_limit_bytes=SMALL),
        cost_estimate=pl.CostEstimate(flops=flops, bytes_accessed=0, transcendentals=0),
        name="stack",
    )(*blocks, *after)


def halves(white, where):
    groups = lax.axis_size("tm")
    blocks = [white[None]] + [swap(white[None], "tm", k) for k in range(1, groups)]
    return stack(blocks[:groups // 2]), stack(blocks[groups // 2:], after=(where,), flops=10**9)


def between_chips(half, parts):
    chips = lax.axis_size("chan") // CORES
    places = [0, *range(chips - 1, 0, -1)]
    blocks = [swap(half, "chan", CORES * k) if k else half for k in places]
    each = chips // parts
    return [(places[i:i + each], blocks[i:i + each]) for i in range(0, chips, each)]


def between_cores(parts):
    collected = [(places, stack(blocks)) for places, blocks in parts]
    return [(places, own, swap(own, "chan", 1)) for places, own in collected]


def per_device(spectra, bad_channels, tile_list):
    groups = lax.axis_size("tm")
    hours = spectra.shape[1] * groups
    tiles = tile_list.shape[0] // groups
    white = whiten(spectra, bad_channels)
    pairs = lax.dynamic_slice_in_dim(tile_list, lax.axis_index("tm") * tiles, tiles, axis=0)
    where = jnp.concatenate([lax.axis_index("chan").reshape(1), pairs.reshape(-1)]).astype(jnp.int32).reshape(1, -1)
    near, far = halves(white, where)
    near, far = between_cores(between_chips(near, 2)), between_cores(between_chips(far, 2))
    partial = correlate(near, groups // 2, where, range(tiles), hours)
    out = correlate(far, groups // 2, where, range(tiles), hours, [partial])
    return out.reshape(tiles, LAGS, TILE, TILE)


def solution(mesh):
    placed = (P(None, "tm", None, "chan"), P("chan"), P("chan", None))
    return jax.shard_map(
        per_device,
        mesh=mesh,
        in_specs=placed,
        out_specs=P(("chan", "tm"), None, None, None),
        check_vma=False,
    )
```

```python
import math

import jax
import jax.numpy as jnp
from jax import lax
from jax.experimental import pallas as pl
from jax.experimental.pallas import tpu as pltpu
from jax.sharding import PartitionSpec as P

F = 64
LAGS = 32
TILE = 128
EPSILON = 1e-06
CORES = 2
SMALL = 4 * 1024 * 1024
VMEM = pl.BlockSpec(memory_space=pltpu.VMEM)
COARSE = (-12, -4, 4, 12)
FINE_PAIRS = ((-4, 0), (-1, 1), (-2, 2), (-3, 3))


def whiten_kernel(spectra_hbm, bad_hbm, out_ref, spectra_ref, bad_ref, sems):
    rows, chans = spectra_ref.shape
    parts = 4
    slices = [pl.ds(i * rows // parts, rows // parts) for i in range(parts)]
    copies = [pltpu.make_async_copy(spectra_hbm.at[at], spectra_ref.at[at], sems.at[i]) for i, at in enumerate(slices)]
    copies.append(pltpu.make_async_copy(bad_hbm, bad_ref, sems.at[parts]))
    for copy in copies:
        copy.start()
    bins = F
    hours = rows // (2 * bins)
    row = lax.broadcasted_iota(jnp.int32, (rows, chans), 0)
    hour = (row // 2) % hours
    src = lax.broadcasted_iota(jnp.int32, (rows, rows), 0)
    dst = lax.broadcasted_iota(jnp.int32, (rows, rows), 1)
    move = jnp.where((src % 2) * (rows // 2) + src // 2 == dst, 1.0, 0.0).astype(jnp.bfloat16)
    for copy in copies:
        copy.wait()
    values = spectra_ref[...].astype(jnp.float32)
    keep = (1 - bad_ref[...]).astype(jnp.float32)
    squares = values * values
    scale = jnp.zeros((rows, chans), jnp.float32)
    for h in range(hours):
        power = jnp.sum(jnp.where(hour == h, squares, 0.0), axis=0, keepdims=True) * (1.0 / (2 * bins))
        scale = jnp.where(hour == h, lax.rsqrt(power + EPSILON) * keep, scale)
    white = (values * scale).astype(jnp.bfloat16)
    out_ref[...] = lax.dot_general(
        white, move, (((0,), (0,)), ((), ())), preferred_element_type=jnp.float32
    ).astype(jnp.bfloat16)


def whiten(spectra, bad_channels):
    chans = spectra.shape[-1]
    spectra = spectra.reshape(-1, chans)
    spectra = pltpu.with_memory_space_constraint(spectra, pltpu.HBM)
    bad_channels = pltpu.with_memory_space_constraint(bad_channels.reshape(1, chans), pltpu.HBM)
    return pl.pallas_call(
        whiten_kernel,
        out_shape=jax.ShapeDtypeStruct((chans, spectra.shape[0]), jnp.bfloat16),
        in_specs=[pl.BlockSpec(memory_space=pltpu.HBM)] * 2,
        out_specs=VMEM,
        scratch_shapes=[
            pltpu.VMEM(spectra.shape, spectra.dtype),
            pltpu.VMEM((1, chans), bad_channels.dtype),
            pltpu.SemaphoreType.DMA((5,)),
        ],
        compiler_params=pltpu.CompilerParams(vmem_limit_bytes=SMALL),
        name="whiten",
    )(spectra, bad_channels)


def cos_sin(turn):
    quarter = F // 2
    shifted = turn + quarter // 2
    x = (shifted % quarter - quarter // 2).astype(jnp.float32) * (math.pi / F)
    y = x * x
    cos = 1 - y * (1 / 2 - y * (1 / 24 - y * (1 / 720 - y * (1 / 40320 - y / 3628800))))
    sin = x * (1 - y * (1 / 6 - y * (1 / 120 - y * (1 / 5040 - y / 362880))))
    quadrant = shifted // quarter % 4
    odd = quadrant % 2 == 1
    cos, sin = jnp.where(odd, sin, cos), jnp.where(odd, cos, sin)
    return jnp.where((quadrant == 1) | (quadrant == 2), -cos, cos), jnp.where(quadrant >= 2, -sin, sin)


def turn_by(re, im, cos, sin, both):
    rc, rs, ic, is_ = re * cos, re * sin, im * cos, im * sin
    forward = (rc - is_, rs + ic)
    return (forward, (rc + is_, ic - rs)) if both else (forward,)


def correlate_kernel(norm, picked, adds, places, where_ref, *refs):
    parts, refs = refs[:2 * len(places)], refs[2 * len(places):]
    partials = refs[:adds]
    out_ref = refs[adds]
    spectra, left_turned, right_turned, *more = refs[adds + 1:]
    groups, _, lanes = spectra.shape
    half = lanes // 2
    hours_dev = half // F
    bin_number = lax.broadcasted_iota(jnp.int32, (8, half), 1) // hours_dev + 1
    step = lax.broadcasted_iota(jnp.int32, (8, half), 0)
    cos, sin = cos_sin(jnp.where(step == 6, 12, step) * bin_number)
    table = {k: (cos[i:i + 1], sin[i:i + 1]) for k, i in ((1, 1), (2, 2), (3, 3), (4, 4), (12, 6))}

    chan = where_ref[0, 0]
    for i, piece in enumerate(parts):
        rows = piece.shape[1]
        for slot, k in enumerate(places[i // 2]):
            place = pl.multiple_of((chan ^ (CORES * k + i % 2)) * rows, 32)
            spectra[:, pl.ds(place, rows), :] = piece[slot * groups:(slot + 1) * groups]

    def load(block, g):
        whole = spectra[g, pl.ds(pl.multiple_of(block * TILE, TILE), TILE), :].astype(jnp.float32)
        return whole[:, :half], whole[:, half:]

    def store(ref, slot, index, g, value):
        rows_at = pl.ds(index * TILE, TILE)
        ref[slot, rows_at, g * lanes:g * lanes + half] = value[0].astype(jnp.bfloat16)
        ref[slot, rows_at, g * lanes + half:(g + 1) * lanes] = value[1].astype(jnp.bfloat16)

    def turn_left(i):
        for g in range(groups):
            re, im = load(where_ref[0, 1 + 2 * picked[i]], g)
            for k in (4, 12):
                forward, backward = turn_by(re, im, *(norm * part for part in table[k]), True)
                store(left_turned, i % slots, COARSE.index(k), g, forward)
                store(left_turned, i % slots, COARSE.index(-k), g, backward)

    def turn_right(i, j):
        for g in range(groups):
            re, im = load(where_ref[0, 2 + 2 * picked[i]], g)
            if j == 0:
                turns = (turn_by(re, im, *table[4], False)[0], (re, im))
            else:
                turns = turn_by(re, im, *table[j], True)
            for s in range(2):
                store(right_turned, i % slots, 2 * j + s, g, turns[s])

    slots = left_turned.shape[0]
    copies = []
    steps = [(i, j) for i in range(len(picked)) for j in range(len(FINE_PAIRS))]
    turn_left(0)
    turn_right(0, 0)
    for (i, j), after in zip(steps, steps[1:] + [None]):
        for u in range(0, len(COARSE), 2):
            if u and after:
                if after[1] == 0:
                    turn_left(after[0])
                turn_right(*after)
            total = lax.dot_general(
                left_turned[i % slots, u * TILE:(u + 2) * TILE, :],
                right_turned[i % slots, 2 * j * TILE:2 * (j + 1) * TILE, :],
                (((1,), (1,)), ((), ())),
                preferred_element_type=jnp.float32,
            )
            for v, s in ((0, 0), (0, 1), (1, 0), (1, 1)):
                fine = FINE_PAIRS[j][s] + 4
                value = total[v * TILE:(v + 1) * TILE, s * TILE:(s + 1) * TILE]
                if adds:
                    each = len(picked) // adds
                    more[0][i, u + v, fine] = partials[i // each][i % each, u + v, fine] + value
                else:
                    out_ref[i, u + v, fine] = value
            ready = slice(u, u + 2) if not after else slice(None) if u else None
            for s in range(2 if adds and ready else 0):
                done = (i, ready, FINE_PAIRS[j][s] + 4)
                copy = pltpu.make_async_copy(more[0].at[done], out_ref.at[done], more[1])
                copy.start(priority=s)
                copies.append(copy)
    for copy in copies:
        copy.wait()


def correlate(parts, groups, where, picked, hours, partials=()):
    places = [part[0] for part in parts]
    pieces = [piece for part in parts for piece in part[1:]]
    _, rows, lanes = pieces[0].shape
    fine = 2 * len(FINE_PAIRS)
    shape = (len(picked), len(COARSE), fine, TILE, TILE)
    norm = 1.0 / math.sqrt(F * hours)
    slots = min(len(picked), 2)
    chans = CORES * sum(map(len, places)) * rows
    scratch = 2 * (groups * chans * lanes + slots * (len(COARSE) + fine) * TILE * groups * lanes)
    adds = len(partials)
    more = []
    if adds:
        more = [pltpu.VMEM(shape, jnp.float32), pltpu.SemaphoreType.DMA]
        scratch += 4 * math.prod(shape)
    return pl.pallas_call(
        lambda *refs: correlate_kernel(norm, picked, adds, places, *refs),
        out_shape=jax.ShapeDtypeStruct(shape, jnp.float32),
        in_specs=[VMEM] * (1 + len(pieces) + adds),
        out_specs=pl.BlockSpec(memory_space=pl.ANY) if adds else VMEM,
        scratch_shapes=[
            pltpu.VMEM((groups, chans, lanes), jnp.bfloat16),
            pltpu.VMEM((slots, len(COARSE) * TILE, groups * lanes), jnp.bfloat16),
            pltpu.VMEM((slots, fine * TILE, groups * lanes), jnp.bfloat16),
            *more,
        ],
        compiler_params=pltpu.CompilerParams(vmem_limit_bytes=scratch + SMALL),
        cost_estimate=pl.CostEstimate(flops=0, bytes_accessed=0, transcendentals=0),
        name="correlate_add" if adds else "correlate",
    )(where, *pieces, *partials)


def swap(array, axis, k):
    return lax.ppermute(array, axis, [(i, i ^ k) for i in range(lax.axis_size(axis))])


def stack_kernel(blocks, *refs):
    out_ref = refs[-1]
    first = 0
    for block in refs[:blocks]:
        out_ref[first:first + block.shape[0]] = block[...]
        first += block.shape[0]


def stack(blocks, after=(), flops=0):
    depth = sum(block.shape[0] for block in blocks)
    return pl.pallas_call(
        lambda *refs: stack_kernel(len(blocks), *refs),
        out_shape=jax.ShapeDtypeStruct((depth, *blocks[0].shape[1:]), blocks[0].dtype),
        in_specs=[VMEM] * len(blocks) + [pl.BlockSpec(memory_space=pl.ANY)] * len(after),
        out_specs=VMEM,
        compiler_params=pltpu.CompilerParams(vmem_limit_bytes=SMALL),
        cost_estimate=pl.CostEstimate(flops=flops, bytes_accessed=0, transcendentals=0),
        name="stack",
    )(*blocks, *after)


def halves(white, where):
    groups = lax.axis_size("tm")
    blocks = [white[None]] + [swap(white[None], "tm", k) for k in range(1, groups)]
    return stack(blocks[:groups // 2]), stack(blocks[groups // 2:], after=(where,), flops=10**9)


def between_chips(half, parts):
    chips = lax.axis_size("chan") // CORES
    places = [0, *range(chips - 1, 0, -1)]
    blocks = [swap(half, "chan", CORES * k) if k else half for k in places]
    each = chips // parts
    return [(places[i:i + each], blocks[i:i + each]) for i in range(0, chips, each)]


def between_cores(parts):
    collected = [(places, stack(blocks)) for places, blocks in parts]
    return [(places, own, swap(own, "chan", 1)) for places, own in collected]


def per_device(spectra, bad_channels, tile_list):
    groups = lax.axis_size("tm")
    hours = spectra.shape[1] * groups
    tiles = tile_list.shape[0] // groups
    white = whiten(spectra, bad_channels)
    pairs = lax.dynamic_slice_in_dim(tile_list, lax.axis_index("tm") * tiles, tiles, axis=0)
    where = jnp.concatenate([lax.axis_index("chan").reshape(1), pairs.reshape(-1)]).astype(jnp.int32).reshape(1, -1)
    near, far = halves(white, where)
    near, far = between_cores(between_chips(near, 2)), between_cores(between_chips(far, 2))
    partial = correlate(near, groups // 2, where, range(tiles), hours)
    out = correlate(far, groups // 2, where, range(tiles), hours, [partial])
    return out.reshape(tiles, LAGS, TILE, TILE)


def solution(mesh):
    placed = (P(None, "tm", None, "chan"), P("chan"), P("chan", None))
    return jax.shard_map(
        per_device,
        mesh=mesh,
        in_specs=placed,
        out_specs=P(("chan", "tm"), None, None, None),
        check_vma=False,
    )
```

```python
import math

import jax
import jax.numpy as jnp
from jax import lax
from jax.experimental import pallas as pl
from jax.experimental.pallas import tpu as pltpu
from jax.sharding import PartitionSpec as P

F = 64
LAGS = 32
TILE = 128
EPSILON = 1e-06
CORES = 2
SMALL = 4 * 1024 * 1024
VMEM = pl.BlockSpec(memory_space=pltpu.VMEM)
COARSE = (-12, -4, 4, 12)
FINE_PAIRS = ((-4, 0), (-1, 1), (-2, 2), (-3, 3))


def whiten_kernel(spectra_hbm, bad_hbm, out_ref, spectra_ref, bad_ref, sems):
    rows, chans = spectra_ref.shape
    parts = 4
    slices = [pl.ds(i * rows // parts, rows // parts) for i in range(parts)]
    copies = [pltpu.make_async_copy(spectra_hbm.at[at], spectra_ref.at[at], sems.at[i]) for i, at in enumerate(slices)]
    copies.append(pltpu.make_async_copy(bad_hbm, bad_ref, sems.at[parts]))
    for copy in copies:
        copy.start()
    bins = F
    hours = rows // (2 * bins)
    row = lax.broadcasted_iota(jnp.int32, (rows, chans), 0)
    hour = (row // 2) % hours
    src = lax.broadcasted_iota(jnp.int32, (rows, rows), 0)
    dst = lax.broadcasted_iota(jnp.int32, (rows, rows), 1)
    move = jnp.where((src % 2) * (rows // 2) + src // 2 == dst, 1.0, 0.0).astype(jnp.bfloat16)
    for copy in copies:
        copy.wait()
    values = spectra_ref[...].astype(jnp.float32)
    keep = (1 - bad_ref[...]).astype(jnp.float32)
    squares = values * values
    scale = jnp.zeros((rows, chans), jnp.float32)
    for h in range(hours):
        power = jnp.sum(jnp.where(hour == h, squares, 0.0), axis=0, keepdims=True) * (1.0 / (2 * bins))
        scale = jnp.where(hour == h, lax.rsqrt(power + EPSILON) * keep, scale)
    white = (values * scale).astype(jnp.bfloat16)
    out_ref[...] = lax.dot_general(
        white, move, (((0,), (0,)), ((), ())), preferred_element_type=jnp.float32
    ).astype(jnp.bfloat16)


def whiten(spectra, bad_channels):
    chans = spectra.shape[-1]
    spectra = spectra.reshape(-1, chans)
    spectra = pltpu.with_memory_space_constraint(spectra, pltpu.HBM)
    bad_channels = pltpu.with_memory_space_constraint(bad_channels.reshape(1, chans), pltpu.HBM)
    return pl.pallas_call(
        whiten_kernel,
        out_shape=jax.ShapeDtypeStruct((chans, spectra.shape[0]), jnp.bfloat16),
        in_specs=[pl.BlockSpec(memory_space=pltpu.HBM)] * 2,
        out_specs=VMEM,
        scratch_shapes=[
            pltpu.VMEM(spectra.shape, spectra.dtype),
            pltpu.VMEM((1, chans), bad_channels.dtype),
            pltpu.SemaphoreType.DMA((5,)),
        ],
        compiler_params=pltpu.CompilerParams(vmem_limit_bytes=SMALL),
        name="whiten",
    )(spectra, bad_channels)


def cos_sin(turn):
    quarter = F // 2
    shifted = turn + quarter // 2
    x = (shifted % quarter - quarter // 2).astype(jnp.float32) * (math.pi / F)
    y = x * x
    cos = 1 - y * (1 / 2 - y * (1 / 24 - y * (1 / 720 - y * (1 / 40320 - y / 3628800))))
    sin = x * (1 - y * (1 / 6 - y * (1 / 120 - y * (1 / 5040 - y / 362880))))
    quadrant = shifted // quarter % 4
    odd = quadrant % 2 == 1
    cos, sin = jnp.where(odd, sin, cos), jnp.where(odd, cos, sin)
    return jnp.where((quadrant == 1) | (quadrant == 2), -cos, cos), jnp.where(quadrant >= 2, -sin, sin)


def turn_by(re, im, cos, sin, both):
    rc, rs, ic, is_ = re * cos, re * sin, im * cos, im * sin
    forward = (rc - is_, rs + ic)
    return (forward, (rc + is_, ic - rs)) if both else (forward,)


def correlate_kernel(norm, picked, adds, places, where_ref, *refs):
    parts, refs = refs[:2 * len(places)], refs[2 * len(places):]
    partials = refs[:adds]
    out_ref = refs[adds]
    spectra, left_turned, right_turned, *more = refs[adds + 1:]
    groups, _, lanes = spectra.shape
    half = lanes // 2
    hours_dev = half // F
    bin_number = lax.broadcasted_iota(jnp.int32, (8, half), 1) // hours_dev + 1
    step = lax.broadcasted_iota(jnp.int32, (8, half), 0)
    cos, sin = cos_sin(jnp.where(step == 6, 12, step) * bin_number)
    table = {k: (cos[i:i + 1], sin[i:i + 1]) for k, i in ((1, 1), (2, 2), (3, 3), (4, 4), (12, 6))}

    chan = where_ref[0, 0]
    for i, piece in enumerate(parts):
        rows = piece.shape[1]
        for slot, k in enumerate(places[i // 2]):
            place = pl.multiple_of((chan ^ (CORES * k + i % 2)) * rows, 32)
            spectra[:, pl.ds(place, rows), :] = piece[slot * groups:(slot + 1) * groups]

    def load(block, g):
        whole = spectra[g, pl.ds(pl.multiple_of(block * TILE, TILE), TILE), :].astype(jnp.float32)
        return whole[:, :half], whole[:, half:]

    def store(ref, slot, index, g, value):
        rows_at = pl.ds(index * TILE, TILE)
        ref[slot, rows_at, g * lanes:g * lanes + half] = value[0].astype(jnp.bfloat16)
        ref[slot, rows_at, g * lanes + half:(g + 1) * lanes] = value[1].astype(jnp.bfloat16)

    def turn_left(i):
        for g in range(groups):
            re, im = load(where_ref[0, 1 + 2 * picked[i]], g)
            for k in (4, 12):
                forward, backward = turn_by(re, im, *(norm * part for part in table[k]), True)
                store(left_turned, i % slots, COARSE.index(k), g, forward)
                store(left_turned, i % slots, COARSE.index(-k), g, backward)

    def turn_right(i, j):
        for g in range(groups):
            re, im = load(where_ref[0, 2 + 2 * picked[i]], g)
            if j == 0:
                turns = (turn_by(re, im, *table[4], False)[0], (re, im))
            else:
                turns = turn_by(re, im, *table[j], True)
            for s in range(2):
                store(right_turned, i % slots, 2 * j + s, g, turns[s])

    slots = left_turned.shape[0]
    copies = []
    steps = [(i, j) for i in range(len(picked)) for j in range(len(FINE_PAIRS))]
    turn_left(0)
    turn_right(0, 0)
    for (i, j), after in zip(steps, steps[1:] + [None]):
        for u in range(0, len(COARSE), 2):
            if u and after:
                if after[1] == 0:
                    turn_left(after[0])
                turn_right(*after)
            total = lax.dot_general(
                left_turned[i % slots, u * TILE:(u + 2) * TILE, :],
                right_turned[i % slots, 2 * j * TILE:2 * (j + 1) * TILE, :],
                (((1,), (1,)), ((), ())),
                preferred_element_type=jnp.float32,
            )
            for v, s in ((0, 0), (0, 1), (1, 0), (1, 1)):
                fine = FINE_PAIRS[j][s] + 4
                value = total[v * TILE:(v + 1) * TILE, s * TILE:(s + 1) * TILE]
                if adds:
                    each = len(picked) // adds
                    more[0][i, u + v, fine] = partials[i // each][i % each, u + v, fine] + value
                else:
                    out_ref[i, u + v, fine] = value
        for s in range(2 if adds else 0):
            done = (i, slice(None), FINE_PAIRS[j][s] + 4)
            copy = pltpu.make_async_copy(more[0].at[done], out_ref.at[done], more[1])
            copy.start(priority=s)
            copies.append(copy)
    for copy in copies:
        copy.wait()


def correlate(parts, groups, where, picked, hours, partials=()):
    places = [part[0] for part in parts]
    pieces = [piece for part in parts for piece in part[1:]]
    _, rows, lanes = pieces[0].shape
    fine = 2 * len(FINE_PAIRS)
    shape = (len(picked), len(COARSE), fine, TILE, TILE)
    norm = 1.0 / math.sqrt(F * hours)
    slots = min(len(picked), 2)
    chans = CORES * sum(map(len, places)) * rows
    scratch = 2 * (groups * chans * lanes + slots * (len(COARSE) + fine) * TILE * groups * lanes)
    adds = len(partials)
    more = []
    if adds:
        more = [pltpu.VMEM(shape, jnp.float32), pltpu.SemaphoreType.DMA]
        scratch += 4 * math.prod(shape)
    return pl.pallas_call(
        lambda *refs: correlate_kernel(norm, picked, adds, places, *refs),
        out_shape=jax.ShapeDtypeStruct(shape, jnp.float32),
        in_specs=[VMEM] * (1 + len(pieces) + adds),
        out_specs=pl.BlockSpec(memory_space=pl.ANY) if adds else VMEM,
        scratch_shapes=[
            pltpu.VMEM((groups, chans, lanes), jnp.bfloat16),
            pltpu.VMEM((slots, len(COARSE) * TILE, groups * lanes), jnp.bfloat16),
            pltpu.VMEM((slots, fine * TILE, groups * lanes), jnp.bfloat16),
            *more,
        ],
        compiler_params=pltpu.CompilerParams(vmem_limit_bytes=scratch + SMALL),
        cost_estimate=pl.CostEstimate(flops=0, bytes_accessed=0, transcendentals=0),
        name="correlate_add" if adds else "correlate",
    )(where, *pieces, *partials)


def swap(array, axis, k):
    return lax.ppermute(array, axis, [(i, i ^ k) for i in range(lax.axis_size(axis))])


def stack_kernel(blocks, *refs):
    out_ref = refs[-1]
    first = 0
    for block in refs[:blocks]:
        out_ref[first:first + block.shape[0]] = block[...]
        first += block.shape[0]


def stack(blocks, after=(), flops=0):
    depth = sum(block.shape[0] for block in blocks)
    return pl.pallas_call(
        lambda *refs: stack_kernel(len(blocks), *refs),
        out_shape=jax.ShapeDtypeStruct((depth, *blocks[0].shape[1:]), blocks[0].dtype),
        in_specs=[VMEM] * len(blocks) + [pl.BlockSpec(memory_space=pl.ANY)] * len(after),
        out_specs=VMEM,
        compiler_params=pltpu.CompilerParams(vmem_limit_bytes=SMALL),
        cost_estimate=pl.CostEstimate(flops=flops, bytes_accessed=0, transcendentals=0),
        name="stack",
    )(*blocks, *after)


def halves(white, where):
    groups = lax.axis_size("tm")
    blocks = [white[None]] + [swap(white[None], "tm", k) for k in range(1, groups)]
    return stack(blocks[:groups // 2]), stack(blocks[groups // 2:], after=(where,), flops=10**9)


def between_chips(half, parts):
    chips = lax.axis_size("chan") // CORES
    places = [0, *range(chips - 1, 0, -1)]
    blocks = [swap(half, "chan", CORES * k) if k else half for k in places]
    each = chips // parts
    return [(places[i:i + each], blocks[i:i + each]) for i in range(0, chips, each)]


def between_cores(parts):
    collected = [(places, stack(blocks)) for places, blocks in parts]
    return [(places, own, swap(own, "chan", 1)) for places, own in collected]


def per_device(spectra, bad_channels, tile_list):
    groups = lax.axis_size("tm")
    hours = spectra.shape[1] * groups
    tiles = tile_list.shape[0] // groups
    white = whiten(spectra, bad_channels)
    at, row, side = (lax.broadcasted_iota(jnp.int32, (1 + 2 * tiles, *tile_list.shape), d) for d in range(3))
    first = 2 * tiles * lax.axis_index("tm")
    blocks = jnp.sum(jnp.where((at > 0) & (at - 1 + first == 2 * row + side), tile_list[None], 0), axis=(1, 2))
    where = jnp.where(jnp.arange(1 + 2 * tiles) == 0, lax.axis_index("chan"), blocks).astype(jnp.int32).reshape(1, -1)
    near, far = halves(white, where)
    near, far = between_cores(between_chips(near, 2)), between_cores(between_chips(far, 2))
    partial = correlate(near, groups // 2, where, range(tiles), hours)
    out = correlate(far, groups // 2, where, range(tiles), hours, [partial])
    return out.reshape(tiles, LAGS, TILE, TILE)


def solution(mesh):
    placed = (P(None, "tm", None, "chan"), P("chan"), P("chan", None))
    return jax.shard_map(
        per_device,
        mesh=mesh,
        in_specs=placed,
        out_specs=P(("chan", "tm"), None, None, None),
        check_vma=False,
    )
```

```python
import math

import jax
import jax.numpy as jnp
from jax import lax
from jax.experimental import pallas as pl
from jax.experimental.pallas import tpu as pltpu
from jax.sharding import PartitionSpec as P

F = 64
LAGS = 32
TILE = 128
EPSILON = 1e-06
CORES = 2
SMALL = 4 * 1024 * 1024
VMEM = pl.BlockSpec(memory_space=pltpu.VMEM)
COARSE = (-12, -4, 4, 12)
FINE_PAIRS = ((-4, 0), (-1, 1), (-2, 2), (-3, 3))


def whiten_kernel(spectra_hbm, bad_hbm, out_ref, spectra_ref, bad_ref, sems):
    rows, chans = spectra_ref.shape
    parts = 4
    slices = [pl.ds(i * rows // parts, rows // parts) for i in range(parts)]
    copies = [pltpu.make_async_copy(spectra_hbm.at[at], spectra_ref.at[at], sems.at[i]) for i, at in enumerate(slices)]
    copies.append(pltpu.make_async_copy(bad_hbm, bad_ref, sems.at[parts]))
    for copy in copies:
        copy.start()
    bins = F
    hours = rows // (2 * bins)
    row = lax.broadcasted_iota(jnp.int32, (rows, chans), 0)
    hour = (row // 2) % hours
    src = lax.broadcasted_iota(jnp.int32, (rows, rows), 0)
    dst = lax.broadcasted_iota(jnp.int32, (rows, rows), 1)
    move = jnp.where((src % 2) * (rows // 2) + src // 2 == dst, 1.0, 0.0).astype(jnp.bfloat16)
    for copy in copies:
        copy.wait()
    values = spectra_ref[...].astype(jnp.float32)
    keep = (1 - bad_ref[...]).astype(jnp.float32)
    squares = values * values
    scale = jnp.zeros((rows, chans), jnp.float32)
    for h in range(hours):
        power = jnp.sum(jnp.where(hour == h, squares, 0.0), axis=0, keepdims=True) * (1.0 / (2 * bins))
        scale = jnp.where(hour == h, lax.rsqrt(power + EPSILON) * keep, scale)
    white = (values * scale).astype(jnp.bfloat16)
    out_ref[...] = lax.dot_general(
        white, move, (((0,), (0,)), ((), ())), preferred_element_type=jnp.float32
    ).astype(jnp.bfloat16)


def whiten(spectra, bad_channels):
    chans = spectra.shape[-1]
    spectra = spectra.reshape(-1, chans)
    spectra = pltpu.with_memory_space_constraint(spectra, pltpu.HBM)
    bad_channels = pltpu.with_memory_space_constraint(bad_channels.reshape(1, chans), pltpu.HBM)
    return pl.pallas_call(
        whiten_kernel,
        out_shape=jax.ShapeDtypeStruct((chans, spectra.shape[0]), jnp.bfloat16),
        in_specs=[pl.BlockSpec(memory_space=pltpu.HBM)] * 2,
        out_specs=VMEM,
        scratch_shapes=[
            pltpu.VMEM(spectra.shape, spectra.dtype),
            pltpu.VMEM((1, chans), bad_channels.dtype),
            pltpu.SemaphoreType.DMA((5,)),
        ],
        compiler_params=pltpu.CompilerParams(vmem_limit_bytes=SMALL),
        name="whiten",
    )(spectra, bad_channels)


def cos_sin(turn):
    quarter = F // 2
    shifted = turn + quarter // 2
    x = (shifted % quarter - quarter // 2).astype(jnp.float32) * (math.pi / F)
    y = x * x
    cos = 1 - y * (1 / 2 - y * (1 / 24 - y * (1 / 720 - y * (1 / 40320 - y / 3628800))))
    sin = x * (1 - y * (1 / 6 - y * (1 / 120 - y * (1 / 5040 - y / 362880))))
    quadrant = shifted // quarter % 4
    odd = quadrant % 2 == 1
    cos, sin = jnp.where(odd, sin, cos), jnp.where(odd, cos, sin)
    return jnp.where((quadrant == 1) | (quadrant == 2), -cos, cos), jnp.where(quadrant >= 2, -sin, sin)


def turn_by(re, im, cos, sin, both):
    rc, rs, ic, is_ = re * cos, re * sin, im * cos, im * sin
    forward = (rc - is_, rs + ic)
    return (forward, (rc + is_, ic - rs)) if both else (forward,)


def correlate_kernel(norm, picked, adds, places, where_ref, *refs):
    parts, refs = refs[:2 * len(places)], refs[2 * len(places):]
    partials = refs[:adds]
    out_ref = refs[adds]
    spectra, left_turned, right_turned, *more = refs[adds + 1:]
    groups, _, lanes = spectra.shape
    half = lanes // 2
    hours_dev = half // F
    bin_number = lax.broadcasted_iota(jnp.int32, (8, half), 1) // hours_dev + 1
    step = lax.broadcasted_iota(jnp.int32, (8, half), 0)
    cos, sin = cos_sin(jnp.where(step == 6, 12, step) * bin_number)
    table = {k: (cos[i:i + 1], sin[i:i + 1]) for k, i in ((1, 1), (2, 2), (3, 3), (4, 4), (12, 6))}

    chan = where_ref[0, 0]
    for i, piece in enumerate(parts):
        rows = piece.shape[1]
        for slot, k in enumerate(places[i // 2]):
            place = pl.multiple_of((chan ^ (CORES * k + i % 2)) * rows, 32)
            spectra[:, pl.ds(place, rows), :] = piece[slot * groups:(slot + 1) * groups]

    def load(block, g):
        whole = spectra[g, pl.ds(pl.multiple_of(block * TILE, TILE), TILE), :].astype(jnp.float32)
        return whole[:, :half], whole[:, half:]

    def store(ref, slot, index, g, value):
        rows_at = pl.ds(index * TILE, TILE)
        ref[slot, rows_at, g * lanes:g * lanes + half] = value[0].astype(jnp.bfloat16)
        ref[slot, rows_at, g * lanes + half:(g + 1) * lanes] = value[1].astype(jnp.bfloat16)

    def turn_left(i):
        for g in range(groups):
            re, im = load(where_ref[0, 1 + picked[i]], g)
            for k in (4, 12):
                forward, backward = turn_by(re, im, *(norm * part for part in table[k]), True)
                store(left_turned, i % slots, COARSE.index(k), g, forward)
                store(left_turned, i % slots, COARSE.index(-k), g, backward)

    def turn_right(i, j):
        for g in range(groups):
            re, im = load(where_ref[0, (where_ref.shape[1] + 1) // 2 + picked[i]], g)
            if j == 0:
                turns = (turn_by(re, im, *table[4], False)[0], (re, im))
            else:
                turns = turn_by(re, im, *table[j], True)
            for s in range(2):
                store(right_turned, i % slots, 2 * j + s, g, turns[s])

    slots = left_turned.shape[0]
    copies = []
    steps = [(i, j) for i in range(len(picked)) for j in range(len(FINE_PAIRS))]
    turn_left(0)
    turn_right(0, 0)
    for (i, j), after in zip(steps, steps[1:] + [None]):
        for u in range(0, len(COARSE), 2):
            if u and after:
                if after[1] == 0:
                    turn_left(after[0])
                turn_right(*after)
            total = lax.dot_general(
                left_turned[i % slots, u * TILE:(u + 2) * TILE, :],
                right_turned[i % slots, 2 * j * TILE:2 * (j + 1) * TILE, :],
                (((1,), (1,)), ((), ())),
                preferred_element_type=jnp.float32,
            )
            for v, s in ((0, 0), (0, 1), (1, 0), (1, 1)):
                fine = FINE_PAIRS[j][s] + 4
                value = total[v * TILE:(v + 1) * TILE, s * TILE:(s + 1) * TILE]
                if adds:
                    each = len(picked) // adds
                    more[0][i, u + v, fine] = partials[i // each][i % each, u + v, fine] + value
                else:
                    out_ref[i, u + v, fine] = value
        for s in range(2 if adds else 0):
            done = (i, slice(None), FINE_PAIRS[j][s] + 4)
            copy = pltpu.make_async_copy(more[0].at[done], out_ref.at[done], more[1])
            copy.start(priority=s)
            copies.append(copy)
    for copy in copies:
        copy.wait()


def correlate(parts, groups, where, picked, hours, partials=()):
    places = [part[0] for part in parts]
    pieces = [piece for part in parts for piece in part[1:]]
    _, rows, lanes = pieces[0].shape
    fine = 2 * len(FINE_PAIRS)
    shape = (len(picked), len(COARSE), fine, TILE, TILE)
    norm = 1.0 / math.sqrt(F * hours)
    slots = min(len(picked), 2)
    chans = CORES * sum(map(len, places)) * rows
    scratch = 2 * (groups * chans * lanes + slots * (len(COARSE) + fine) * TILE * groups * lanes)
    adds = len(partials)
    more = []
    if adds:
        more = [pltpu.VMEM(shape, jnp.float32), pltpu.SemaphoreType.DMA]
        scratch += 4 * math.prod(shape)
    return pl.pallas_call(
        lambda *refs: correlate_kernel(norm, picked, adds, places, *refs),
        out_shape=jax.ShapeDtypeStruct(shape, jnp.float32),
        in_specs=[VMEM] * (1 + len(pieces) + adds),
        out_specs=pl.BlockSpec(memory_space=pl.ANY) if adds else VMEM,
        scratch_shapes=[
            pltpu.VMEM((groups, chans, lanes), jnp.bfloat16),
            pltpu.VMEM((slots, len(COARSE) * TILE, groups * lanes), jnp.bfloat16),
            pltpu.VMEM((slots, fine * TILE, groups * lanes), jnp.bfloat16),
            *more,
        ],
        compiler_params=pltpu.CompilerParams(vmem_limit_bytes=scratch + SMALL),
        cost_estimate=pl.CostEstimate(flops=0, bytes_accessed=0, transcendentals=0),
        name="correlate_add" if adds else "correlate",
    )(where, *pieces, *partials)


def swap(array, axis, k):
    return lax.ppermute(array, axis, [(i, i ^ k) for i in range(lax.axis_size(axis))])


def stack_kernel(blocks, *refs):
    out_ref = refs[-1]
    first = 0
    for block in refs[:blocks]:
        out_ref[first:first + block.shape[0]] = block[...]
        first += block.shape[0]


def stack(blocks, after=(), flops=0):
    depth = sum(block.shape[0] for block in blocks)
    return pl.pallas_call(
        lambda *refs: stack_kernel(len(blocks), *refs),
        out_shape=jax.ShapeDtypeStruct((depth, *blocks[0].shape[1:]), blocks[0].dtype),
        in_specs=[VMEM] * len(blocks) + [pl.BlockSpec(memory_space=pl.ANY)] * len(after),
        out_specs=VMEM,
        compiler_params=pltpu.CompilerParams(vmem_limit_bytes=SMALL),
        cost_estimate=pl.CostEstimate(flops=flops, bytes_accessed=0, transcendentals=0),
        name="stack",
    )(*blocks, *after)


def halves(white, where):
    groups = lax.axis_size("tm")
    blocks = [white[None]] + [swap(white[None], "tm", k) for k in range(1, groups)]
    return stack(blocks[:groups // 2]), stack(blocks[groups // 2:], after=(where,), flops=10**9)


def between_chips(half, parts):
    chips = lax.axis_size("chan") // CORES
    places = [0, *range(chips - 1, 0, -1)]
    blocks = [swap(half, "chan", CORES * k) if k else half for k in places]
    each = chips // parts
    return [(places[i:i + each], blocks[i:i + each]) for i in range(0, chips, each)]


def between_cores(parts):
    collected = [(places, stack(blocks)) for places, blocks in parts]
    return [(places, own, swap(own, "chan", 1)) for places, own in collected]


def per_device(spectra, bad_channels, tile_list):
    groups = lax.axis_size("tm")
    hours = spectra.shape[1] * groups
    tiles = tile_list.shape[0] // groups
    white = whiten(spectra, bad_channels)
    pairs = lax.dynamic_slice_in_dim(tile_list.T, lax.axis_index("tm") * tiles, tiles, axis=1)
    where = jnp.concatenate([lax.axis_index("chan").reshape(1), pairs.reshape(-1)]).astype(jnp.int32).reshape(1, -1)
    near, far = halves(white, where)
    near, far = between_cores(between_chips(near, 2)), between_cores(between_chips(far, 2))
    partial = correlate(near, groups // 2, where, range(tiles), hours)
    out = correlate(far, groups // 2, where, range(tiles), hours, [partial])
    return out.reshape(tiles, LAGS, TILE, TILE)


def solution(mesh):
    placed = (P(None, "tm", None, "chan"), P("chan"), P("chan", None))
    return jax.shard_map(
        per_device,
        mesh=mesh,
        in_specs=placed,
        out_specs=P(("chan", "tm"), None, None, None),
        check_vma=False,
    )
```

```python
import math

import jax
import jax.numpy as jnp
from jax import lax
from jax.experimental import pallas as pl
from jax.experimental.pallas import tpu as pltpu
from jax.sharding import PartitionSpec as P

F = 64
LAGS = 32
TILE = 128
EPSILON = 1e-06
CORES = 2
SMALL = 4 * 1024 * 1024
VMEM = pl.BlockSpec(memory_space=pltpu.VMEM)
COARSE = (-12, -4, 4, 12)
FINE_PAIRS = ((-4, 0), (-1, 1), (-2, 2), (-3, 3))


def whiten_kernel(spectra_hbm, bad_hbm, out_ref, spectra_ref, bad_ref, sems):
    rows, chans = spectra_ref.shape
    parts = 4
    slices = [pl.ds(i * rows // parts, rows // parts) for i in range(parts)]
    copies = [pltpu.make_async_copy(spectra_hbm.at[at], spectra_ref.at[at], sems.at[i]) for i, at in enumerate(slices)]
    copies.append(pltpu.make_async_copy(bad_hbm, bad_ref, sems.at[parts]))
    for copy in copies:
        copy.start()
    bins = F
    hours = rows // (2 * bins)
    row = lax.broadcasted_iota(jnp.int32, (rows, chans), 0)
    hour = (row // 2) % hours
    src = lax.broadcasted_iota(jnp.int32, (rows, rows), 0)
    dst = lax.broadcasted_iota(jnp.int32, (rows, rows), 1)
    move = jnp.where((src % 2) * (rows // 2) + src // 2 == dst, 1.0, 0.0).astype(jnp.bfloat16)
    for copy in copies:
        copy.wait()
    values = spectra_ref[...].astype(jnp.float32)
    keep = (1 - bad_ref[...]).astype(jnp.float32)
    squares = values * values
    scale = jnp.zeros((rows, chans), jnp.float32)
    for h in range(hours):
        power = jnp.sum(jnp.where(hour == h, squares, 0.0), axis=0, keepdims=True) * (1.0 / (2 * bins))
        scale = jnp.where(hour == h, lax.rsqrt(power + EPSILON) * keep, scale)
    white = (values * scale).astype(jnp.bfloat16)
    out_ref[...] = lax.dot_general(
        white, move, (((0,), (0,)), ((), ())), preferred_element_type=jnp.float32
    ).astype(jnp.bfloat16)


def whiten(spectra, bad_channels):
    chans = spectra.shape[-1]
    spectra = spectra.reshape(-1, chans)
    spectra = pltpu.with_memory_space_constraint(spectra, pltpu.HBM)
    bad_channels = pltpu.with_memory_space_constraint(bad_channels.reshape(1, chans), pltpu.HBM)
    return pl.pallas_call(
        whiten_kernel,
        out_shape=jax.ShapeDtypeStruct((chans, spectra.shape[0]), jnp.bfloat16),
        in_specs=[pl.BlockSpec(memory_space=pltpu.HBM)] * 2,
        out_specs=VMEM,
        scratch_shapes=[
            pltpu.VMEM(spectra.shape, spectra.dtype),
            pltpu.VMEM((1, chans), bad_channels.dtype),
            pltpu.SemaphoreType.DMA((5,)),
        ],
        compiler_params=pltpu.CompilerParams(vmem_limit_bytes=SMALL),
        name="whiten",
    )(spectra, bad_channels)


def cos_sin(turn):
    quarter = F // 2
    shifted = turn + quarter // 2
    x = (shifted % quarter - quarter // 2).astype(jnp.float32) * (math.pi / F)
    y = x * x
    cos = 1 - y * (1 / 2 - y * (1 / 24 - y * (1 / 720 - y * (1 / 40320 - y / 3628800))))
    sin = x * (1 - y * (1 / 6 - y * (1 / 120 - y * (1 / 5040 - y / 362880))))
    quadrant = shifted // quarter % 4
    odd = quadrant % 2 == 1
    cos, sin = jnp.where(odd, sin, cos), jnp.where(odd, cos, sin)
    return jnp.where((quadrant == 1) | (quadrant == 2), -cos, cos), jnp.where(quadrant >= 2, -sin, sin)


def turn_by(re, im, cos, sin, both):
    rc, rs, ic, is_ = re * cos, re * sin, im * cos, im * sin
    forward = (rc - is_, rs + ic)
    return (forward, (rc + is_, ic - rs)) if both else (forward,)


def correlate_kernel(norm, picked, adds, places, where_ref, *refs):
    parts, refs = refs[:2 * len(places)], refs[2 * len(places):]
    partials = refs[:adds]
    out_ref = refs[adds]
    spectra, left_turned, right_turned, *more = refs[adds + 1:]
    groups, _, lanes = spectra.shape
    half = lanes // 2
    hours_dev = half // F
    bin_number = lax.broadcasted_iota(jnp.int32, (8, half), 1) // hours_dev + 1
    step = lax.broadcasted_iota(jnp.int32, (8, half), 0)
    cos, sin = cos_sin(jnp.where(step == 6, 12, step) * bin_number)
    table = {k: (cos[i:i + 1], sin[i:i + 1]) for k, i in ((1, 1), (2, 2), (3, 3), (4, 4), (12, 6))}

    chan = where_ref[0, 0]
    for i, piece in enumerate(parts):
        rows = piece.shape[1]
        for slot, k in enumerate(places[i // 2]):
            place = pl.multiple_of((chan ^ (CORES * k + i % 2)) * rows, 32)
            spectra[:, pl.ds(place, rows), :] = piece[slot * groups:(slot + 1) * groups]

    def load(block, g):
        whole = spectra[g, pl.ds(pl.multiple_of(block * TILE, TILE), TILE), :].astype(jnp.float32)
        return whole[:, :half], whole[:, half:]

    def store(ref, slot, index, g, value):
        rows_at = pl.ds(index * TILE, TILE)
        ref[slot, rows_at, g * lanes:g * lanes + half] = value[0].astype(jnp.bfloat16)
        ref[slot, rows_at, g * lanes + half:(g + 1) * lanes] = value[1].astype(jnp.bfloat16)

    def turn_left(i):
        for g in range(groups):
            re, im = load(where_ref[0, 1 + picked[i]], g)
            for k in (4, 12):
                forward, backward = turn_by(re, im, *(norm * part for part in table[k]), True)
                store(left_turned, i % slots, COARSE.index(k), g, forward)
                store(left_turned, i % slots, COARSE.index(-k), g, backward)

    def turn_right(i, j):
        for g in range(groups):
            re, im = load(where_ref[0, (where_ref.shape[1] + 1) // 2 + picked[i]], g)
            if j == 0:
                turns = (turn_by(re, im, *table[4], False)[0], (re, im))
            else:
                turns = turn_by(re, im, *table[j], True)
            for s in range(2):
                store(right_turned, i % slots, 2 * j + s, g, turns[s])

    slots = left_turned.shape[0]
    copies = []
    steps = [(i, j) for i in range(len(picked)) for j in range(len(FINE_PAIRS))]
    turn_left(0)
    turn_right(0, 0)
    for (i, j), after in zip(steps, steps[1:] + [None]):
        for u in range(0, len(COARSE), 2):
            if u and after:
                if after[1] == 0:
                    turn_left(after[0])
                turn_right(*after)
            total = lax.dot_general(
                left_turned[i % slots, u * TILE:(u + 2) * TILE, :],
                right_turned[i % slots, 2 * j * TILE:2 * (j + 1) * TILE, :],
                (((1,), (1,)), ((), ())),
                preferred_element_type=jnp.float32,
            )
            for v, s in ((0, 0), (0, 1), (1, 0), (1, 1)):
                fine = FINE_PAIRS[j][s] + 4
                value = total[v * TILE:(v + 1) * TILE, s * TILE:(s + 1) * TILE]
                if adds:
                    each = len(picked) // adds
                    more[0][i, u + v, fine] = partials[i // each][i % each, u + v, fine] + value
                else:
                    out_ref[i, u + v, fine] = value
        for s in range(2 if adds else 0):
            done = (i, slice(None), FINE_PAIRS[j][s] + 4)
            copy = pltpu.make_async_copy(more[0].at[done], out_ref.at[done], more[1])
            copy.start(priority=s)
            copies.append(copy)
    for copy in copies:
        copy.wait()


def correlate(parts, groups, where, picked, hours, partials=()):
    places = [part[0] for part in parts]
    pieces = [piece for part in parts for piece in part[1:]]
    _, rows, lanes = pieces[0].shape
    fine = 2 * len(FINE_PAIRS)
    shape = (len(picked), len(COARSE), fine, TILE, TILE)
    norm = 1.0 / math.sqrt(F * hours)
    slots = min(len(picked), 2)
    chans = CORES * sum(map(len, places)) * rows
    scratch = 2 * (groups * chans * lanes + slots * (len(COARSE) + fine) * TILE * groups * lanes)
    adds = len(partials)
    more = []
    if adds:
        more = [pltpu.VMEM(shape, jnp.float32), pltpu.SemaphoreType.DMA]
        scratch += 4 * math.prod(shape)
    return pl.pallas_call(
        lambda *refs: correlate_kernel(norm, picked, adds, places, *refs),
        out_shape=jax.ShapeDtypeStruct(shape, jnp.float32),
        in_specs=[VMEM] * (1 + len(pieces) + adds),
        out_specs=pl.BlockSpec(memory_space=pl.ANY) if adds else VMEM,
        scratch_shapes=[
            pltpu.VMEM((groups, chans, lanes), jnp.bfloat16),
            pltpu.VMEM((slots, len(COARSE) * TILE, groups * lanes), jnp.bfloat16),
            pltpu.VMEM((slots, fine * TILE, groups * lanes), jnp.bfloat16),
            *more,
        ],
        compiler_params=pltpu.CompilerParams(vmem_limit_bytes=scratch + SMALL),
        cost_estimate=pl.CostEstimate(flops=0, bytes_accessed=0, transcendentals=0),
        name="correlate_add" if adds else "correlate",
    )(where, *pieces, *partials)


def swap(array, axis, k):
    return lax.ppermute(array, axis, [(i, i ^ k) for i in range(lax.axis_size(axis))])


def stack_kernel(blocks, *refs):
    out_ref = refs[-1]
    first = 0
    for block in refs[:blocks]:
        out_ref[first:first + block.shape[0]] = block[...]
        first += block.shape[0]


def stack(blocks, after=(), flops=0):
    depth = sum(block.shape[0] for block in blocks)
    return pl.pallas_call(
        lambda *refs: stack_kernel(len(blocks), *refs),
        out_shape=jax.ShapeDtypeStruct((depth, *blocks[0].shape[1:]), blocks[0].dtype),
        in_specs=[VMEM] * len(blocks) + [pl.BlockSpec(memory_space=pl.ANY)] * len(after),
        out_specs=VMEM,
        compiler_params=pltpu.CompilerParams(vmem_limit_bytes=SMALL),
        cost_estimate=pl.CostEstimate(flops=flops, bytes_accessed=0, transcendentals=0),
        name="stack",
    )(*blocks, *after)


def halves(white, where):
    groups = lax.axis_size("tm")
    blocks = [white[None]] + [swap(white[None], "tm", k) for k in range(1, groups)]
    return stack(blocks[:groups // 2]), stack(blocks[groups // 2:], after=(where,), flops=10**9)


def between_chips(half, parts):
    chips = lax.axis_size("chan") // CORES
    places = [0, *range(chips - 1, 0, -1)]
    blocks = [swap(half, "chan", CORES * k) if k else half for k in places]
    each = chips // parts
    return [(places[i:i + each], blocks[i:i + each]) for i in range(0, chips, each)]


def between_cores(parts):
    collected = [(places, stack(blocks)) for places, blocks in parts]
    return [(places, own, swap(own, "chan", 1)) for places, own in collected]


def per_device(spectra, bad_channels, tile_list):
    groups = lax.axis_size("tm")
    hours = spectra.shape[1] * groups
    tiles = tile_list.shape[0] // groups
    white = whiten(spectra, bad_channels)
    pairs = lax.dynamic_slice_in_dim(tile_list.T, lax.axis_index("tm") * tiles, tiles, axis=1)
    where = jnp.concatenate([lax.axis_index("chan").reshape(1), pairs[0], pairs[1]]).astype(jnp.int32).reshape(1, -1)
    near, far = halves(white, where)
    near, far = between_cores(between_chips(near, 2)), between_cores(between_chips(far, 2))
    partial = correlate(near, groups // 2, where, range(tiles), hours)
    out = correlate(far, groups // 2, where, range(tiles), hours, [partial])
    return out.reshape(tiles, LAGS, TILE, TILE)


def solution(mesh):
    placed = (P(None, "tm", None, "chan"), P("chan"), P("chan", None))
    return jax.shard_map(
        per_device,
        mesh=mesh,
        in_specs=placed,
        out_specs=P(("chan", "tm"), None, None, None),
        check_vma=False,
    )
```
